32 devices in a mesh: groups: 2 (over y), seq: 4 (over z), chan: 4 (over x, core).
Axes of the slice: x: 2, y: 2, z: 4, core: 2. Of those that a mesh axis runs over, the one named last changes fastest.
Arguments:
- dna_bases: int32 [4096], P(('groups', 'seq')), parts along dimension 0, may hold values from 0 to 3
- w_stem: bfloat16 [768, 5, 4], P('chan'), may hold values from -2.5 to 2.5
- w_enc: bfloat16 [1536, 5, 768], P(None, None, 'chan'), may hold values from -0.09375 to 0.09375
- w_dec: bfloat16 [768, 5, 1536], P(None, None, 'chan'), may hold values from -0.0625 to 0.0625
- targets: bfloat16 [4096, 768], P(('groups', 'seq'), 'chan'), parts along dimension 0, may hold values from -6 to 6
Outputs:
- pred: bfloat16 [4096, 768], P(('groups', 'seq'), 'chan'), parts along dimension 0
- g_enc: float32 [3072, 5, 768], P(('groups', 'seq'), None, 'chan'), parts along dimension 0
- g_dec: float32 [1536, 5, 1536], P(('groups', 'seq'), None, 'chan'), parts along dimension 0
The draws below stay inside these ranges and needn't reach their ends.
There are 2 independent parts, one for each index of `groups`. The reference program is written for one: setup_inputs(seed, part) draws one part's arguments, and reference() takes and returns one part's arrays. A program takes and returns all parts, laid end to end along the dimension named above; an argument that names none is the same for every part. Nothing has to cross between parts.
Inputs may be any that keep to these rules, and one draw needn't show every extreme that they name: `dna_bases`: each entry is one of the four bases.
All inputs are finite; a program needn't handle non-finite values.
Results may differ from the reference program's by a relative error of at most 0.009.
Values may be sent and summed in bfloat16 or wider, within the bound.
No kernel may reach another device: no remote copies, remote signals or barrier semaphores. Data moves between devices by JAX's collectives and lax.ppermute only.
A program may use at most 192 MiB of HBM per device.

```python
import math
import jax
import jax.numpy as jnp
from jax import lax

C1 = 768
C2 = 1536
KW = 5
LENGTH = 2048
N_SEQ = 4


def set_ends(drawn, stream_key, least, largest):
    spot = [jax.random.randint(jax.random.fold_in(stream_key, axis), (), 0, length) for axis, length in enumerate(drawn.shape)]
    widest = drawn.shape.index(max(drawn.shape))
    beside = spot[:widest] + [(spot[widest] + 1) % drawn.shape[widest]] + spot[widest + 1:]
    return drawn.at[tuple(spot)].set(least).at[tuple(beside)].set(largest)


def strengthened(values, key, source, target, shards_of, factor):
    def block_of(position):
        return (jnp.arange(values.shape[position]) // (values.shape[position] // shards_of)).reshape((-1,) + (1,) * (values.ndim - 1 - position))

    one_side = jax.random.permutation(key, shards_of)[block_of(target)]
    far = (block_of(target) + shards_of // 2) % shards_of
    return jnp.where((block_of(source) == one_side) | (block_of(source) == far), factor * values, values)


def shard_levels(own_key, shape, shards, least, high):
    def one(position, shards_of):
        steps = jax.random.uniform(jax.random.fold_in(jax.random.fold_in(own_key, 6), position), (shards_of,), jnp.float32, least / len(shards), high / len(shards))
        return jnp.repeat(jnp.exp(steps), shape[position] // shards_of).reshape((-1,) + (1,) * (len(shape) - position - 1))

    factor_of = one(*shards[0])
    for cut in shards[1:]:
        factor_of = factor_of * one(*cut)
    return factor_of


def noise(key, extent, spread, limit, cuts=(), kind=jnp.bfloat16):
    drawn = jax.random.normal(key, extent, jnp.float32) * spread
    if len(cuts) > 0:
        drawn = shard_levels(key, extent, cuts, -0.22, 0.18) * drawn
    return jnp.clip(drawn, min=-limit, max=limit).astype(kind)


def bell_draw_with(stream_key, dims, spread, reach, shards, heavy, kind=jnp.bfloat16):
    values = spread * jax.random.normal(stream_key, dims, jnp.float32)
    if shards:
        values = values * shard_levels(stream_key, dims, shards, -0.22, 0.18)
    return jnp.clip(strengthened(values, jax.random.fold_in(stream_key, 3), *heavy), -reach, reach).astype(kind)


def setup_inputs(seed: int = 0, part: int = 0) -> dict:
    splits = jax.random.split(jax.random.key(seed), 6)
    part_keys = jax.random.split(jax.random.fold_in(splits[5], part), 6)
    dna_bases = set_ends(jax.random.randint(part_keys[0], (LENGTH,), 0, 4), jax.random.fold_in(part_keys[0], 1), 0, 3).astype(jnp.int32)
    w_stem = noise(splits[1], (C1, KW, 4), KW ** -0.5, 2.5, ((0, 4),))
    w_enc = noise(splits[2], (C2, KW, C1), (KW * C1) ** -0.5, 0.09375, ((2, 4),))
    w_dec = noise(splits[3], (C1, KW, C2), (KW * C2) ** -0.5, 0.0625, ((2, 4),))
    targets = bell_draw_with(part_keys[4], (LENGTH, C1), 1.0, 6.0, ((0, 4), (1, 4)), (0, 1, 4, 2.0))
    return dict(dna_bases=dna_bases, w_stem=w_stem, w_enc=w_enc, w_dec=w_dec, targets=targets)


SQRT_TWO_PI = 0.7978845608028654
CUBIC = 0.044715

def gelu_value(value):
    inner = jnp.tanh(SQRT_TWO_PI * (value + CUBIC * value * value * value))
    return 0.5 * value * (1.0 + inner)

def gelu_slope(value):
    inner = jnp.tanh(SQRT_TWO_PI * (value + CUBIC * value * value * value))
    return 0.5 * (1.0 + inner) + 0.5 * value * (1.0 - inner * inner) * SQRT_TWO_PI * (1.0 + 3.0 * CUBIC * value * value)

def pad_rows(array, margin):
    return jnp.pad(array, ((margin, margin), (0, 0)))

def conv_rows(padded, weight):
    row_count = padded.shape[0] - 4
    total = jnp.zeros((row_count, weight.shape[0]), jnp.float32)
    for k in range(KW):
        total = total + jnp.dot(padded[k:k + row_count].astype(jnp.float32), weight[:, k, :].astype(jnp.float32).T)
    return total

def block_grad(cotangent, padded):
    row_count = cotangent.shape[0] // N_SEQ
    width = cotangent.shape[1]

    def one_block(total, index):
        first = index * row_count
        part = lax.dynamic_slice_in_dim(cotangent, first, row_count, 0).astype(jnp.float32)
        window = lax.dynamic_slice_in_dim(padded, first, row_count + 4, 0).astype(jnp.float32)
        pieces = [jnp.dot(part.T, window[k:k + row_count]) for k in range(KW)]
        piece = jnp.stack(pieces, axis=1).astype(jnp.bfloat16)
        return (total + lax.optimization_barrier(piece).astype(jnp.float32), None)
    start_total = jnp.zeros((width, KW, padded.shape[1]), jnp.float32)
    total, _ = lax.scan(one_block, start_total, jnp.arange(N_SEQ, dtype=jnp.int32))
    return total

def reference(dna_bases, w_stem, w_enc, w_dec, targets):
    length = dna_bases.shape[0]
    onehot = (dna_bases[:, None] == jnp.arange(4, dtype=jnp.int32)[None, :]).astype(jnp.bfloat16)
    stem_out = gelu_value(conv_rows(pad_rows(onehot, 2), w_stem)).astype(jnp.bfloat16)
    stem_pad = pad_rows(stem_out, 2)
    enc_pre = conv_rows(stem_pad, w_enc)
    active = gelu_value(enc_pre).astype(jnp.bfloat16).astype(jnp.float32)
    pooled = (0.5 * (active[0::2] + active[1::2])).astype(jnp.bfloat16)
    up_pad = pad_rows(jnp.repeat(pooled, 2, axis=0), 2)
    output = conv_rows(up_pad, w_dec) + stem_out.astype(jnp.float32)
    pred = output.astype(jnp.bfloat16)
    scale = 1.0 / math.sqrt(length)
    slope_out = ((output - targets.astype(jnp.float32)) * scale).astype(jnp.bfloat16)
    g_dec = block_grad(slope_out, up_pad)
    slope_pad = pad_rows(slope_out, 2).astype(jnp.float32)
    up_grad = jnp.zeros((length, w_dec.shape[2]), jnp.float32)
    for k in range(KW):
        up_grad = up_grad + jnp.dot(slope_pad[4 - k:4 - k + length], w_dec[:, k, :].astype(jnp.float32))
    pool_grad = up_grad[0::2] + up_grad[1::2]
    act_grad = 0.5 * jnp.repeat(pool_grad, 2, axis=0)
    pre_grad = (act_grad * gelu_slope(enc_pre)).astype(jnp.bfloat16)
    g_enc = block_grad(pre_grad, stem_pad)
    return (pred, g_enc, g_dec)
```

```python
import functools
import math

import jax
import jax.numpy as jnp
from jax import lax
from jax.experimental import pallas as pl
from jax.experimental.pallas import tpu as pltpu
from jax.sharding import PartitionSpec as P

KW = 5

SQRT_TWO_PI = 0.7978845608028654
CUBIC = 0.044715

SIDE = 64
OUTER = 16
INNER = 8
F32 = jnp.float32
BF16 = jnp.bfloat16
MIB = 1024 * 1024


def gelu_value(value):
    inner = jnp.tanh(SQRT_TWO_PI * (value + CUBIC * value * value * value))
    return 0.5 * value * (1.0 + inner)


def gelu_both(value):
    square = value * value
    inner = jnp.tanh(SQRT_TWO_PI * (value + CUBIC * square * value))
    slope = 0.5 * (1.0 + inner) + 0.5 * value * (1.0 - inner * inner) * SQRT_TWO_PI * (
        1.0 + 3.0 * CUBIC * square
    )
    return 0.5 * value * (1.0 + inner), slope


def dot(a, b, contract):
    return lax.dot_general(a, b, (contract, ((), ())), preferred_element_type=F32)


def tap_onehots(bases, start, width):
    total = bases.shape[1]
    before = pltpu.roll(bases, total - (start - 1), 1)[:, :width]
    here = pltpu.roll(bases, total - start, 1)[:, :width]
    after = pltpu.roll(bases, total - (start + 1), 1)[:, :width]
    taps = [before[0:1], before[1:2], here[0:1], here[1:2], after[0:1], after[1:2]]
    row = lax.broadcasted_iota(jnp.int32, (4 * KW, width), 0)
    tap, base = row >> 2, row & 3
    out = []
    for first in (0, 1):
        value = jnp.full((4 * KW, width), -1, jnp.int32)
        for k in range(KW):
            value = jnp.where(tap == k, jnp.broadcast_to(taps[first + k], value.shape), value)
        out.append(jnp.where(value == base, 1.0, 0.0).astype(BF16))
    return out


def valid_pairs(shape, dim, first, total):
    pair = lax.broadcasted_iota(jnp.int32, shape, dim) + first
    return (pair >= 0) & (pair < total)


def enc_kernel(place, bases, stem_w, w_own, w_oth, keep, send, stem_out, even, odd, lhs, *, pairs, total):
    seq, hi, lo = place[0], place[1], place[2]
    rows = pairs + 2 * INNER
    wide = pairs + 2 * OUTER
    block = keep.shape[1]
    hots = tap_onehots(bases[...], SIDE - OUTER, wide)
    for q in range(2):
        for hot, held in zip(hots, (even, odd)):
            raw = dot(hot, stem_w[q], ((0,), (0,)))
            ok = valid_pairs(raw.shape, 0, seq * pairs - OUTER, total)
            held[...] = jnp.where(ok, gelu_value(raw), 0.0).astype(BF16).astype(F32)
        gap = OUTER - INNER
        for k in range(6):
            source = even if k % 2 == 0 else odd
            lhs[q, k] = source[gap + k // 2 - 1 : gap + k // 2 - 1 + rows, :].astype(BF16)
        if q == 0:
            stem_out[0] = lhs[0, 2]
            stem_out[1] = lhs[0, 3]
    for part in range(2):
        own_at = pl.multiple_of((2 * (hi if part == 0 else 1 - hi) + lo) * block, 128)
        oth_at = pl.multiple_of((hi if part == 0 else 1 - hi) * block, 128)
        acc = jnp.zeros((2 * rows, block), F32)
        for k in range(KW):
            acc = acc + dot(
                lhs[0, k : k + 2].reshape(2 * rows, -1), w_own[k, :, pl.ds(own_at, block)], ((1,), (0,))
            )
            acc = acc + dot(
                lhs[1, k : k + 2].reshape(2 * rows, -1), w_oth[k, :, pl.ds(oth_at, block)], ((1,), (0,))
            )
        if part == 0:
            keep[...] = acc
        else:
            send[...] = acc.astype(BF16)


def pool_kernel(place, keep, came, pooled, centre, slope, *, pairs, total):
    rows = pairs + 2 * INNER
    value = keep[...] + came[...].astype(F32)
    active, grad = gelu_both(value)
    active = active.astype(BF16).astype(F32)
    both = 0.5 * (active[:rows] + active[rows:])
    ok = valid_pairs(both.shape, 0, place[0] * pairs - INNER, total)
    both = jnp.where(ok, both, 0.0).astype(BF16)
    pooled[...] = both
    centre[...] = both[INNER : INNER + pairs].astype(BF16)
    grad = 0.5 * grad
    slope[0] = grad[INNER : INNER + pairs]
    slope[1] = grad[rows + INNER : rows + INNER + pairs]


def dec_kernel(own, oth, w_own, w_oth, stem, targets, part, send, held, *, pairs):
    rows = pairs + 2 * INNER
    held[:8] = jnp.zeros((8, held.shape[1]), F32)
    held[8 + rows :] = jnp.zeros((8, held.shape[1]), F32)
    acc = jnp.zeros(part.shape, F32)
    for source, weight in ((own, w_own), (oth, w_oth)):
        held[8 : 8 + rows] = source[...].astype(F32)
        for k in range(3):
            acc = acc + dot(held[7 + k : 7 + k + rows].astype(BF16), weight[k], ((1,), (1,)))
    half = part.shape[1] // 2
    for parity in range(2):
        value = acc[:, parity * half : (parity + 1) * half]
        value = value + stem[parity].astype(F32) - targets[parity].astype(F32)
        part[:, parity * half : (parity + 1) * half] = value
        send[:, parity * half : (parity + 1) * half] = value.astype(BF16)


def slope_kernel(place, part, came, targets, pred, sums, held, *, pairs, total, scale):
    rows = pairs + 2 * INNER
    half = part.shape[1] // 2
    ok = valid_pairs((rows, half), 0, place[0] * pairs - INNER, total)
    slopes = []
    for parity in range(2):
        cols = slice(parity * half, (parity + 1) * half)
        value = part[:, cols] + came[:, cols].astype(F32)
        out = value + targets[parity].astype(F32)
        pred[parity] = out[INNER : INNER + pairs].astype(BF16)
        slopes.append(jnp.where(ok, value * scale, 0.0).astype(BF16).astype(F32))
    held[:rows] = slopes[0]
    held[rows:] = jnp.zeros((8, half), F32)
    sums[0] = (slopes[0] + slopes[1]).astype(BF16)
    sums[1] = (slopes[1] + held[1 : 1 + rows]).astype(BF16)


def shifted_sums(held, pairs):
    return [
        held[0, INNER + 1 : INNER + 1 + pairs].astype(BF16),
        held[1, INNER : INNER + pairs].astype(BF16),
        held[0, INNER : INNER + pairs].astype(BF16),
        held[1, INNER - 1 : INNER - 1 + pairs].astype(BF16),
        held[0, INNER - 1 : INNER - 1 + pairs].astype(BF16),
    ]


def back_kernel(own, oth, w_own, w_oth, slope, out, held, *, pairs):
    acc = jnp.zeros((pairs, out.shape[2]), F32)
    for source, weight in ((own, w_own), (oth, w_oth)):
        held[...] = source[...].astype(F32)
        for k, tap in enumerate(shifted_sums(held, pairs)):
            acc = acc + dot(tap, weight[k], ((1,), (0,)))
    out[0] = (acc * slope[0]).astype(BF16)
    out[1] = (acc * slope[1]).astype(BF16)


def taps_kernel(place, bases, stem_w, out, *, pairs, total, devices):
    block = lax.rem(place[0] - pl.program_id(0) + devices, devices)
    hots = tap_onehots(bases[0], SIDE, bases.shape[2])
    channels = stem_w.shape[0]
    parts = []
    for hot in hots:
        raw = dot(stem_w[...], hot, ((1,), (0,)))
        width = raw.shape[1]
        col = lax.broadcasted_iota(jnp.int32, raw.shape, 1)
        pair = jnp.where(col >= width - SIDE, col - width, col) + block * pairs
        ok = (pair >= 0) & (pair < total)
        parts.append(jnp.where(ok, gelu_value(raw), 0.0))
    width = parts[0].shape[1]
    taps = []
    for step in (-1, 0, 1):
        for held in parts:
            moved = held if step == 0 else pltpu.roll(held, (-step) % width, 1)
            taps.append(moved[:, :pairs].astype(BF16))
    for k in range(KW):
        out[0, k * channels : (k + 1) * channels, :pairs] = taps[k]
        out[0, k * channels : (k + 1) * channels, pairs:] = taps[k + 1]


def dec_grad_kernel(sums, pooled, out, held, *, pairs):
    held[...] = sums[0].astype(F32)

    @pl.when(pl.program_id(0) == 0)
    def _():
        out[...] = jnp.zeros(out.shape, F32)

    for k, tap in enumerate(shifted_sums(held, pairs)):
        out[k] += dot(tap, pooled[0], ((0,), (0,)))


def enc_grad_kernel(place, taps, own, oth, out, *, slots):
    step = pl.program_id(0)

    @pl.when(step == 0)
    def _():
        out[...] = jnp.zeros(out.shape, F32)

    @pl.when(step < slots)
    def _():
        out[...] += dot(taps[0], own[0], ((1,), (0,)))

    @pl.when(step >= slots)
    def _():
        out[...] += dot(taps[0], oth[0], ((1,), (0,)))


def whole(shape):
    return pl.BlockSpec(shape, lambda *_: (0,) * len(shape))


SCALARS = pl.BlockSpec(memory_space=pltpu.SMEM)


def call(kernel, ins, outs, scratch=(), limit=48, flops=0, name=None):
    specs = [SCALARS if i.dtype == jnp.int32 and i.ndim == 1 else whole(i.shape) for i in ins]
    size = sum(i.size * i.dtype.itemsize for i in ins) + sum(
        math.prod(s) * jnp.dtype(d).itemsize for s, d in outs
    )
    return pl.pallas_call(
        kernel,
        in_specs=specs,
        out_specs=[whole(s) for s, _ in outs],
        out_shape=[jax.ShapeDtypeStruct(s, d) for s, d in outs],
        scratch_shapes=[pltpu.VMEM(s, d) for s, d in scratch],
        compiler_params=pltpu.CompilerParams(vmem_limit_bytes=limit * MIB),
        cost_estimate=pl.CostEstimate(flops=flops, bytes_accessed=size, transcendentals=0),
        name=name,
    )(*ins)


def fast_shards(dna_bases, w_stem, w_enc, w_dec, targets):
    devices = lax.axis_size("seq")
    seq, chan = lax.axis_index("seq"), lax.axis_index("chan")
    hi, lo = chan // 2, chan % 2
    place = jnp.stack([seq, hi, lo]).astype(jnp.int32)
    pairs = dna_bases.shape[0] // 2
    total = pairs * devices
    rows = pairs + 2 * INNER
    stem_c = w_stem.shape[0]
    enc_c = w_dec.shape[2]
    across = [(c, c ^ 2) for c in range(4)]
    cores = [(c, c ^ 1) for c in range(4)]

    def ring(array, step):
        return lax.ppermute(array, "seq", [(i, (i + step) % devices) for i in range(devices)])

    enc_w = w_enc.transpose(1, 2, 0)
    dec_w = w_dec.transpose(1, 0, 2).reshape(KW, 2, 2, stem_c, enc_c)

    def pick(array, axis, index):
        return lax.dynamic_index_in_dim(array, index, axis, keepdims=False)

    stem_w = w_stem.transpose(1, 2, 0).reshape(4 * KW, stem_c)
    stem_oth = lax.ppermute(stem_w, "chan", cores)
    enc_send = pick(enc_w.reshape(KW, stem_c, 2, 2, enc_c), 3, 1 - lo).reshape(KW, stem_c, 2 * enc_c)
    enc_oth = lax.ppermute(enc_send, "chan", cores)

    own = dna_bases.reshape(pairs, 2).T
    blocks = [own] + [ring(own, r) for r in range(1, devices)]

    def bases_of(r):
        joined = jnp.concatenate(
            [blocks[(r + 1) % devices][:, pairs - SIDE :], blocks[r], blocks[(r - 1) % devices][:, :SIDE]], axis=1
        )
        first = lax.rem(seq - r + devices, devices) * pairs - SIDE
        pair = first + jnp.arange(pairs + 2 * SIDE, dtype=jnp.int32)[None, :]
        return jnp.where((pair >= 0) & (pair < total), joined, -1)

    keep, send, stem = call(
        functools.partial(enc_kernel, pairs=pairs, total=total),
        [place, bases_of(0), jnp.stack([stem_w, stem_oth]), enc_w, enc_oth],
        [((2 * rows, enc_c), F32), ((2 * rows, enc_c), BF16), ((2, rows, stem_c), BF16)],
        [
            ((pairs + 2 * OUTER, stem_c), F32),
            ((pairs + 2 * OUTER, stem_c), F32),
            ((2, 6, rows, stem_c), BF16),
        ],
        flops=4 * rows * 2 * stem_c * KW * 2 * enc_c,
        name="enc_conv",
    )
    came = lax.ppermute(send, "chan", across)

    dec_w, targets_in, bases_in, _ = lax.optimization_barrier((dec_w, targets, blocks, send))
    dec_own = pick(dec_w, 2, lo).reshape(KW, 2 * stem_c, enc_c)
    dec_oth = pick(dec_w, 2, 1 - lo).reshape(KW, 2 * stem_c, enc_c)
    dec_came = lax.ppermute(dec_oth, "chan", cores)

    def combined(w):
        even = jnp.stack([w[0] + w[1], w[2] + w[3], w[4]])
        odd = jnp.stack([w[0], w[1] + w[2], w[3] + w[4]])
        return jnp.concatenate([even, odd], axis=1)

    comb_own, comb_came = combined(dec_own), combined(dec_came)
    split = targets_in.reshape(pairs, 2, stem_c).transpose(1, 0, 2)
    split = jnp.concatenate(
        [ring(split[:, pairs - INNER :], 1), split, ring(split[:, :INNER], devices - 1)], axis=1
    )

    def placed(array):
        blank = jnp.zeros_like(array)
        return jnp.where(
            hi == 0, jnp.concatenate([array, blank], axis=2), jnp.concatenate([blank, array], axis=2)
        )

    targets_at, stem_at = placed(split), placed(stem)
    blocks = bases_in
    bases_all = jnp.stack([bases_of(r) for r in range(devices)])
    taps = pl.pallas_call(
        functools.partial(taps_kernel, pairs=pairs, total=total, devices=devices),
        grid=(devices,),
        in_specs=[
            SCALARS,
            pl.BlockSpec((1, 2, pairs + 2 * SIDE), lambda r: (r, 0, 0)),
            whole((stem_c, 4 * KW)),
        ],
        out_specs=pl.BlockSpec((1, KW * stem_c, 2 * pairs), lambda r: (r, 0, 0)),
        out_shape=jax.ShapeDtypeStruct((devices, KW * stem_c, 2 * pairs), BF16),
        compiler_params=pltpu.CompilerParams(vmem_limit_bytes=24 * MIB),
        name="stem_taps",
    )(place, bases_all, stem_w.T)

    pooled, centre, slope = call(
        functools.partial(pool_kernel, pairs=pairs, total=total),
        [place, keep, came],
        [((rows, enc_c), BF16), ((pairs, enc_c), BF16), ((2, pairs, enc_c), F32)],
        name="gelu_pool",
    )
    pooled_oth = lax.ppermute(pooled, "chan", cores)
    part, send = call(
        functools.partial(dec_kernel, pairs=pairs),
        [pooled, pooled_oth, comb_own, comb_came, stem_at, targets_at],
        [((rows, 4 * stem_c), F32), ((rows, 4 * stem_c), BF16)],
        [((rows + 16, enc_c), F32)],
        flops=2 * rows * 2 * enc_c * 3 * 4 * stem_c,
        name="dec_conv",
    )
    came = lax.ppermute(send, "chan", across)
    centre, _ = lax.optimization_barrier((centre, send))
    pooled_all = jnp.stack([centre] + [ring(centre, r) for r in range(1, devices)])

    pred, sums = call(
        functools.partial(slope_kernel, pairs=pairs, total=total, scale=1.0 / math.sqrt(2 * total)),
        [place, part, came, targets_at],
        [((2, pairs, 2 * stem_c), BF16), ((2, rows, 2 * stem_c), BF16)],
        [((rows + 8, 2 * stem_c), F32)],
        name="out_slope",
    )
    sums_oth = lax.ppermute(sums, "chan", cores)
    (pre,) = call(
        functools.partial(back_kernel, pairs=pairs),
        [sums, sums_oth, dec_own, dec_oth, slope],
        [((2, pairs, enc_c), BF16)],
        [((2, rows, 2 * stem_c), F32)],
        flops=2 * pairs * KW * 4 * stem_c * enc_c,
        name="up_grad",
    )
    pred = pick(pred.reshape(2, pairs, 2, stem_c), 2, hi)
    pred = pred.transpose(1, 0, 2).reshape(2 * pairs, stem_c)

    per_chan = devices // 4
    width = 4 * enc_c // devices

    def chan_of(block):
        return block // per_chan

    other = lax.ppermute(pre.reshape(2 * pairs, enc_c), "chan", across)
    pieces = jnp.stack([pre.reshape(2 * pairs, enc_c), other])
    mine = lax.rem(chan_of(seq), 2) == lo

    def piece(step):
        target = lax.rem(seq + step, devices)
        column = chan_of(target)
        block = pick(pieces, 0, (column // 2 != hi).astype(jnp.int32))
        return lax.dynamic_slice_in_dim(block, lax.rem(target, per_chan) * width, width, axis=1)

    def link(step):
        out = []
        for s in range(devices):
            t = (s + step) % devices
            for x in range(2):
                out.append((s * 4 + 2 * x + chan_of(t) % 2, t * 4 + 2 * x + (chan_of(t) + step) % 2))
        return out

    arrived = [piece(0)] + [
        lax.ppermute(piece(r), ("seq", "chan"), link(r)) for r in range(1, devices)
    ]
    held = jnp.stack(
        [jnp.where(mine, arrived[2 * i], arrived[2 * i + 1]) for i in range(devices // 2)]
    )
    held_oth = lax.ppermute(held, "chan", cores)
    slots = devices // 2
    parity = jnp.where(mine, 0, 1).astype(jnp.int32).reshape(1)

    def taps_at(i, p):
        first = i < slots
        return (jnp.where(first, 2 * i + p[0], 2 * (i - slots) + 1 - p[0]), 0, 0)

    g_enc = pl.pallas_call(
        functools.partial(enc_grad_kernel, slots=slots),
        grid_spec=pltpu.PrefetchScalarGridSpec(
            num_scalar_prefetch=1,
            grid=(devices,),
            in_specs=[
                pl.BlockSpec((1, KW * stem_c, 2 * pairs), taps_at),
                pl.BlockSpec((1, 2 * pairs, width), lambda i, p: (jnp.minimum(i, slots - 1), 0, 0)),
                pl.BlockSpec((1, 2 * pairs, width), lambda i, p: (jnp.maximum(i - slots, 0), 0, 0)),
            ],
            out_specs=pl.BlockSpec((KW * stem_c, width), lambda i, p: (0, 0)),
        ),
        out_shape=jax.ShapeDtypeStruct((KW * stem_c, width), F32),
        compiler_params=pltpu.CompilerParams(vmem_limit_bytes=32 * MIB),
        name="enc_grad",
    )(parity, taps, held, held_oth)
    g_enc = g_enc.reshape(KW, stem_c, width).transpose(2, 0, 1)

    natural = jnp.where(lo == 0, jnp.stack([sums, sums_oth]), jnp.stack([sums_oth, sums]))
    natural = natural.reshape(2, 2, rows, 2, stem_c).transpose(1, 2, 3, 0, 4).reshape(2, rows, 4 * stem_c)
    narrow = 4 * stem_c // devices
    half = pick(natural, 0, lo)

    def sums_for(array, step):
        return lax.dynamic_slice_in_dim(array, lax.rem(seq + step, devices) * narrow, narrow, axis=array.ndim - 1)

    half_all = jnp.stack([sums_for(half, 0)] + [ring(sums_for(half, r), r) for r in range(1, devices)])
    half_oth = lax.ppermute(half_all, "chan", cores)
    sums_all = jnp.where(
        lo == 0, jnp.stack([half_all, half_oth], axis=1), jnp.stack([half_oth, half_all], axis=1)
    )
    g_dec = pl.pallas_call(
        functools.partial(dec_grad_kernel, pairs=pairs),
        grid=(devices,),
        in_specs=[
            pl.BlockSpec((1, 2, rows, narrow), lambda r: (r, 0, 0, 0)),
            pl.BlockSpec((1, pairs, enc_c), lambda r: (r, 0, 0)),
        ],
        out_specs=pl.BlockSpec((KW, narrow, enc_c), lambda r: (0, 0, 0)),
        out_shape=jax.ShapeDtypeStruct((KW, narrow, enc_c), F32),
        scratch_shapes=[pltpu.VMEM((2, rows, narrow), F32)],
        compiler_params=pltpu.CompilerParams(vmem_limit_bytes=32 * MIB),
        name="dec_grad",
    )(sums_all, pooled_all)
    g_dec = g_dec.transpose(1, 0, 2)
    return (pred, g_enc, g_dec)


def solution(mesh):
    return jax.shard_map(
        fast_shards,
        mesh=mesh,
        in_specs=(
            P(("groups", "seq")),
            P("chan", None, None),
            P(None, None, "chan"),
            P(None, None, "chan"),
            P(("groups", "seq"), "chan"),
        ),
        out_specs=(
            P(("groups", "seq"), "chan"),
            P(("groups", "seq"), None, "chan"),
            P(("groups", "seq"), None, "chan"),
        ),
        check_vma=False,
    )
```

```python
import functools
import math

import jax
import jax.numpy as jnp
from jax import lax
from jax.experimental import pallas as pl
from jax.experimental.pallas import tpu as pltpu
from jax.sharding import PartitionSpec as P

KW = 5

SQRT_TWO_PI = 0.7978845608028654
CUBIC = 0.044715

SIDE = 64
OUTER = 16
INNER = 8
F32 = jnp.float32
BF16 = jnp.bfloat16
MIB = 1024 * 1024


def gelu_value(value):
    inner = jnp.tanh(SQRT_TWO_PI * (value + CUBIC * value * value * value))
    return 0.5 * value * (1.0 + inner)


def gelu_both(value):
    square = value * value
    inner = jnp.tanh(SQRT_TWO_PI * (value + CUBIC * square * value))
    slope = 0.5 * (1.0 + inner) + 0.5 * value * (1.0 - inner * inner) * SQRT_TWO_PI * (
        1.0 + 3.0 * CUBIC * square
    )
    return 0.5 * value * (1.0 + inner), slope


def dot(a, b, contract):
    return lax.dot_general(a, b, (contract, ((), ())), preferred_element_type=F32)


def assemble(own, after, before, block, devices):
    side = 2 * SIDE
    pairs = own.shape[1]
    column = lax.broadcasted_iota(jnp.int32, (2, side), 1)
    after = jnp.where(block == devices - 1, -1, after[:, :side])
    before = jnp.where(block == 0, -1, before[:, pairs - side :])
    return jnp.concatenate([own, jnp.where(column < SIDE, after, before)], axis=1)


def tap_onehots(bases, start, width):
    total = bases.shape[1]
    before = pltpu.roll(bases, (1 - start) % total, 1)[:, :width]
    here = bases[:, :width] if start == 0 else pltpu.roll(bases, -start % total, 1)[:, :width]
    after = pltpu.roll(bases, (-1 - start) % total, 1)[:, :width]
    taps = [before[0:1], before[1:2], here[0:1], here[1:2], after[0:1], after[1:2]]
    row = lax.broadcasted_iota(jnp.int32, (4 * KW, width), 0)
    tap, base = row >> 2, row & 3
    out = []
    for first in (0, 1):
        value = jnp.full((4 * KW, width), -1, jnp.int32)
        for k in range(KW):
            value = jnp.where(tap == k, jnp.broadcast_to(taps[first + k], value.shape), value)
        out.append(jnp.where(value == base, 1.0, 0.0).astype(BF16))
    return out


def valid_pairs(shape, dim, first, total):
    pair = lax.broadcasted_iota(jnp.int32, shape, dim) + first
    return (pair >= 0) & (pair < total)


def stem_kernel(place, own, after, before, stem_own, stem_oth, w_own, acc, stem_out, lhs_oth, even, odd, lhs, *, pairs, devices):
    seq, hi, lo = place[0], place[1], place[2]
    rows = pairs + 2 * INNER
    wide = pairs + 2 * OUTER
    block = acc.shape[1] // 2
    bases = assemble(own[...], after[...], before[...], seq, devices)
    hots = tap_onehots(bases, -OUTER, wide)
    gap = OUTER - INNER
    for weight, held_lhs in ((stem_own, lhs), (stem_oth, lhs_oth)):
        for hot, held in zip(hots, (even, odd)):
            raw = dot(hot, weight[...], ((0,), (0,)))
            ok = valid_pairs(raw.shape, 0, seq * pairs - OUTER, pairs * devices)
            held[...] = jnp.where(ok, gelu_value(raw), 0.0).astype(BF16).astype(F32)
        for k in range(6):
            source = even if k % 2 == 0 else odd
            held_lhs[k] = source[gap + k // 2 - 1 : gap + k // 2 - 1 + rows, :].astype(BF16)
    stem_out[0] = lhs[2]
    stem_out[1] = lhs[3]
    for part in range(2):
        at = pl.multiple_of((2 * (hi if part == 0 else 1 - hi) + lo) * block, 128)
        total = jnp.zeros((2 * rows, block), F32)
        for k in range(KW):
            total = total + dot(lhs[k : k + 2].reshape(2 * rows, -1), w_own[k, :, pl.ds(at, block)], ((1,), (0,)))
        acc[:, part * block : (part + 1) * block] = total


def enc_kernel(place, acc, lhs, w_oth, keep, send):
    hi = place[1]
    rows, block = keep.shape
    for part in range(2):
        at = pl.multiple_of((hi if part == 0 else 1 - hi) * block, 128)
        total = acc[:, part * block : (part + 1) * block]
        for k in range(KW):
            total = total + dot(lhs[k : k + 2].reshape(rows, -1), w_oth[k, :, pl.ds(at, block)], ((1,), (0,)))
        if part == 0:
            keep[...] = total
        else:
            send[...] = total.astype(BF16)


def pool_kernel(place, keep, came, pooled, centre, slope, *, pairs, total):
    rows = pairs + 2 * INNER
    value = keep[...] + came[...].astype(F32)
    active, grad = gelu_both(value)
    active = active.astype(BF16).astype(F32)
    both = 0.5 * (active[:rows] + active[rows:])
    ok = valid_pairs(both.shape, 0, place[0] * pairs - INNER, total)
    both = jnp.where(ok, both, 0.0).astype(BF16)
    pooled[...] = both
    centre[...] = both[INNER : INNER + pairs].astype(BF16)
    grad = 0.5 * grad
    slope[0] = grad[INNER : INNER + pairs]
    slope[1] = grad[rows + INNER : rows + INNER + pairs]


def dec_kernel(own, oth, w_own, w_oth, stem, targets, part, send, held, *, pairs):
    rows = pairs + 2 * INNER
    held[:8] = jnp.zeros((8, held.shape[1]), F32)
    held[8 + rows :] = jnp.zeros((8, held.shape[1]), F32)
    acc = jnp.zeros(part.shape, F32)
    for source, weight in ((own, w_own), (oth, w_oth)):
        held[8 : 8 + rows] = source[...].astype(F32)
        for k in range(3):
            acc = acc + dot(held[7 + k : 7 + k + rows].astype(BF16), weight[k], ((1,), (1,)))
    half = part.shape[1] // 2
    for parity in range(2):
        value = acc[:, parity * half : (parity + 1) * half]
        value = value + stem[parity].astype(F32) - targets[parity].astype(F32)
        part[:, parity * half : (parity + 1) * half] = value
        send[:, parity * half : (parity + 1) * half] = value.astype(BF16)


def slope_kernel(place, part, came, targets, pred, sums, low, high, held, *, pairs, total, scale):
    rows = pairs + 2 * INNER
    half = part.shape[1] // 2
    ok = valid_pairs((rows, half), 0, place[0] * pairs - INNER, total)
    slopes = []
    for parity in range(2):
        cols = slice(parity * half, (parity + 1) * half)
        value = part[:, cols] + came[:, cols].astype(F32)
        out = value + targets[parity].astype(F32)
        pred[parity] = out[INNER : INNER + pairs].astype(BF16)
        slopes.append(jnp.where(ok, value * scale, 0.0).astype(BF16).astype(F32))
    held[:rows] = slopes[0]
    held[rows:] = jnp.zeros((8, half), F32)
    for i, value in enumerate((slopes[0] + slopes[1], slopes[1] + held[1 : 1 + rows])):
        value = value.astype(BF16)
        sums[i] = value
        low[i] = value[:, : half // 2]
        high[i] = value[:, half // 2 :]


def lane_tiles(channels):
    return [(first, min(first + 128, channels)) for first in range(0, channels, 128)]


def targets_kernel(place, own, before, after, out, held):
    channels, count = own.shape
    side = before.shape[1]
    rows = count // 2 + 2 * INNER
    high = place[1] == 1
    for first, last in lane_tiles(channels):
        wide = last - first
        held[:side, :wide] = before[first:last].astype(F32).T
        held[side : side + count, :wide] = own[first:last].astype(F32).T
        held[side + count :, :wide] = after[first:last].astype(F32).T
        for parity in range(2):
            value = held[pl.ds(side - 2 * INNER + parity, rows, stride=2), :][:, :wide].astype(BF16)
            blank = jnp.zeros_like(value)
            out[parity, :, first:last] = jnp.where(high, blank, value)
            out[parity, :, channels + first : channels + last] = jnp.where(high, value, blank)


def pred_kernel(place, source, out, held):
    channels, count = out.shape
    for first, last in lane_tiles(channels):
        wide = last - first
        for parity in range(2):
            value = source[parity].astype(F32)
            value = jnp.where(place[1] == 1, value[:, channels + first : channels + last], value[:, first:last])
            if wide < 128:
                value = jnp.concatenate([value, jnp.zeros((count // 2, 128 - wide), F32)], axis=1)
            held[pl.ds(parity, count // 2, stride=2), :] = value
        out[first:last] = held[:, :wide].T.astype(BF16)


def shifted_sums(held, pairs):
    return [
        held[0, INNER + 1 : INNER + 1 + pairs].astype(BF16),
        held[1, INNER : INNER + pairs].astype(BF16),
        held[0, INNER : INNER + pairs].astype(BF16),
        held[1, INNER - 1 : INNER - 1 + pairs].astype(BF16),
        held[0, INNER - 1 : INNER - 1 + pairs].astype(BF16),
    ]


def back_kernel(own, oth, w_own, w_oth, slope, out, held, *, pairs):
    acc = jnp.zeros((pairs, out.shape[2]), F32)
    for source, weight in ((own, w_own), (oth, w_oth)):
        held[...] = source[...].astype(F32)
        for k, tap in enumerate(shifted_sums(held, pairs)):
            acc = acc + dot(tap, weight[k], ((1,), (0,)))
    out[0] = (acc * slope[0]).astype(BF16)
    out[1] = (acc * slope[1]).astype(BF16)


def taps_kernel(place, *refs, pairs, devices):
    blocks, (stem_w, out) = refs[:devices], refs[devices:]
    channels = stem_w.shape[0]
    for r in range(devices):
        block = lax.rem(place[0] - r + devices, devices)
        bases = assemble(blocks[r][...], blocks[r - 1][...], blocks[(r + 1) % devices][...], block, devices)
        width = bases.shape[1]
        parts = []
        for hot in tap_onehots(bases, 0, width):
            raw = dot(stem_w[...], hot, ((1,), (0,)))
            column = lax.broadcasted_iota(jnp.int32, raw.shape, 1)
            pair = jnp.where(column >= width - SIDE, column - width, column) + block * pairs
            ok = (pair >= 0) & (pair < pairs * devices)
            parts.append(jnp.where(ok, gelu_value(raw), 0.0))
        taps = []
        for step in (-1, 0, 1):
            for held in parts:
                moved = held if step == 0 else pltpu.roll(held, -step % width, 1)
                taps.append(moved[:, :pairs].astype(BF16))
        at = 2 * r * pairs
        for k in range(KW):
            out[k * channels : (k + 1) * channels, at : at + pairs] = taps[k]
            out[k * channels : (k + 1) * channels, at + pairs : at + 2 * pairs] = taps[k + 1]


def pick_kernel(place, source, out):
    out[...] = source[...]


def dec_pick_kernel(place, own, oth, own_out, oth_out, comb):
    own_out[...] = own[...]
    oth_out[...] = oth[...]
    combine(own, comb)


def comb_kernel(came, comb):
    combine(came, comb)


def combine(weight, comb):
    comb[0, 0] = weight[0] + weight[1]
    comb[1, 0] = weight[2] + weight[3]
    comb[2, 0] = weight[4]
    comb[0, 1] = weight[0]
    comb[1, 1] = weight[1] + weight[2]
    comb[2, 1] = weight[3] + weight[4]


def dec_grad_kernel(place, own0, own1, oth0, oth1, pool0, pool1, pool2, pool3, out, held, taps, pooled, *, pairs):
    slots = (own0, own1, oth0, oth1)
    blocks = (pool0, pool1, pool2, pool3)
    parity = place[3]
    odd = lax.rem(place[0], 2)
    for block, step in zip(blocks, (0, 3 - 2 * odd, 2, 1 + 2 * odd)):
        pooled[pl.ds(pl.multiple_of(step * pairs, pairs), pairs), :] = block[...]
    for i, slot in enumerate(slots):
        held[...] = slot[...].astype(F32)
        step = 2 * (i % 2) + (parity if i < 2 else 1 - parity)
        at = pl.ds(pl.multiple_of(step * pairs, pairs), pairs)
        for k, tap in enumerate(shifted_sums(held, pairs)):
            taps[k, at, :] = tap
    for k in range(KW):
        out[k] = dot(taps[k], pooled[...], ((0,), (0,)))


def enc_grad_kernel(place, taps, own0, own1, oth0, oth1, out, joined):
    @pl.when(pl.program_id(0) == 0)
    def _():
        size = own0.shape[0]
        for i, slot in enumerate((own0, own1, oth0, oth1)):
            step = 2 * (i % 2) + (place[3] if i < 2 else 1 - place[3])
            joined[pl.ds(pl.multiple_of(step * size, size), size), :] = slot[...]

    out[...] = dot(taps[...], joined[...], ((1,), (0,)))


def whole(shape):
    return pl.BlockSpec(shape, lambda *_: (0,) * len(shape))


SCALARS = pl.BlockSpec(memory_space=pltpu.SMEM)


def call(kernel, ins, outs, scratch=(), limit=48, flops=0, name=None):
    specs = [SCALARS if i.dtype == jnp.int32 and i.ndim == 1 else whole(i.shape) for i in ins]
    size = sum(i.size * i.dtype.itemsize for i in ins) + sum(
        math.prod(s) * jnp.dtype(d).itemsize for s, d in outs
    )
    return pl.pallas_call(
        kernel,
        in_specs=specs,
        out_specs=[whole(s) for s, _ in outs],
        out_shape=[jax.ShapeDtypeStruct(s, d) for s, d in outs],
        scratch_shapes=[pltpu.VMEM(s, d) for s, d in scratch],
        compiler_params=pltpu.CompilerParams(vmem_limit_bytes=limit * MIB),
        cost_estimate=pl.CostEstimate(flops=flops, bytes_accessed=size, transcendentals=0),
        name=name,
    )(*ins)


def gated(values, gates):
    return lax.optimization_barrier((values, gates))[0]


def shards(dna_bases, w_stem, w_enc, w_dec, targets):
    devices = lax.axis_size("seq")
    seq, chan = lax.axis_index("seq"), lax.axis_index("chan")
    hi, lo = chan // 2, chan % 2
    parity = lax.rem(lo + seq, 2)
    place = jnp.stack([seq, hi, lo, parity]).astype(jnp.int32)
    pairs = dna_bases.shape[0] // 2
    total = pairs * devices
    rows = pairs + 2 * INNER
    stem_c = w_stem.shape[0]
    enc_c = w_dec.shape[2]
    across = [(c, c ^ 2) for c in range(4)]
    cores = [(c, c ^ 1) for c in range(4)]

    def ring(array, step):
        return lax.ppermute(array, "seq", [(i, (i + step) % devices) for i in range(devices)])

    def swap(array, distance):
        return lax.ppermute(array, "seq", [(i, i ^ distance) for i in range(devices)])

    own = dna_bases.reshape(pairs, 2).T
    blocks = {0: own, 1: ring(own, 1), devices - 1: ring(own, devices - 1)}

    stem_w = w_stem.transpose(1, 2, 0).reshape(4 * KW, stem_c)
    stem_oth = lax.ppermute(stem_w, "chan", cores)
    enc_w = w_enc.transpose(1, 2, 0)
    enc_send = pl.pallas_call(
        pick_kernel,
        grid_spec=pltpu.PrefetchScalarGridSpec(
            num_scalar_prefetch=1,
            grid=(2,),
            in_specs=[pl.BlockSpec((KW, stem_c, enc_c), lambda h, at: (0, 0, 2 * h + 1 - at[2]))],
            out_specs=pl.BlockSpec((KW, stem_c, enc_c), lambda h, at: (0, 0, h)),
        ),
        out_shape=jax.ShapeDtypeStruct((KW, stem_c, 2 * enc_c), BF16),
        compiler_params=pltpu.CompilerParams(vmem_limit_bytes=8 * MIB),
        name="enc_pick",
    )(place, enc_w)
    enc_oth = lax.ppermute(enc_send, "chan", cores)

    dec_w = w_dec.transpose(1, 0, 2).reshape(KW, 4, stem_c, enc_c)
    picked = (KW, 1, stem_c, enc_c)
    dec_own, dec_oth, comb_own = pl.pallas_call(
        dec_pick_kernel,
        grid_spec=pltpu.PrefetchScalarGridSpec(
            num_scalar_prefetch=1,
            grid=(2,),
            in_specs=[
                pl.BlockSpec(picked, lambda h, at: (0, 2 * h + at[2], 0, 0)),
                pl.BlockSpec(picked, lambda h, at: (0, 2 * h + 1 - at[2], 0, 0)),
            ],
            out_specs=[
                pl.BlockSpec(picked, lambda h, at: (0, h, 0, 0)),
                pl.BlockSpec(picked, lambda h, at: (0, h, 0, 0)),
                pl.BlockSpec((3, 2, 1, stem_c, enc_c), lambda h, at: (0, 0, h, 0, 0)),
            ],
        ),
        out_shape=[
            jax.ShapeDtypeStruct((KW, 2, stem_c, enc_c), BF16),
            jax.ShapeDtypeStruct((KW, 2, stem_c, enc_c), BF16),
            jax.ShapeDtypeStruct((3, 2, 2, stem_c, enc_c), BF16),
        ],
        compiler_params=pltpu.CompilerParams(vmem_limit_bytes=12 * MIB),
        name="dec_pick",
    )(place, dec_w, dec_w)
    blocks[1], blocks[devices - 1] = gated((blocks[1], blocks[devices - 1]), (dec_own, dec_oth, comb_own))
    acc, stem, lhs = call(
        functools.partial(stem_kernel, pairs=pairs, devices=devices),
        [place, own, blocks[devices - 1], blocks[1], stem_w, stem_oth, enc_w],
        [((2 * rows, 2 * enc_c), F32), ((2, rows, stem_c), BF16), ((6, rows, stem_c), BF16)],
        [
            ((pairs + 2 * OUTER, stem_c), F32),
            ((pairs + 2 * OUTER, stem_c), F32),
            ((6, rows, stem_c), BF16),
        ],
        limit=14,
        flops=4 * rows * stem_c * KW * 2 * enc_c,
        name="stem_conv",
    )
    keep, send = call(
        enc_kernel,
        [place, acc, lhs, enc_oth],
        [((2 * rows, enc_c), F32), ((2 * rows, enc_c), BF16)],
        limit=12,
        flops=4 * rows * stem_c * KW * 2 * enc_c,
        name="enc_conv",
    )
    came = lax.ppermute(send, "chan", across)

    dec_oth, targets_in, own_in = gated((dec_oth, targets, own), send)
    for r in range(2, devices - 1):
        blocks[r] = ring(own_in, r)
    dec_came = lax.ppermute(dec_oth, "chan", cores)
    comb_came = pl.pallas_call(
        comb_kernel,
        grid=(2,),
        in_specs=[pl.BlockSpec(picked, lambda h: (0, h, 0, 0))],
        out_specs=pl.BlockSpec((3, 2, 1, stem_c, enc_c), lambda h: (0, 0, h, 0, 0)),
        out_shape=jax.ShapeDtypeStruct((3, 2, 2, stem_c, enc_c), BF16),
        compiler_params=pltpu.CompilerParams(vmem_limit_bytes=8 * MIB),
        name="dec_combine",
    )(dec_came)
    targets_in = targets_in.T
    count, edge = 2 * pairs, 2 * SIDE
    (targets_at,) = call(
        targets_kernel,
        [place, targets_in, ring(targets_in[:, count - edge :], 1), ring(targets_in[:, :edge], devices - 1)],
        [((2, rows, 2 * stem_c), BF16)],
        [((count + 2 * edge, 128), F32)],
        limit=6,
        name="targets",
    )
    blank = jnp.zeros_like(stem)
    stem_at = jnp.where(hi == 0, jnp.concatenate([stem, blank], axis=2), jnp.concatenate([blank, stem], axis=2))
    came = gated(came, (comb_came, targets_at, stem_at, [blocks[r] for r in range(2, devices - 1)]))

    pooled, centre, slope = call(
        functools.partial(pool_kernel, pairs=pairs, total=total),
        [place, keep, came],
        [((rows, enc_c), BF16), ((pairs, enc_c), BF16), ((2, pairs, enc_c), F32)],
        limit=8,
        name="gelu_pool",
    )
    pooled_oth = lax.ppermute(pooled, "chan", cores)
    part, send = call(
        functools.partial(dec_kernel, pairs=pairs),
        [
            pooled,
            pooled_oth,
            comb_own.reshape(3, 4 * stem_c, enc_c),
            comb_came.reshape(3, 4 * stem_c, enc_c),
            stem_at,
            targets_at,
        ],
        [((rows, 4 * stem_c), F32), ((rows, 4 * stem_c), BF16)],
        [((rows + 16, enc_c), F32)],
        limit=11,
        flops=2 * rows * 2 * enc_c * 3 * 4 * stem_c,
        name="dec_conv",
    )
    came = lax.ppermute(send, "chan", across)

    centre = gated(centre, send)
    beyond, beside = swap(centre, 2), swap(centre, 1)
    (taps,) = call(
        functools.partial(taps_kernel, pairs=pairs, devices=devices),
        [place] + [blocks[r] for r in range(devices)] + [stem_w.T],
        [((KW * stem_c, 2 * pairs * devices), BF16)],
        limit=12,
        name="stem_taps",
    )
    came, beyond, beside = gated((came, beyond, beside), taps)
    pooled_all = [centre, beside, beyond, swap(beyond, 1)]

    pred, sums, low, high = call(
        functools.partial(slope_kernel, pairs=pairs, total=total, scale=1.0 / math.sqrt(2 * total)),
        [place, part, came, targets_at],
        [
            ((2, pairs, 2 * stem_c), BF16),
            ((2, rows, 2 * stem_c), BF16),
            ((2, rows, stem_c), BF16),
            ((2, rows, stem_c), BF16),
        ],
        [((rows + 8, 2 * stem_c), F32)],
        limit=7,
        name="out_slope",
    )
    sums_oth = lax.ppermute(sums, "chan", cores)
    (pre,) = call(
        functools.partial(back_kernel, pairs=pairs),
        [
            sums,
            sums_oth,
            dec_own.reshape(KW, 2 * stem_c, enc_c),
            dec_oth.reshape(KW, 2 * stem_c, enc_c),
            slope,
        ],
        [((2, pairs, enc_c), BF16)],
        [((2, rows, 2 * stem_c), F32)],
        limit=11,
        flops=2 * pairs * KW * 4 * stem_c * enc_c,
        name="up_grad",
    )
    (pred,) = call(
        pred_kernel,
        [place, pred],
        [((stem_c, 2 * pairs), BF16)],
        [((2 * pairs, 128), F32)],
        limit=5,
        name="pred",
    )
    pred = pred.T

    def link(steps):
        out = []
        for s in range(devices):
            for step in steps:
                t = (s + step) % devices
                for x in range(2):
                    out.append((s * 4 + 2 * x + t % 2, t * 4 + 2 * x + (t + step) % 2))
        return out

    def to_owner(first, second, gate=None):
        def piece(step):
            return jnp.where(lax.rem(seq + step, devices) < 2, first, second)

        near = lax.ppermute(piece(2 - parity), ("seq", "chan"), link((1, 2)))
        far = lax.ppermute(piece(3), ("seq", "chan"), link((3,)))
        local = piece(0)
        if gate is not None:
            near, far = gated((near, far), gate)
        mine = [jnp.where(parity == 0, local, near), jnp.where(parity == 0, near, far)]
        return mine, [lax.ppermute(m, "chan", cores) for m in mine]

    sums_mine, sums_came = to_owner(low, high)
    pre = pre.reshape(2 * pairs, enc_c)
    pre_oth = lax.ppermute(pre, "chan", across)
    pre_oth = gated(pre_oth, (sums_mine, pooled_all))

    (g_dec,) = call(
        functools.partial(dec_grad_kernel, pairs=pairs),
        [place] + sums_mine + sums_came + pooled_all,
        [((KW, stem_c, enc_c), F32)],
        [
            ((2, rows, stem_c), F32),
            ((KW, devices * pairs, stem_c), BF16),
            ((devices * pairs, enc_c), BF16),
        ],
        limit=12,
        flops=2 * KW * stem_c * devices * pairs * enc_c,
        name="dec_grad",
    )
    pre_mine, pre_came = to_owner(
        jnp.where(hi == 0, pre, pre_oth), jnp.where(hi == 0, pre_oth, pre), (g_dec, pred)
    )
    g_dec = g_dec.transpose(1, 0, 2)
    pre_slots = pre_mine + pre_came
    g_enc = pl.pallas_call(
        enc_grad_kernel,
        grid=(KW,),
        in_specs=[SCALARS, pl.BlockSpec((stem_c, 2 * pairs * devices), lambda k: (k, 0))]
        + [whole(p.shape) for p in pre_slots],
        out_specs=pl.BlockSpec((stem_c, enc_c), lambda k: (k, 0)),
        out_shape=jax.ShapeDtypeStruct((KW * stem_c, enc_c), F32),
        scratch_shapes=[pltpu.VMEM((2 * pairs * devices, enc_c), BF16)],
        compiler_params=pltpu.CompilerParams(vmem_limit_bytes=9 * MIB),
        name="enc_grad",
    )(place, taps, *pre_slots)
    g_enc = g_enc.reshape(KW, stem_c, enc_c).transpose(2, 0, 1)
    return (pred, g_enc, g_dec)


def extended(block, sides, width):
    for axis, dim in sides:
        count = lax.axis_size(axis)
        forward = [(i, i + 1) for i in range(count - 1)]
        backward = [(target, source) for source, target in forward]
        low = lax.ppermute(
            lax.slice_in_dim(block, block.shape[dim] - width, None, axis=dim), axis, forward
        )
        high = lax.ppermute(lax.slice_in_dim(block, 0, width, axis=dim), axis, backward)
        block = jnp.concatenate([low, block, high], axis=dim)
    return block


def gelu_slope(value):
    inner = jnp.tanh(SQRT_TWO_PI * (value + CUBIC * value * value * value))
    return 0.5 * (1.0 + inner) + 0.5 * value * (1.0 - inner * inner) * SQRT_TWO_PI * (
        1.0 + 3.0 * CUBIC * value * value
    )


def rim_cells(block, margin):
    return extended(block, (("seq", 0),), margin)


def channel_sum(partial_value):
    return lax.psum_scatter(partial_value, "chan", scatter_dimension=1, tiled=True)


def channel_gather(block):
    return lax.all_gather(block, "chan", axis=1, tiled=True)


def conv_rows(padded, weight):
    row_count = padded.shape[0] - 4
    total = jnp.zeros((row_count, weight.shape[0]), jnp.float32)
    for k in range(KW):
        total = total + lax.dot_general(
            padded[k : k + row_count],
            weight[:, k, :],
            (((1,), (1,)), ((), ())),
            preferred_element_type=jnp.float32,
        )
    return total


def grad_taps(picked, padded):
    row_count = picked.shape[0]
    pieces = [
        lax.dot_general(
            picked,
            padded[k : k + row_count],
            (((0,), (0,)), ((), ())),
            preferred_element_type=jnp.float32,
        )
        for k in range(KW)
    ]
    return jnp.stack(pieces, axis=1)


def weight_grad(cotangent, padded):
    rounded = grad_taps(cotangent, padded).astype(jnp.bfloat16)
    return lax.psum_scatter(
        lax.optimization_barrier(rounded).astype(jnp.float32),
        "seq",
        scatter_dimension=0,
        tiled=True,
    )


def general_shards(dna_bases, w_stem, w_enc, w_dec, targets):
    row_count = dna_bases.shape[0]
    devices = lax.axis_size("seq")
    length = row_count * devices
    onehot = (dna_bases[:, None] == jnp.arange(4, dtype=jnp.int32)[None, :]).astype(jnp.bfloat16)
    onehot_pad = rim_cells(onehot, 2)
    stem_out = gelu_value(conv_rows(onehot_pad, w_stem)).astype(jnp.bfloat16)
    stem_pad = rim_cells(stem_out, 2)
    enc_pre = channel_sum(conv_rows(stem_pad, w_enc))
    active = gelu_value(enc_pre).astype(jnp.bfloat16).astype(jnp.float32)
    pooled = (0.5 * active.reshape(row_count // 2, 2, -1).sum(axis=1)).astype(jnp.bfloat16)
    pooled_pad = rim_cells(pooled, 1)
    up_pad = jnp.repeat(pooled_pad, 2, axis=0)
    output = channel_sum(conv_rows(up_pad, w_dec)) + stem_out.astype(jnp.float32)
    pred = output.astype(jnp.bfloat16)
    scale = 1.0 / math.sqrt(length)
    slope_out = ((output - targets.astype(jnp.float32)) * scale).astype(jnp.bfloat16)
    slope_all = channel_gather(slope_out)
    g_dec = weight_grad(slope_all, up_pad)
    slope_pad = rim_cells(slope_all, 2)
    up_grad = jnp.zeros((row_count, w_dec.shape[2]), jnp.float32)
    for k in range(KW):
        up_grad = up_grad + jnp.dot(
            slope_pad[4 - k : 4 - k + row_count], w_dec[:, k, :], preferred_element_type=jnp.float32
        )
    pool_grad = up_grad.reshape(row_count // 2, 2, -1).sum(axis=1)
    act_grad = 0.5 * jnp.repeat(pool_grad, 2, axis=0)
    pre_grad = (act_grad * gelu_slope(enc_pre)).astype(jnp.bfloat16)
    pre_all = channel_gather(pre_grad)
    g_enc = weight_grad(pre_all, stem_pad)
    return (pred, g_enc, g_dec)


def solution(mesh):
    sizes = mesh.shape["seq"], mesh.shape["chan"]
    return jax.shard_map(
        shards if sizes == (4, 4) else general_shards,
        mesh=mesh,
        in_specs=(
            P(("groups", "seq")),
            P("chan", None, None),
            P(None, None, "chan"),
            P(None, None, "chan"),
            P(("groups", "seq"), "chan"),
        ),
        out_specs=(
            P(("groups", "seq"), "chan"),
            P(("groups", "seq"), None, "chan"),
            P(("groups", "seq"), None, "chan"),
        ),
        check_vma=False,
    )
```

```python
import functools
import math

import jax
import jax.numpy as jnp
from jax import lax
from jax.experimental import pallas as pl
from jax.experimental.pallas import tpu as pltpu
from jax.sharding import PartitionSpec as P

KW = 5

SQRT_TWO_PI = 0.7978845608028654
CUBIC = 0.044715

STEM_ROWS = 32
SIDE = 64
OUTER = 16
INNER = 8
F32 = jnp.float32
BF16 = jnp.bfloat16
MIB = 1024 * 1024


def gelu_value(value):
    inner = jnp.tanh(SQRT_TWO_PI * (value + CUBIC * value * value * value))
    return 0.5 * value * (1.0 + inner)


def gelu_slope(value):
    inner = jnp.tanh(SQRT_TWO_PI * (value + CUBIC * value * value * value))
    return 0.5 * (1.0 + inner) + 0.5 * value * (1.0 - inner * inner) * SQRT_TWO_PI * (
        1.0 + 3.0 * CUBIC * value * value
    )


def dot(a, b, contract):
    return lax.dot_general(a, b, (contract, ((), ())), preferred_element_type=F32)


def assemble(own, after, before, block, devices):
    side = 2 * SIDE
    pairs = own.shape[1]
    column = lax.broadcasted_iota(jnp.int32, (2, side), 1)
    after = jnp.where(block == devices - 1, -1, after[:, :side])
    before = jnp.where(block == 0, -1, before[:, pairs - side :])
    return jnp.concatenate([own, jnp.where(column < SIDE, after, before)], axis=1)


def split_parity(bases):
    count = bases.shape[1]
    row = lax.broadcasted_iota(jnp.int32, (count, count), 0)
    column = lax.broadcasted_iota(jnp.int32, (count, count), 1)
    source = jnp.where(column < count // 2, 2 * column, 2 * column - count + 1)
    chosen = jnp.where(row == source, 1.0, 0.0).astype(BF16)
    wide = jnp.broadcast_to(bases, (16, count)).astype(F32).astype(BF16)
    value = dot(wide, chosen, ((1,), (0,))).astype(jnp.int32)
    return jnp.concatenate([value[0:1, : count // 2], value[0:1, count // 2 :]], axis=0)


def tap_onehots(bases, start, width):
    total = bases.shape[1]
    before = pltpu.roll(bases, (1 - start) % total, 1)[:, :width]
    here = bases[:, :width] if start == 0 else pltpu.roll(bases, -start % total, 1)[:, :width]
    after = pltpu.roll(bases, (-1 - start) % total, 1)[:, :width]
    taps = [before[0:1], before[1:2], here[0:1], here[1:2], after[0:1], after[1:2]]
    row = lax.broadcasted_iota(jnp.int32, (4 * KW, width), 0)
    tap, base = row >> 2, row & 3
    out = []
    for first in (0, 1):
        value = jnp.full((4 * KW, width), -1, jnp.int32)
        for k in range(KW):
            value = jnp.where(tap == k, jnp.broadcast_to(taps[first + k], value.shape), value)
        out.append(jnp.where(value == base, 1.0, 0.0).astype(BF16))
    return out


def valid_pairs(shape, dim, first, total):
    pair = lax.broadcasted_iota(jnp.int32, shape, dim) + first
    return (pair >= 0) & (pair < total)


def stem_kernel(
    place, own, after, before, stem_own, w_oth, w_own, acc, stem_out, lhs_oth, split, even, odd, lhs, *, pairs, devices
):
    seq, hi, lo = place[0], place[1], place[2]
    rows = pairs + 2 * INNER
    wide = pairs + 2 * OUTER
    block = acc.shape[1] // 2
    swapped = lax.rem(seq, 2) == 1
    first, second = after[...], before[...]
    for i, raw in enumerate((own[...], jnp.where(swapped, second, first), jnp.where(swapped, first, second))):
        split[i] = split_parity(raw)
    hots = tap_onehots(assemble(split[0], split[1], split[2], seq, devices), -OUTER, wide)
    gap = OUTER - INNER
    stem_oth = w_oth[: stem_own.shape[0], : stem_own.shape[1]]
    for weight, held_lhs in ((stem_own[...], lhs), (stem_oth, lhs_oth)):
        for hot, held in zip(hots, (even, odd)):
            raw = dot(hot, weight, ((0,), (0,)))
            ok = valid_pairs(raw.shape, 0, seq * pairs - OUTER, pairs * devices)
            held[...] = jnp.where(ok, gelu_value(raw), 0.0).astype(BF16).astype(F32)
        for k in range(6):
            source = even if k % 2 == 0 else odd
            held_lhs[k] = source[gap + k // 2 - 1 : gap + k // 2 - 1 + rows, :].astype(BF16)
    stem_out[0] = lhs[2]
    stem_out[1] = lhs[3]
    for part in range(2):
        at = pl.multiple_of((2 * (hi if part == 0 else 1 - hi) + lo) * block, 128)
        total = jnp.zeros((2 * rows, block), F32)
        for k in range(KW):
            total = total + dot(lhs[k : k + 2].reshape(2 * rows, -1), w_own[k, :, pl.ds(at, block)], ((1,), (0,)))
        acc[:, part * block : (part + 1) * block] = total


def enc_kernel(place, acc, lhs, w_oth, keep, send):
    hi = place[1]
    rows, block = keep.shape
    for part in range(2):
        at = pl.multiple_of((hi if part == 0 else 1 - hi) * block, 128)
        total = acc[:, part * block : (part + 1) * block]
        for k in range(KW):
            total = total + dot(lhs[k : k + 2].reshape(rows, -1), w_oth[k * lhs.shape[2] : (k + 1) * lhs.shape[2], pl.ds(at, block)], ((1,), (0,)))
        if part == 0:
            keep[...] = total
        else:
            send[...] = total.astype(BF16)


def pool_kernel(place, keep, came, pooled, centre, *, pairs, total):
    rows = pairs + 2 * INNER
    value = keep[...] + came[...].astype(F32)
    active = gelu_value(value).astype(BF16).astype(F32)
    both = 0.5 * (active[:rows] + active[rows:])
    ok = valid_pairs(both.shape, 0, place[0] * pairs - INNER, total)
    both = jnp.where(ok, both, 0.0).astype(BF16)
    pooled[...] = both
    centre[...] = both[INNER : INNER + pairs].astype(BF16)


def dec_kernel(own, oth, w_own, w_oth, stem, targets, part, send, held, *, pairs):
    rows = pairs + 2 * INNER
    held[:8] = jnp.zeros((8, held.shape[1]), F32)
    held[8 + rows :] = jnp.zeros((8, held.shape[1]), F32)
    acc = jnp.zeros(part.shape, F32)
    for source, weight in ((own, w_own), (oth, w_oth)):
        held[8 : 8 + rows] = source[...].astype(F32)
        for k in range(3):
            acc = acc + dot(held[7 + k : 7 + k + rows].astype(BF16), weight[k], ((1,), (1,)))
    half = part.shape[1] // 2
    for parity in range(2):
        value = acc[:, parity * half : (parity + 1) * half]
        value = value + stem[parity].astype(F32) - targets[parity].astype(F32)
        part[:, parity * half : (parity + 1) * half] = value
        send[:, parity * half : (parity + 1) * half] = value.astype(BF16)


def slope_kernel(place, part, came, targets, pred, sums, local, near, far, held, *, pairs, total, scale):
    rows = pairs + 2 * INNER
    half = part.shape[1] // 2
    quarter = half // 2
    ok = valid_pairs((rows, half), 0, place[0] * pairs - INNER, total)
    second = place[1] == 1
    slopes = []
    for parity in range(2):
        cols = slice(parity * half, (parity + 1) * half)
        value = part[:, cols] + came[:, cols].astype(F32)
        out = (value + targets[parity].astype(F32))[INNER : INNER + pairs]
        pred[parity] = jnp.where(second, out[:, quarter:], out[:, :quarter]).astype(BF16)
        slopes.append(jnp.where(ok, value * scale, 0.0).astype(BF16).astype(F32))
    held[:rows] = slopes[0]
    held[rows:] = jnp.zeros((8, half), F32)
    both = slopes[0] + slopes[1], slopes[1] + held[1 : 1 + rows]
    for i in range(2):
        for h in range(2):
            sums[h, i] = both[i][:, h * quarter : (h + 1) * quarter].astype(BF16)
    for out, step in ((local, 0), (near, 2 - place[3]), (far, 3)):
        out[...] = sums[lax.rem(place[0] + step, 4) // 2]


def lane_tiles(channels):
    return [(first, min(first + 128, channels)) for first in range(0, channels, 128)]


def targets_kernel(place, own, before, after, out, held):
    channels, count = own.shape
    side = before.shape[1]
    rows = count // 2 + 2 * INNER
    high = place[1] == 1
    for first, last in lane_tiles(channels):
        wide = last - first
        held[:side, :wide] = before[first:last].astype(F32).T
        held[side : side + count, :wide] = own[first:last].astype(F32).T
        held[side + count :, :wide] = after[first:last].astype(F32).T
        for parity in range(2):
            value = held[pl.ds(side - 2 * INNER + parity, rows, stride=2), :][:, :wide].astype(BF16)
            blank = jnp.zeros_like(value)
            out[parity, :, first:last] = jnp.where(high, blank, value)
            out[parity, :, channels + first : channels + last] = jnp.where(high, value, blank)


def pred_kernel(source, out, held):
    channels, count = out.shape
    for first, last in lane_tiles(channels):
        wide = last - first
        for parity in range(2):
            value = source[parity, :, first:last].astype(F32)
            if wide < 128:
                value = jnp.concatenate([value, jnp.zeros((count // 2, 128 - wide), F32)], axis=1)
            held[pl.ds(parity, count // 2, stride=2), :] = value
        out[first:last] = held[:, :wide].T.astype(BF16)


def shifted_sums(held, pairs):
    return [
        held[0, INNER + 1 : INNER + 1 + pairs].astype(BF16),
        held[1, INNER : INNER + pairs].astype(BF16),
        held[0, INNER : INNER + pairs].astype(BF16),
        held[1, INNER - 1 : INNER - 1 + pairs].astype(BF16),
        held[0, INNER - 1 : INNER - 1 + pairs].astype(BF16),
    ]


def back_kernel(place, own, oth, weight, out, held, *, pairs):
    acc = jnp.zeros(out.shape, F32)
    for source, core in ((own, place[2]), (oth, 1 - place[2])):
        for h in range(2):
            held[...] = source[h].astype(F32)
            for k, tap in enumerate(shifted_sums(held, pairs)):
                acc = acc + dot(tap, weight[k, 2 * h + core], ((1,), (0,)))
    out[...] = (0.5 * acc).astype(BF16)


def owner_slope_kernel(place, *refs, slot, pairs, devices):
    blocks, weights = refs[:devices], refs[devices : devices + 4]
    out, bases, even, odd, lhs = refs[devices + 4 :]
    for r in range(devices):
        bases[r] = blocks[r][...]
    wide = pairs + 2 * INNER
    step = 2 * slot + place[3]
    block = lax.rem(place[0] - step + devices, devices)
    before, after = lax.rem(step + 1, devices), lax.rem(step + devices - 1, devices)
    joined = assemble(bases[step], bases[after], bases[before], block, devices)
    hots = tap_onehots(joined, -INNER, wide)
    total = jnp.zeros(out.shape, F32)
    for kernel in weights:
        channels = lhs.shape[2]
        weight = kernel[KW * channels : KW * channels + 4 * KW, :channels]
        for hot, held in zip(hots, (even, odd)):
            raw = dot(hot, weight, ((0,), (0,)))
            ok = valid_pairs(raw.shape, 0, block * pairs - INNER, pairs * devices)
            held[...] = jnp.where(ok, gelu_value(raw), 0.0).astype(BF16).astype(F32)
        for k in range(6):
            source = even if k % 2 == 0 else odd
            lhs[k] = source[INNER + k // 2 - 1 : INNER + k // 2 - 1 + pairs, :].astype(BF16)
        for k in range(KW):
            total = total + dot(
                lhs[k : k + 2].reshape(2 * pairs, -1), kernel[k * channels : (k + 1) * channels, :], ((1,), (0,))
            )
    out[...] = gelu_slope(total).astype(BF16)


def taps_kernel(place, *refs, pairs, devices):
    blocks, (stem_w, out) = refs[:devices], refs[devices:]
    channels = stem_w.shape[1]
    for r in range(devices):
        block = lax.rem(place[0] - r + devices, devices)
        bases = assemble(blocks[r][...], blocks[r - 1][...], blocks[(r + 1) % devices][...], block, devices)
        width = bases.shape[1]
        parts = []
        for hot in tap_onehots(bases, 0, width):
            raw = dot(stem_w[...], hot, ((0,), (0,)))
            column = lax.broadcasted_iota(jnp.int32, raw.shape, 1)
            pair = jnp.where(column >= width - SIDE, column - width, column) + block * pairs
            ok = (pair >= 0) & (pair < pairs * devices)
            parts.append(jnp.where(ok, gelu_value(raw), 0.0))
        taps = []
        for step in (-1, 0, 1):
            for held in parts:
                moved = held if step == 0 else pltpu.roll(held, -step % width, 1)
                taps.append(moved[:, :pairs].astype(BF16))
        at = 2 * r * pairs
        for k in range(KW):
            out[k * channels : (k + 1) * channels, at : at + pairs] = taps[k]
            out[k * channels : (k + 1) * channels, at + pairs : at + 2 * pairs] = taps[k + 1]


def picks_kernel(place, stem, enc, mine, enc_oth, sems):
    seq, core = place[0], 1 - place[2]
    taps, channels, _ = enc.shape
    block = mine.shape[1]

    def columns(index):
        return pl.ds(pl.multiple_of(index * block, 128), block)

    copies = []
    for k in range(taps):
        rows = pl.ds(k * channels, channels)
        for h in range(2):
            copies.append((enc.at[k, :, columns(2 * h + core)], enc_oth.at[rows, h * block : (h + 1) * block]))
        copies.append((enc.at[k, :, columns(seq)], mine.at[rows]))
    copies = [pltpu.make_async_copy(*ends, sems.at[i]) for i, ends in enumerate(copies)]
    for copy in copies:
        copy.start()
    enc_oth[taps * channels :, : stem.shape[1]] = stem[...]
    mine[taps * channels :, : stem.shape[1]] = stem[...]
    for copy in copies:
        copy.wait()


def pick_kernel(place, source, out):
    out[...] = source[...]


def comb_kernel(place, own, came, comb_own, comb_came):
    combine(own, comb_own)
    combine(came, comb_came)


def combine(weight, comb):
    comb[0, 0] = weight[0] + weight[1]
    comb[1, 0] = weight[2] + weight[3]
    comb[2, 0] = weight[4]
    comb[0, 1] = weight[0]
    comb[1, 1] = weight[1] + weight[2]
    comb[2, 1] = weight[3] + weight[4]


def dec_grad_kernel(place, own, came, pool0, pool1, pool2, pool3, out, held, taps, pooled, *, pairs):
    blocks = (pool0, pool1, pool2, pool3)
    parity = place[3]
    odd = lax.rem(place[0], 2)
    for block, step in zip(blocks, (0, 3 - 2 * odd, 2, 1 + 2 * odd)):
        pooled[pl.ds(pl.multiple_of(step * pairs, pairs), pairs), :] = block[...]
    for i in range(4):
        slots = own if i < 2 else came
        held[...] = slots[i % 2].astype(F32)
        step = 2 * (i % 2) + (parity if i < 2 else 1 - parity)
        at = pl.ds(pl.multiple_of(step * pairs, pairs), pairs)
        for k, tap in enumerate(shifted_sums(held, pairs)):
            taps[k, at, :] = tap
    for k in range(KW):
        out[k] = dot(taps[k], pooled[...], ((0,), (0,)))


def enc_grad_kernel(place, taps, own, came, slope0, slope1, slope2, slope3, out, joined):
    @pl.when(pl.program_id(0) == 0)
    def _():
        pairs = own.shape[1]
        for i, slope in enumerate((slope0, slope1, slope2, slope3)):
            step = 2 * (i % 2) + (place[3] if i < 2 else 1 - place[3])
            grad = (own if i < 2 else came)[i % 2].astype(F32)
            for parity in range(2):
                value = grad * slope[parity * pairs : (parity + 1) * pairs].astype(F32)
                at = pl.multiple_of((2 * step + parity) * pairs, pairs)
                joined[pl.ds(at, pairs), :] = value.astype(BF16)

    out[...] = dot(taps[...], joined[...], ((1,), (0,)))


def whole(shape):
    return pl.BlockSpec(shape, lambda *_: (0,) * len(shape))


SCALARS = pl.BlockSpec(memory_space=pltpu.SMEM)


def call(kernel, ins, outs, scratch=(), limit=16, name=None, last=()):
    specs = [SCALARS if i.dtype == jnp.int32 and i.ndim == 1 else whole(i.shape) for i in ins]
    for at in last:
        shape = ins[at].shape
        specs[at] = pl.BlockSpec((STEM_ROWS,) + shape[1:], lambda *_: (shape[0] // STEM_ROWS - 1, 0))
    return pl.pallas_call(
        kernel,
        grid=(1,) if last else (),
        in_specs=specs,
        out_specs=[whole(s) for s, _ in outs],
        out_shape=[jax.ShapeDtypeStruct(s, d) for s, d in outs],
        scratch_shapes=[pltpu.VMEM(s, d) for s, d in scratch],
        compiler_params=pltpu.CompilerParams(vmem_limit_bytes=limit * MIB),
        name=name,
    )(*ins)


def gated(values, gates):
    return lax.optimization_barrier((values, gates))[0]


def shards(dna_bases, w_stem, w_enc, w_dec, targets):
    devices = lax.axis_size("seq")
    seq, chan = lax.axis_index("seq"), lax.axis_index("chan")
    hi, lo = chan // 2, chan % 2
    parity = (lo + seq) % 2
    pairs = dna_bases.shape[0] // 2
    total = pairs * devices
    rows = pairs + 2 * INNER
    stem_c = w_stem.shape[0]
    enc_c = w_dec.shape[2]
    across = [(c, c ^ 2) for c in range(4)]
    cores = [(c, c ^ 1) for c in range(4)]

    def ring(array, step):
        return lax.ppermute(array, "seq", [(i, (i + step) % devices) for i in range(devices)])

    def swap(array, distance):
        return lax.ppermute(array, "seq", [(i, i ^ distance) for i in range(devices)])

    place = jnp.stack([seq, hi, lo, parity]).astype(jnp.int32)
    first_chip, even = hi == 0, parity == 0
    target = [(seq + step) % devices // 2 == hi for step in (0, 2 - parity, 3)]
    own = dna_bases.reshape(1, 2 * pairs)
    stem_w = w_stem.transpose(1, 2, 0).reshape(4 * KW, stem_c)
    own, place, first_chip, even, target = lax.optimization_barrier((own, place, first_chip, even, target))

    first = swap(own, 1)
    second = lax.ppermute(own, "seq", [(i, (i + 1 - 2 * (1 - i % 2)) % devices) for i in range(devices)])
    enc_w = w_enc.transpose(1, 2, 0)
    dec_w = w_dec.transpose(1, 0, 2).reshape(KW, 4, stem_c, enc_c)
    picked = (KW, 1, stem_c, enc_c)
    stem_rows = jnp.concatenate([stem_w, jnp.zeros((STEM_ROWS - 4 * KW, stem_c), BF16)])
    mine, enc_send = pl.pallas_call(
        picks_kernel,
        in_specs=[SCALARS, whole(stem_rows.shape), pl.BlockSpec(memory_space=pl.ANY)],
        out_specs=[pl.BlockSpec(memory_space=pltpu.VMEM)] * 2,
        out_shape=[
            jax.ShapeDtypeStruct((KW * stem_c + STEM_ROWS, enc_c), BF16),
            jax.ShapeDtypeStruct((KW * stem_c + STEM_ROWS, 2 * enc_c), BF16),
        ],
        scratch_shapes=[pltpu.SemaphoreType.DMA((3 * KW,))],
        compiler_params=pltpu.CompilerParams(vmem_limit_bytes=5 * MIB),
        name="picks",
    )(place, stem_rows, enc_w)
    enc_oth = lax.ppermute(enc_send, "chan", cores)
    mine_far = lax.ppermute(mine, "chan", across)
    dec_send = pl.pallas_call(
        pick_kernel,
        grid_spec=pltpu.PrefetchScalarGridSpec(
            num_scalar_prefetch=1,
            grid=(2,),
            in_specs=[pl.BlockSpec(picked, lambda h, at: (0, 2 * h + 1 - at[2], 0, 0))],
            out_specs=pl.BlockSpec(picked, lambda h, at: (0, h, 0, 0)),
        ),
        out_shape=jax.ShapeDtypeStruct((KW, 2, stem_c, enc_c), BF16),
        compiler_params=pltpu.CompilerParams(vmem_limit_bytes=8 * MIB),
        name="dec_pick",
    )(place, dec_w)
    dec_came = lax.ppermute(dec_send, "chan", cores)

    acc, stem, lhs, split = call(
        functools.partial(stem_kernel, pairs=pairs, devices=devices),
        [place, own, first, second, stem_w, enc_oth, enc_w],
        [
            ((2 * rows, 2 * enc_c), F32),
            ((2, rows, stem_c), BF16),
            ((6, rows, stem_c), BF16),
            ((3, 2, pairs), jnp.int32),
        ],
        [
            ((pairs + 2 * OUTER, stem_c), F32),
            ((pairs + 2 * OUTER, stem_c), F32),
            ((6, rows, stem_c), BF16),
        ],
        limit=14,
        name="stem_conv",
        last=(5,),
    )
    keep, send = call(
        enc_kernel,
        [place, acc, lhs, enc_oth],
        [((2 * rows, enc_c), F32), ((2 * rows, enc_c), BF16)],
        limit=12,
        name="enc_conv",
    )
    came = lax.ppermute(gated(send, mine_far), "chan", across)

    targets_in, place_in = gated((targets, place), send)
    blocks = {0: split[0], 1: split[2], devices - 1: split[1]}
    for r in range(2, devices - 1):
        blocks[r] = ring(split[0], r)
    comb_own, comb_came = pl.pallas_call(
        comb_kernel,
        grid_spec=pltpu.PrefetchScalarGridSpec(
            num_scalar_prefetch=1,
            grid=(2,),
            in_specs=[
                pl.BlockSpec(picked, lambda h, at: (0, 2 * h + at[2], 0, 0)),
                pl.BlockSpec(picked, lambda h, at: (0, h, 0, 0)),
            ],
            out_specs=[pl.BlockSpec((3, 2, 1, stem_c, enc_c), lambda h, at: (0, 0, h, 0, 0))] * 2,
        ),
        out_shape=[jax.ShapeDtypeStruct((3, 2, 2, stem_c, enc_c), BF16)] * 2,
        compiler_params=pltpu.CompilerParams(vmem_limit_bytes=12 * MIB),
        name="dec_taps",
    )(place_in, dec_w, dec_came)
    targets_in = targets_in.T
    count, edge = 2 * pairs, 2 * SIDE
    (targets_at,) = call(
        targets_kernel,
        [place, targets_in, ring(targets_in[:, count - edge :], 1), ring(targets_in[:, :edge], devices - 1)],
        [((2, rows, 2 * stem_c), BF16)],
        [((count + 2 * edge, 128), F32)],
        limit=6,
        name="targets",
    )
    blank = jnp.zeros_like(stem)
    stem_at = jnp.where(
        first_chip, jnp.concatenate([stem, blank], axis=2), jnp.concatenate([blank, stem], axis=2)
    )
    place_in = gated(place, (comb_own, comb_came, targets_at, stem_at, list(blocks.values())))

    pooled, centre = call(
        functools.partial(pool_kernel, pairs=pairs, total=total),
        [place_in, keep, came],
        [((rows, enc_c), BF16), ((pairs, enc_c), BF16)],
        limit=8,
        name="gelu_pool",
    )
    pooled_oth = lax.ppermute(pooled, "chan", cores)
    part, send = call(
        functools.partial(dec_kernel, pairs=pairs),
        [
            pooled,
            pooled_oth,
            comb_own.reshape(3, 4 * stem_c, enc_c),
            comb_came.reshape(3, 4 * stem_c, enc_c),
            stem_at,
            targets_at,
        ],
        [((rows, 4 * stem_c), F32), ((rows, 4 * stem_c), BF16)],
        [((rows + 16, enc_c), F32)],
        limit=11,
        name="dec_conv",
    )
    came = lax.ppermute(send, "chan", across)

    centre, place_in = gated((centre, place), send)
    beyond, beside = swap(centre, 2), swap(centre, 1)
    (taps,) = call(
        functools.partial(taps_kernel, pairs=pairs, devices=devices),
        [place_in] + [blocks[r] for r in range(devices)] + [stem_w],
        [((KW * stem_c, 2 * pairs * devices), BF16)],
        limit=12,
        name="stem_taps",
    )

    weights = [mine, mine_far]
    weights += [lax.ppermute(w, "chan", cores) for w in gated(weights, keep)]

    def owner_slope(slot, at):
        (out,) = call(
            functools.partial(owner_slope_kernel, slot=slot, pairs=pairs, devices=devices),
            [at] + [blocks[r] for r in range(devices)] + weights,
            [((2 * pairs, enc_c), BF16)],
            [
                ((devices, 2, pairs), jnp.int32),
                ((rows, stem_c), F32),
                ((rows, stem_c), F32),
                ((6, pairs, stem_c), BF16),
            ],
            limit=10,
            name="owner_slope",
        )
        return out, lax.ppermute(out, "chan", cores)

    slope0, slope0_came = owner_slope(0, gated(place, taps))

    pred, sums, local, near, far = call(
        functools.partial(slope_kernel, pairs=pairs, total=total, scale=1.0 / math.sqrt(2 * total)),
        [gated(place, (beyond, beside, slope0)), part, came, targets_at],
        [((2, pairs, stem_c), BF16), ((2, 2, rows, stem_c), BF16)] + [((2, rows, stem_c), BF16)] * 3,
        [((rows + 8, 2 * stem_c), F32)],
        limit=7,
        name="out_slope",
    )
    sums_oth = lax.ppermute(sums, "chan", cores)
    (pre,) = call(
        functools.partial(back_kernel, pairs=pairs),
        [place, sums, sums_oth, dec_w],
        [((pairs, enc_c), BF16)],
        [((2, rows, stem_c), F32)],
        limit=11,
        name="up_grad",
    )

    def link(steps):
        out = []
        for s in range(devices):
            for step in steps:
                t = (s + step) % devices
                for x in range(2):
                    out.append((s * 4 + 2 * x + t % 2, t * 4 + 2 * x + (t + step) % 2))
        return out

    def to_owner(local, near, far):
        near = lax.ppermute(near, ("seq", "chan"), link((1, 2)))
        far = lax.ppermute(far, ("seq", "chan"), link((3,)))
        return local, near, far

    def slots(local, near, far):
        return jnp.stack([jnp.where(even, local, near), jnp.where(even, near, far)])

    local, near, far = to_owner(local, near, far)
    pre_oth = lax.ppermute(pre, "chan", across)
    slope1, slope1_came = owner_slope(1, gated(place, pre))
    near, far = gated((near, far), slope1)
    far_pooled = swap(beyond, 1)
    sums_pieces = local, near, far
    pre_oth = gated(pre_oth, (near, far, slope1))
    pieces = [jnp.where(own_block, pre, pre_oth) for own_block in target]
    local, near, far = to_owner(*pieces)
    sums_mine = gated(slots(*sums_pieces), pieces)
    sums_came = lax.ppermute(sums_mine, "chan", cores)

    (pred,) = call(
        pred_kernel,
        [pred],
        [((stem_c, 2 * pairs), BF16)],
        [((2 * pairs, 128), F32)],
        limit=5,
        name="pred",
    )
    pred = pred.T
    (g_dec,) = call(
        functools.partial(dec_grad_kernel, pairs=pairs),
        [place, sums_mine, sums_came, centre, beside, beyond, far_pooled],
        [((KW, stem_c, enc_c), F32)],
        [
            ((2, rows, stem_c), F32),
            ((KW, devices * pairs, stem_c), BF16),
            ((devices * pairs, enc_c), BF16),
        ],
        limit=12,
        name="dec_grad",
    )
    near, far = gated((near, far), (g_dec, pred))
    pre_mine = slots(local, near, far)
    pre_came = lax.ppermute(pre_mine, "chan", cores)
    g_enc = pl.pallas_call(
        enc_grad_kernel,
        grid=(2,),
        in_specs=[SCALARS, pl.BlockSpec((KW * stem_c // 2, 2 * pairs * devices), lambda k: (k, 0))]
        + [whole(pre_mine.shape)] * 2
        + [whole(slope0.shape)] * 4,
        out_specs=pl.BlockSpec((KW * stem_c // 2, enc_c), lambda k: (k, 0)),
        out_shape=jax.ShapeDtypeStruct((KW * stem_c, enc_c), F32),
        scratch_shapes=[pltpu.VMEM((2 * pairs * devices, enc_c), BF16)],
        compiler_params=pltpu.CompilerParams(vmem_limit_bytes=13 * MIB),
        name="enc_grad",
    )(place, taps, pre_mine, pre_came, slope0, slope1, slope0_came, slope1_came)
    g_enc = g_enc.reshape(KW, stem_c, enc_c).transpose(2, 0, 1)
    return (pred, g_enc, g_dec.transpose(1, 0, 2))


def extended(block, sides, width):
    for axis, dim in sides:
        count = lax.axis_size(axis)
        forward = [(i, i + 1) for i in range(count - 1)]
        backward = [(target, source) for source, target in forward]
        low = lax.ppermute(
            lax.slice_in_dim(block, block.shape[dim] - width, None, axis=dim), axis, forward
        )
        high = lax.ppermute(lax.slice_in_dim(block, 0, width, axis=dim), axis, backward)
        block = jnp.concatenate([low, block, high], axis=dim)
    return block


def rim_cells(block, margin):
    return extended(block, (("seq", 0),), margin)


def channel_sum(partial_value):
    return lax.psum_scatter(partial_value, "chan", scatter_dimension=1, tiled=True)


def channel_gather(block):
    return lax.all_gather(block, "chan", axis=1, tiled=True)


def conv_rows(padded, weight):
    row_count = padded.shape[0] - 4
    total = jnp.zeros((row_count, weight.shape[0]), jnp.float32)
    for k in range(KW):
        total = total + lax.dot_general(
            padded[k : k + row_count],
            weight[:, k, :],
            (((1,), (1,)), ((), ())),
            preferred_element_type=jnp.float32,
        )
    return total


def grad_taps(picked, padded):
    row_count = picked.shape[0]
    pieces = [
        lax.dot_general(
            picked,
            padded[k : k + row_count],
            (((0,), (0,)), ((), ())),
            preferred_element_type=jnp.float32,
        )
        for k in range(KW)
    ]
    return jnp.stack(pieces, axis=1)


def weight_grad(cotangent, padded):
    rounded = grad_taps(cotangent, padded).astype(jnp.bfloat16)
    return lax.psum_scatter(
        lax.optimization_barrier(rounded).astype(jnp.float32),
        "seq",
        scatter_dimension=0,
        tiled=True,
    )


def general_shards(dna_bases, w_stem, w_enc, w_dec, targets):
    row_count = dna_bases.shape[0]
    devices = lax.axis_size("seq")
    length = row_count * devices
    onehot = (dna_bases[:, None] == jnp.arange(4, dtype=jnp.int32)[None, :]).astype(jnp.bfloat16)
    onehot_pad = rim_cells(onehot, 2)
    stem_out = gelu_value(conv_rows(onehot_pad, w_stem)).astype(jnp.bfloat16)
    stem_pad = rim_cells(stem_out, 2)
    enc_pre = channel_sum(conv_rows(stem_pad, w_enc))
    active = gelu_value(enc_pre).astype(jnp.bfloat16).astype(jnp.float32)
    pooled = (0.5 * active.reshape(row_count // 2, 2, -1).sum(axis=1)).astype(jnp.bfloat16)
    pooled_pad = rim_cells(pooled, 1)
    up_pad = jnp.repeat(pooled_pad, 2, axis=0)
    output = channel_sum(conv_rows(up_pad, w_dec)) + stem_out.astype(jnp.float32)
    pred = output.astype(jnp.bfloat16)
    scale = 1.0 / math.sqrt(length)
    slope_out = ((output - targets.astype(jnp.float32)) * scale).astype(jnp.bfloat16)
    slope_all = channel_gather(slope_out)
    g_dec = weight_grad(slope_all, up_pad)
    slope_pad = rim_cells(slope_all, 2)
    up_grad = jnp.zeros((row_count, w_dec.shape[2]), jnp.float32)
    for k in range(KW):
        up_grad = up_grad + jnp.dot(
            slope_pad[4 - k : 4 - k + row_count], w_dec[:, k, :], preferred_element_type=jnp.float32
        )
    pool_grad = up_grad.reshape(row_count // 2, 2, -1).sum(axis=1)
    act_grad = 0.5 * jnp.repeat(pool_grad, 2, axis=0)
    pre_grad = (act_grad * gelu_slope(enc_pre)).astype(jnp.bfloat16)
    pre_all = channel_gather(pre_grad)
    g_enc = weight_grad(pre_all, stem_pad)
    return (pred, g_enc, g_dec)


def solution(mesh):
    sizes = mesh.shape["seq"], mesh.shape["chan"]
    return jax.shard_map(
        shards if sizes == (4, 4) else general_shards,
        mesh=mesh,
        in_specs=(
            P(("groups", "seq")),
            P("chan", None, None),
            P(None, None, "chan"),
            P(None, None, "chan"),
            P(("groups", "seq"), "chan"),
        ),
        out_specs=(
            P(("groups", "seq"), "chan"),
            P(("groups", "seq"), None, "chan"),
            P(("groups", "seq"), None, "chan"),
        ),
        check_vma=False,
    )
```

```python
import functools
import math

import jax
import jax.numpy as jnp
from jax import lax
from jax.experimental import pallas as pl
from jax.experimental.pallas import tpu as pltpu
from jax.sharding import PartitionSpec as P

KW = 5

SQRT_TWO_PI = 0.7978845608028654
CUBIC = 0.044715

STEM_ROWS = 32
FIRST = 3
SIDE = 64
OUTER = 16
INNER = 8
F32 = jnp.float32
BF16 = jnp.bfloat16
MIB = 1024 * 1024


def gelu_value(value):
    inner = jnp.tanh(SQRT_TWO_PI * (value + CUBIC * value * value * value))
    return 0.5 * value * (1.0 + inner)


def gelu_slope(value):
    inner = jnp.tanh(SQRT_TWO_PI * (value + CUBIC * value * value * value))
    return 0.5 * (1.0 + inner) + 0.5 * value * (1.0 - inner * inner) * SQRT_TWO_PI * (
        1.0 + 3.0 * CUBIC * value * value
    )


def dot(a, b, contract):
    return lax.dot_general(a, b, (contract, ((), ())), preferred_element_type=F32)


def assemble(own, after, before, block, devices):
    side = 2 * SIDE
    pairs = own.shape[1]
    column = lax.broadcasted_iota(jnp.int32, (2, side), 1)
    after = jnp.where(block == devices - 1, -1, after[:, :side])
    before = jnp.where(block == 0, -1, before[:, pairs - side :])
    return jnp.concatenate([own, jnp.where(column < SIDE, after, before)], axis=1)


def split_parity(bases):
    count = bases.shape[1]
    row = lax.broadcasted_iota(jnp.int32, (count, count), 0)
    column = lax.broadcasted_iota(jnp.int32, (count, count), 1)
    source = jnp.where(column < count // 2, 2 * column, 2 * column - count + 1)
    chosen = jnp.where(row == source, 1.0, 0.0).astype(BF16)
    wide = jnp.broadcast_to(bases, (16, count)).astype(F32).astype(BF16)
    value = dot(wide, chosen, ((1,), (0,))).astype(jnp.int32)
    return jnp.concatenate([value[0:1, : count // 2], value[0:1, count // 2 :]], axis=0)


def tap_onehots(bases, start, width):
    total = bases.shape[1]
    before = pltpu.roll(bases, (1 - start) % total, 1)[:, :width]
    here = bases[:, :width] if start == 0 else pltpu.roll(bases, -start % total, 1)[:, :width]
    after = pltpu.roll(bases, (-1 - start) % total, 1)[:, :width]
    taps = [before[0:1], before[1:2], here[0:1], here[1:2], after[0:1], after[1:2]]
    row = lax.broadcasted_iota(jnp.int32, (4 * KW, width), 0)
    tap, base = row >> 2, row & 3
    out = []
    for first in (0, 1):
        value = jnp.full((4 * KW, width), -1, jnp.int32)
        for k in range(KW):
            value = jnp.where(tap == k, jnp.broadcast_to(taps[first + k], value.shape), value)
        out.append(jnp.where(value == base, 1.0, 0.0).astype(BF16))
    return out


def valid_pairs(shape, dim, first, total):
    pair = lax.broadcasted_iota(jnp.int32, shape, dim) + first
    return (pair >= 0) & (pair < total)


def stem_kernel(
    place, own, after, before, stem_own, w_oth, w_own, acc, stem_out, lhs_oth, split, even, odd, lhs, *, pairs, devices
):
    seq, hi, lo = place[0], place[1], place[2]
    rows = pairs + 2 * INNER
    wide = pairs + 2 * OUTER
    block = acc.shape[1] // 2
    swapped = lax.rem(seq, 2) == 1
    first, second = after[...], before[...]
    for i, raw in enumerate((own[...], jnp.where(swapped, second, first), jnp.where(swapped, first, second))):
        split[i] = split_parity(raw)
    hots = tap_onehots(assemble(split[0], split[1], split[2], seq, devices), -OUTER, wide)
    gap = OUTER - INNER
    stem_oth = w_oth[: stem_own.shape[0], : stem_own.shape[1]]
    for weight, held_lhs in ((stem_own[...], lhs), (stem_oth, lhs_oth)):
        for hot, held in zip(hots, (even, odd)):
            raw = dot(hot, weight, ((0,), (0,)))
            ok = valid_pairs(raw.shape, 0, seq * pairs - OUTER, pairs * devices)
            held[...] = jnp.where(ok, gelu_value(raw), 0.0).astype(BF16).astype(F32)
        for k in range(6):
            source = even if k % 2 == 0 else odd
            held_lhs[k] = source[gap + k // 2 - 1 : gap + k // 2 - 1 + rows, :].astype(BF16)
    stem_out[0] = lhs[2]
    stem_out[1] = lhs[3]
    for part in range(2):
        at = pl.multiple_of((2 * (hi if part == 0 else 1 - hi) + lo) * block, 128)
        total = jnp.zeros((2 * rows, block), F32)
        for k in range(KW):
            total = total + dot(lhs[k : k + 2].reshape(2 * rows, -1), w_own[k, :, pl.ds(at, block)], ((1,), (0,)))
        acc[:, part * block : (part + 1) * block] = total


def enc_kernel(place, acc, lhs, w_oth, keep, send):
    hi = place[1]
    rows, block = keep.shape
    for part in range(2):
        at = pl.multiple_of((hi if part == 0 else 1 - hi) * block, 128)
        total = acc[:, part * block : (part + 1) * block]
        for k in range(KW):
            total = total + dot(lhs[k : k + 2].reshape(rows, -1), w_oth[k * lhs.shape[2] : (k + 1) * lhs.shape[2], pl.ds(at, block)], ((1,), (0,)))
        if part == 0:
            keep[...] = total
        else:
            send[...] = total.astype(BF16)


def pool_kernel(place, keep, came, pooled, centre, *, pairs, total):
    rows = pairs + 2 * INNER
    value = keep[...] + came[...].astype(F32)
    active = gelu_value(value).astype(BF16).astype(F32)
    both = 0.5 * (active[:rows] + active[rows:])
    ok = valid_pairs(both.shape, 0, place[0] * pairs - INNER, total)
    both = jnp.where(ok, both, 0.0).astype(BF16)
    pooled[...] = both
    centre[...] = both[INNER : INNER + pairs].astype(BF16)


def dec_kernel(own, oth, w_own, w_oth, stem, targets, part, send, held, *, pairs):
    rows = pairs + 2 * INNER
    held[:8] = jnp.zeros((8, held.shape[1]), F32)
    held[8 + rows :] = jnp.zeros((8, held.shape[1]), F32)
    acc = jnp.zeros(part.shape, F32)
    for source, weight in ((own, w_own), (oth, w_oth)):
        held[8 : 8 + rows] = source[...].astype(F32)
        for k in range(3):
            acc = acc + dot(held[7 + k : 7 + k + rows].astype(BF16), weight[k], ((1,), (1,)))
    half = part.shape[1] // 2
    for parity in range(2):
        value = acc[:, parity * half : (parity + 1) * half]
        value = value + stem[parity].astype(F32) - targets[parity].astype(F32)
        part[:, parity * half : (parity + 1) * half] = value
        send[:, parity * half : (parity + 1) * half] = value.astype(BF16)


def slope_kernel(place, part, came, targets, pred, sums, local, near, far, held, *, pairs, total, scale):
    rows = pairs + 2 * INNER
    half = part.shape[1] // 2
    quarter = half // 2
    ok = valid_pairs((rows, half), 0, place[0] * pairs - INNER, total)
    second = place[1] == 1
    slopes = []
    for parity in range(2):
        cols = slice(parity * half, (parity + 1) * half)
        value = part[:, cols] + came[:, cols].astype(F32)
        out = (value + targets[parity].astype(F32))[INNER : INNER + pairs]
        pred[parity] = jnp.where(second, out[:, quarter:], out[:, :quarter]).astype(BF16)
        slopes.append(jnp.where(ok, value * scale, 0.0).astype(BF16).astype(F32))
    held[:rows] = slopes[0]
    held[rows:] = jnp.zeros((8, half), F32)
    both = slopes[0] + slopes[1], slopes[1] + held[1 : 1 + rows]
    for i in range(2):
        for h in range(2):
            sums[h, i] = both[i][:, h * quarter : (h + 1) * quarter].astype(BF16)
    for out, step in ((local, 0), (near, 2 - place[3]), (far, 3)):
        out[...] = sums[lax.rem(place[0] + step, 4) // 2]


def lane_tiles(channels):
    return [(first, min(first + 128, channels)) for first in range(0, channels, 128)]


def targets_kernel(place, own, before, after, out, held):
    channels, count = own.shape
    side = before.shape[1]
    rows = count // 2 + 2 * INNER
    high = place[1] == 1
    for first, last in lane_tiles(channels):
        wide = last - first
        held[:side, :wide] = before[first:last].astype(F32).T
        held[side : side + count, :wide] = own[first:last].astype(F32).T
        held[side + count :, :wide] = after[first:last].astype(F32).T
        for parity in range(2):
            value = held[pl.ds(side - 2 * INNER + parity, rows, stride=2), :][:, :wide].astype(BF16)
            blank = jnp.zeros_like(value)
            out[parity, :, first:last] = jnp.where(high, blank, value)
            out[parity, :, channels + first : channels + last] = jnp.where(high, value, blank)


def pred_kernel(source, out, held):
    channels, count = out.shape
    for first, last in lane_tiles(channels):
        wide = last - first
        for parity in range(2):
            value = source[parity, :, first:last].astype(F32)
            if wide < 128:
                value = jnp.concatenate([value, jnp.zeros((count // 2, 128 - wide), F32)], axis=1)
            held[pl.ds(parity, count // 2, stride=2), :] = value
        out[first:last] = held[:, :wide].T.astype(BF16)


def shifted_sums(held, pairs):
    return [
        held[0, INNER + 1 : INNER + 1 + pairs].astype(BF16),
        held[1, INNER : INNER + pairs].astype(BF16),
        held[0, INNER : INNER + pairs].astype(BF16),
        held[1, INNER - 1 : INNER - 1 + pairs].astype(BF16),
        held[0, INNER - 1 : INNER - 1 + pairs].astype(BF16),
    ]


def back_kernel(place, own, oth, weight, out, held, *, pairs):
    acc = jnp.zeros(out.shape, F32)
    for source, core in ((own, place[2]), (oth, 1 - place[2])):
        for h in range(2):
            held[...] = source[h].astype(F32)
            for k, tap in enumerate(shifted_sums(held, pairs)):
                acc = acc + dot(tap, weight[k, 2 * h + core], ((1,), (0,)))
    out[...] = (0.5 * acc).astype(BF16)


def owner_slope_kernel(place, *refs, slot, pairs, devices):
    blocks, weights = refs[:devices], refs[devices : devices + 6]
    out, bases, even, odd, lhs = refs[devices + 6 :]
    for r in range(devices):
        bases[r] = blocks[r][...]
    wide = pairs + 2 * INNER
    step = 2 * slot + place[3]
    block = lax.rem(place[0] - step + devices, devices)
    before, after = lax.rem(step + 1, devices), lax.rem(step + devices - 1, devices)
    joined = assemble(bases[step], bases[after], bases[before], block, devices)
    hots = tap_onehots(joined, -INNER, wide)
    total = jnp.zeros(out.shape, F32)
    channels = lhs.shape[2]
    for some, others in ((0, None), (1, None), (2, 3), (4, 5)):
        count = KW if others is None else FIRST
        weight = weights[some][count * channels : count * channels + 4 * KW, :channels]
        for hot, held in zip(hots, (even, odd)):
            raw = dot(hot, weight, ((0,), (0,)))
            ok = valid_pairs(raw.shape, 0, block * pairs - INNER, pairs * devices)
            held[...] = jnp.where(ok, gelu_value(raw), 0.0).astype(BF16).astype(F32)
        for k in range(6):
            source = even if k % 2 == 0 else odd
            lhs[k] = source[INNER + k // 2 - 1 : INNER + k // 2 - 1 + pairs, :].astype(BF16)
        for k in range(KW):
            at, step = (some, k) if k < count else (others, k - count)
            tap = weights[at][step * channels : (step + 1) * channels, :]
            total = total + dot(lhs[k : k + 2].reshape(2 * pairs, -1), tap, ((1,), (0,)))
    out[...] = gelu_slope(total).astype(BF16)


def taps_kernel(place, *refs, pairs, devices):
    blocks, (stem_w, out) = refs[:devices], refs[devices:]
    channels = stem_w.shape[1]
    for r in range(devices):
        block = lax.rem(place[0] - r + devices, devices)
        bases = assemble(blocks[r][...], blocks[r - 1][...], blocks[(r + 1) % devices][...], block, devices)
        width = bases.shape[1]
        parts = []
        for hot in tap_onehots(bases, 0, width):
            raw = dot(stem_w[...], hot, ((0,), (0,)))
            column = lax.broadcasted_iota(jnp.int32, raw.shape, 1)
            pair = jnp.where(column >= width - SIDE, column - width, column) + block * pairs
            ok = (pair >= 0) & (pair < pairs * devices)
            parts.append(jnp.where(ok, gelu_value(raw), 0.0))
        taps = []
        for step in (-1, 0, 1):
            for held in parts:
                moved = held if step == 0 else pltpu.roll(held, -step % width, 1)
                taps.append(moved[:, :pairs].astype(BF16))
        at = 2 * r * pairs
        for k in range(KW):
            out[k * channels : (k + 1) * channels, at : at + pairs] = taps[k]
            out[k * channels : (k + 1) * channels, at + pairs : at + 2 * pairs] = taps[k + 1]


def picks_kernel(place, stem, enc, mine, mine0, mine1, enc_oth, sems):
    seq, core = place[0], 1 - place[2]
    taps, channels, _ = enc.shape
    block = mine0.shape[1]

    def columns(index):
        return pl.ds(pl.multiple_of(index * block, 128), block)

    copies = []
    for k in range(taps):
        rows = pl.ds(k * channels, channels)
        for h in range(2):
            copies.append((enc.at[k, :, columns(2 * h + core)], enc_oth.at[rows, h * block : (h + 1) * block]))
        copies.append((enc.at[k, :, columns(seq)], mine.at[rows]))
        if k < FIRST:
            copies.append((enc.at[k, :, columns(seq)], mine0.at[rows]))
        else:
            copies.append((enc.at[k, :, columns(seq)], mine1.at[pl.ds((k - FIRST) * channels, channels)]))
    copies = [pltpu.make_async_copy(*ends, sems.at[i]) for i, ends in enumerate(copies)]
    for copy in copies:
        copy.start()
    enc_oth[taps * channels :, : stem.shape[1]] = stem[...]
    mine0[FIRST * channels :, : stem.shape[1]] = stem[...]
    mine[taps * channels :, : stem.shape[1]] = stem[...]
    for copy in copies:
        copy.wait()


def pick_kernel(place, source, out):
    out[...] = source[...]


def comb_kernel(place, own, came, comb_own, comb_came):
    combine(own, comb_own)
    combine(came, comb_came)


def combine(weight, comb):
    comb[0, 0] = weight[0] + weight[1]
    comb[1, 0] = weight[2] + weight[3]
    comb[2, 0] = weight[4]
    comb[0, 1] = weight[0]
    comb[1, 1] = weight[1] + weight[2]
    comb[2, 1] = weight[3] + weight[4]


def dec_grad_kernel(place, own, came, pool0, pool1, pool2, pool3, out, held, taps, pooled, *, pairs):
    blocks = (pool0, pool1, pool2, pool3)
    parity = place[3]
    odd = lax.rem(place[0], 2)
    for block, step in zip(blocks, (0, 3 - 2 * odd, 2, 1 + 2 * odd)):
        pooled[pl.ds(pl.multiple_of(step * pairs, pairs), pairs), :] = block[...]
    for i in range(4):
        slots = own if i < 2 else came
        held[...] = slots[i % 2].astype(F32)
        step = 2 * (i % 2) + (parity if i < 2 else 1 - parity)
        at = pl.ds(pl.multiple_of(step * pairs, pairs), pairs)
        for k, tap in enumerate(shifted_sums(held, pairs)):
            taps[k, at, :] = tap
    for k in range(KW):
        out[k] = dot(taps[k], pooled[...], ((0,), (0,)))


def enc_grad_kernel(place, taps, own, came, slope0, slope1, slope2, slope3, out, joined):
    @pl.when(pl.program_id(0) == 0)
    def _():
        pairs = own.shape[1]
        for i, slope in enumerate((slope0, slope1, slope2, slope3)):
            step = 2 * (i % 2) + (place[3] if i < 2 else 1 - place[3])
            grad = (own if i < 2 else came)[i % 2].astype(F32)
            for parity in range(2):
                value = grad * slope[parity * pairs : (parity + 1) * pairs].astype(F32)
                at = pl.multiple_of((2 * step + parity) * pairs, pairs)
                joined[pl.ds(at, pairs), :] = value.astype(BF16)

    out[...] = dot(taps[...], joined[...], ((1,), (0,)))


def whole(shape):
    return pl.BlockSpec(shape, lambda *_: (0,) * len(shape))


SCALARS = pl.BlockSpec(memory_space=pltpu.SMEM)


def call(kernel, ins, outs, scratch=(), limit=16, name=None, last=()):
    specs = [SCALARS if i.dtype == jnp.int32 and i.ndim == 1 else whole(i.shape) for i in ins]
    for at in last:
        shape = ins[at].shape
        specs[at] = pl.BlockSpec((STEM_ROWS,) + shape[1:], lambda *_: (shape[0] // STEM_ROWS - 1, 0))
    return pl.pallas_call(
        kernel,
        grid=(1,) if last else (),
        in_specs=specs,
        out_specs=[whole(s) for s, _ in outs],
        out_shape=[jax.ShapeDtypeStruct(s, d) for s, d in outs],
        scratch_shapes=[pltpu.VMEM(s, d) for s, d in scratch],
        compiler_params=pltpu.CompilerParams(vmem_limit_bytes=limit * MIB),
        name=name,
    )(*ins)


def gated(values, gates):
    return lax.optimization_barrier((values, gates))[0]


def shards(dna_bases, w_stem, w_enc, w_dec, targets):
    devices = lax.axis_size("seq")
    seq, chan = lax.axis_index("seq"), lax.axis_index("chan")
    hi, lo = chan // 2, chan % 2
    parity = (lo + seq) % 2
    pairs = dna_bases.shape[0] // 2
    total = pairs * devices
    rows = pairs + 2 * INNER
    stem_c = w_stem.shape[0]
    enc_c = w_dec.shape[2]
    across = [(c, c ^ 2) for c in range(4)]
    cores = [(c, c ^ 1) for c in range(4)]

    def ring(array, step):
        return lax.ppermute(array, "seq", [(i, (i + step) % devices) for i in range(devices)])

    def swap(array, distance):
        return lax.ppermute(array, "seq", [(i, i ^ distance) for i in range(devices)])

    place = jnp.stack([seq, hi, lo, parity]).astype(jnp.int32)
    first_chip, even = hi == 0, parity == 0
    target = [(seq + step) % devices // 2 == hi for step in (0, 2 - parity, 3)]
    own = dna_bases.reshape(1, 2 * pairs)
    stem_w = w_stem.transpose(1, 2, 0).reshape(4 * KW, stem_c)
    own, place, first_chip, even, target = lax.optimization_barrier((own, place, first_chip, even, target))

    first = swap(own, 1)
    second = lax.ppermute(own, "seq", [(i, (i + 1 - 2 * (1 - i % 2)) % devices) for i in range(devices)])
    enc_w = w_enc.transpose(1, 2, 0)
    dec_w = w_dec.transpose(1, 0, 2).reshape(KW, 4, stem_c, enc_c)
    picked = (KW, 1, stem_c, enc_c)
    stem_rows = jnp.concatenate([stem_w, jnp.zeros((STEM_ROWS - 4 * KW, stem_c), BF16)])
    mine, mine0, mine1, enc_send = pl.pallas_call(
        picks_kernel,
        in_specs=[SCALARS, whole(stem_rows.shape), pl.BlockSpec(memory_space=pl.ANY)],
        out_specs=[pl.BlockSpec(memory_space=pltpu.VMEM)] * 4,
        out_shape=[
            jax.ShapeDtypeStruct((KW * stem_c + STEM_ROWS, enc_c), BF16),
            jax.ShapeDtypeStruct((FIRST * stem_c + STEM_ROWS, enc_c), BF16),
            jax.ShapeDtypeStruct(((KW - FIRST) * stem_c, enc_c), BF16),
            jax.ShapeDtypeStruct((KW * stem_c + STEM_ROWS, 2 * enc_c), BF16),
        ],
        scratch_shapes=[pltpu.SemaphoreType.DMA((4 * KW,))],
        compiler_params=pltpu.CompilerParams(vmem_limit_bytes=6 * MIB),
        name="picks",
    )(place, stem_rows, enc_w)
    enc_oth = lax.ppermute(enc_send, "chan", cores)
    mine0_far = lax.ppermute(mine0, "chan", across)
    dec_send = pl.pallas_call(
        pick_kernel,
        grid_spec=pltpu.PrefetchScalarGridSpec(
            num_scalar_prefetch=1,
            grid=(2,),
            in_specs=[pl.BlockSpec(picked, lambda h, at: (0, 2 * h + 1 - at[2], 0, 0))],
            out_specs=pl.BlockSpec(picked, lambda h, at: (0, h, 0, 0)),
        ),
        out_shape=jax.ShapeDtypeStruct((KW, 2, stem_c, enc_c), BF16),
        compiler_params=pltpu.CompilerParams(vmem_limit_bytes=8 * MIB),
        name="dec_pick",
    )(place, dec_w)
    dec_came = lax.ppermute(dec_send, "chan", cores)

    acc, stem, lhs, split = call(
        functools.partial(stem_kernel, pairs=pairs, devices=devices),
        [place, own, first, second, stem_w, enc_oth, enc_w],
        [
            ((2 * rows, 2 * enc_c), F32),
            ((2, rows, stem_c), BF16),
            ((6, rows, stem_c), BF16),
            ((3, 2, pairs), jnp.int32),
        ],
        [
            ((pairs + 2 * OUTER, stem_c), F32),
            ((pairs + 2 * OUTER, stem_c), F32),
            ((6, rows, stem_c), BF16),
        ],
        limit=14,
        name="stem_conv",
        last=(5,),
    )
    keep, send = call(
        enc_kernel,
        [place, acc, lhs, enc_oth],
        [((2 * rows, enc_c), F32), ((2 * rows, enc_c), BF16)],
        limit=12,
        name="enc_conv",
    )
    came = lax.ppermute(gated(send, mine0_far), "chan", across)

    targets_in, place_in = gated((targets, place), send)
    blocks = {0: split[0], 1: split[2], devices - 1: split[1]}
    for r in range(2, devices - 1):
        blocks[r] = ring(split[0], r)
    comb_own, comb_came = pl.pallas_call(
        comb_kernel,
        grid_spec=pltpu.PrefetchScalarGridSpec(
            num_scalar_prefetch=1,
            grid=(2,),
            in_specs=[
                pl.BlockSpec(picked, lambda h, at: (0, 2 * h + at[2], 0, 0)),
                pl.BlockSpec(picked, lambda h, at: (0, h, 0, 0)),
            ],
            out_specs=[pl.BlockSpec((3, 2, 1, stem_c, enc_c), lambda h, at: (0, 0, h, 0, 0))] * 2,
        ),
        out_shape=[jax.ShapeDtypeStruct((3, 2, 2, stem_c, enc_c), BF16)] * 2,
        compiler_params=pltpu.CompilerParams(vmem_limit_bytes=12 * MIB),
        name="dec_taps",
    )(place_in, dec_w, dec_came)
    targets_in = targets_in.T
    count, edge = 2 * pairs, 2 * SIDE
    below, above = ring(targets_in[:, count - edge :], 1), ring(targets_in[:, :edge], devices - 1)
    mine1_far = lax.ppermute(gated(mine1, below), "chan", across)
    (targets_at,) = call(
        targets_kernel,
        [place, targets_in, below, above],
        [((2, rows, 2 * stem_c), BF16)],
        [((count + 2 * edge, 128), F32)],
        limit=6,
        name="targets",
    )
    blank = jnp.zeros_like(stem)
    stem_at = jnp.where(
        first_chip, jnp.concatenate([stem, blank], axis=2), jnp.concatenate([blank, stem], axis=2)
    )
    place_in = gated(place, (comb_own, comb_came, targets_at, stem_at, list(blocks.values())))

    pooled, centre = call(
        functools.partial(pool_kernel, pairs=pairs, total=total),
        [place_in, keep, came],
        [((rows, enc_c), BF16), ((pairs, enc_c), BF16)],
        limit=8,
        name="gelu_pool",
    )
    pooled_oth = lax.ppermute(pooled, "chan", cores)
    part, send = call(
        functools.partial(dec_kernel, pairs=pairs),
        [
            pooled,
            pooled_oth,
            comb_own.reshape(3, 4 * stem_c, enc_c),
            comb_came.reshape(3, 4 * stem_c, enc_c),
            stem_at,
            targets_at,
        ],
        [((rows, 4 * stem_c), F32), ((rows, 4 * stem_c), BF16)],
        [((rows + 16, enc_c), F32)],
        limit=11,
        name="dec_conv",
    )
    came = lax.ppermute(gated(send, mine1_far), "chan", across)

    centre, place_in = gated((centre, place), send)
    beyond, beside = swap(centre, 2), swap(centre, 1)

    weights = [mine, lax.ppermute(gated(mine, keep), "chan", cores), mine0_far, mine1_far]
    weights += [lax.ppermute(w, "chan", cores) for w in weights[2:]]

    def owner_slope(slot, at):
        (out,) = call(
            functools.partial(owner_slope_kernel, slot=slot, pairs=pairs, devices=devices),
            [at] + [blocks[r] for r in range(devices)] + weights,
            [((2 * pairs, enc_c), BF16)],
            [
                ((devices, 2, pairs), jnp.int32),
                ((rows, stem_c), F32),
                ((rows, stem_c), F32),
                ((6, pairs, stem_c), BF16),
            ],
            limit=10,
            name="owner_slope",
        )
        return out, lax.ppermute(out, "chan", cores)

    slope0, slope0_came = owner_slope(0, gated(place, send))

    pred, sums, local, near, far = call(
        functools.partial(slope_kernel, pairs=pairs, total=total, scale=1.0 / math.sqrt(2 * total)),
        [gated(place, (beyond, beside, slope0)), part, came, targets_at],
        [((2, pairs, stem_c), BF16), ((2, 2, rows, stem_c), BF16)] + [((2, rows, stem_c), BF16)] * 3,
        [((rows + 8, 2 * stem_c), F32)],
        limit=7,
        name="out_slope",
    )
    sums_oth = lax.ppermute(sums, "chan", cores)
    (pre,) = call(
        functools.partial(back_kernel, pairs=pairs),
        [place, sums, sums_oth, dec_w],
        [((pairs, enc_c), BF16)],
        [((2, rows, stem_c), F32)],
        limit=11,
        name="up_grad",
    )

    def link(steps):
        out = []
        for s in range(devices):
            for step in steps:
                t = (s + step) % devices
                for x in range(2):
                    out.append((s * 4 + 2 * x + t % 2, t * 4 + 2 * x + (t + step) % 2))
        return out

    def to_owner(local, near, far):
        near = lax.ppermute(near, ("seq", "chan"), link((1, 2)))
        far = lax.ppermute(far, ("seq", "chan"), link((3,)))
        return local, near, far

    def slots(local, near, far):
        return jnp.stack([jnp.where(even, local, near), jnp.where(even, near, far)])

    local, near, far = to_owner(local, near, far)
    pre_oth = lax.ppermute(pre, "chan", across)
    slope1, slope1_came = owner_slope(1, gated(place, pre))
    (taps,) = call(
        functools.partial(taps_kernel, pairs=pairs, devices=devices),
        [gated(place, slope1)] + [blocks[r] for r in range(devices)] + [stem_w],
        [((KW * stem_c, 2 * pairs * devices), BF16)],
        limit=12,
        name="stem_taps",
    )
    near, far = gated((near, far), taps)
    far_pooled = swap(beyond, 1)
    sums_pieces = local, near, far
    pre_oth = gated(pre_oth, (near, far, slope1, taps))
    pieces = [jnp.where(own_block, pre, pre_oth) for own_block in target]
    local, near, far = to_owner(*pieces)
    sums_mine = gated(slots(*sums_pieces), pieces)
    sums_came = lax.ppermute(sums_mine, "chan", cores)

    (pred,) = call(
        pred_kernel,
        [pred],
        [((stem_c, 2 * pairs), BF16)],
        [((2 * pairs, 128), F32)],
        limit=5,
        name="pred",
    )
    pred = pred.T
    (g_dec,) = call(
        functools.partial(dec_grad_kernel, pairs=pairs),
        [place, sums_mine, sums_came, centre, beside, beyond, far_pooled],
        [((KW, stem_c, enc_c), F32)],
        [
            ((2, rows, stem_c), F32),
            ((KW, devices * pairs, stem_c), BF16),
            ((devices * pairs, enc_c), BF16),
        ],
        limit=12,
        name="dec_grad",
    )
    near, far = gated((near, far), (g_dec, pred))
    pre_mine = slots(local, near, far)
    pre_came = lax.ppermute(pre_mine, "chan", cores)
    g_enc = pl.pallas_call(
        enc_grad_kernel,
        grid=(2,),
        in_specs=[SCALARS, pl.BlockSpec((KW * stem_c // 2, 2 * pairs * devices), lambda k: (k, 0))]
        + [whole(pre_mine.shape)] * 2
        + [whole(slope0.shape)] * 4,
        out_specs=pl.BlockSpec((KW * stem_c // 2, enc_c), lambda k: (k, 0)),
        out_shape=jax.ShapeDtypeStruct((KW * stem_c, enc_c), F32),
        scratch_shapes=[pltpu.VMEM((2 * pairs * devices, enc_c), BF16)],
        compiler_params=pltpu.CompilerParams(vmem_limit_bytes=13 * MIB),
        name="enc_grad",
    )(place, taps, pre_mine, pre_came, slope0, slope1, slope0_came, slope1_came)
    g_enc = g_enc.reshape(KW, stem_c, enc_c).transpose(2, 0, 1)
    return (pred, g_enc, g_dec.transpose(1, 0, 2))


def extended(block, sides, width):
    for axis, dim in sides:
        count = lax.axis_size(axis)
        forward = [(i, i + 1) for i in range(count - 1)]
        backward = [(target, source) for source, target in forward]
        low = lax.ppermute(
            lax.slice_in_dim(block, block.shape[dim] - width, None, axis=dim), axis, forward
        )
        high = lax.ppermute(lax.slice_in_dim(block, 0, width, axis=dim), axis, backward)
        block = jnp.concatenate([low, block, high], axis=dim)
    return block


def rim_cells(block, margin):
    return extended(block, (("seq", 0),), margin)


def channel_sum(partial_value):
    return lax.psum_scatter(partial_value, "chan", scatter_dimension=1, tiled=True)


def channel_gather(block):
    return lax.all_gather(block, "chan", axis=1, tiled=True)


def conv_rows(padded, weight):
    row_count = padded.shape[0] - 4
    total = jnp.zeros((row_count, weight.shape[0]), jnp.float32)
    for k in range(KW):
        total = total + lax.dot_general(
            padded[k : k + row_count],
            weight[:, k, :],
            (((1,), (1,)), ((), ())),
            preferred_element_type=jnp.float32,
        )
    return total


def grad_taps(picked, padded):
    row_count = picked.shape[0]
    pieces = [
        lax.dot_general(
            picked,
            padded[k : k + row_count],
            (((0,), (0,)), ((), ())),
            preferred_element_type=jnp.float32,
        )
        for k in range(KW)
    ]
    return jnp.stack(pieces, axis=1)


def weight_grad(cotangent, padded):
    rounded = grad_taps(cotangent, padded).astype(jnp.bfloat16)
    return lax.psum_scatter(
        lax.optimization_barrier(rounded).astype(jnp.float32),
        "seq",
        scatter_dimension=0,
        tiled=True,
    )


def general_shards(dna_bases, w_stem, w_enc, w_dec, targets):
    row_count = dna_bases.shape[0]
    devices = lax.axis_size("seq")
    length = row_count * devices
    onehot = (dna_bases[:, None] == jnp.arange(4, dtype=jnp.int32)[None, :]).astype(jnp.bfloat16)
    onehot_pad = rim_cells(onehot, 2)
    stem_out = gelu_value(conv_rows(onehot_pad, w_stem)).astype(jnp.bfloat16)
    stem_pad = rim_cells(stem_out, 2)
    enc_pre = channel_sum(conv_rows(stem_pad, w_enc))
    active = gelu_value(enc_pre).astype(jnp.bfloat16).astype(jnp.float32)
    pooled = (0.5 * active.reshape(row_count // 2, 2, -1).sum(axis=1)).astype(jnp.bfloat16)
    pooled_pad = rim_cells(pooled, 1)
    up_pad = jnp.repeat(pooled_pad, 2, axis=0)
    output = channel_sum(conv_rows(up_pad, w_dec)) + stem_out.astype(jnp.float32)
    pred = output.astype(jnp.bfloat16)
    scale = 1.0 / math.sqrt(length)
    slope_out = ((output - targets.astype(jnp.float32)) * scale).astype(jnp.bfloat16)
    slope_all = channel_gather(slope_out)
    g_dec = weight_grad(slope_all, up_pad)
    slope_pad = rim_cells(slope_all, 2)
    up_grad = jnp.zeros((row_count, w_dec.shape[2]), jnp.float32)
    for k in range(KW):
        up_grad = up_grad + jnp.dot(
            slope_pad[4 - k : 4 - k + row_count], w_dec[:, k, :], preferred_element_type=jnp.float32
        )
    pool_grad = up_grad.reshape(row_count // 2, 2, -1).sum(axis=1)
    act_grad = 0.5 * jnp.repeat(pool_grad, 2, axis=0)
    pre_grad = (act_grad * gelu_slope(enc_pre)).astype(jnp.bfloat16)
    pre_all = channel_gather(pre_grad)
    g_enc = weight_grad(pre_all, stem_pad)
    return (pred, g_enc, g_dec)


def solution(mesh):
    sizes = mesh.shape["seq"], mesh.shape["chan"]
    return jax.shard_map(
        shards if sizes == (4, 4) else general_shards,
        mesh=mesh,
        in_specs=(
            P(("groups", "seq")),
            P("chan", None, None),
            P(None, None, "chan"),
            P(None, None, "chan"),
            P(("groups", "seq"), "chan"),
        ),
        out_specs=(
            P(("groups", "seq"), "chan"),
            P(("groups", "seq"), None, "chan"),
            P(("groups", "seq"), None, "chan"),
        ),
        check_vma=False,
    )
```

```python
import functools
import math

import jax
import jax.numpy as jnp
from jax import lax
from jax.experimental import pallas as pl
from jax.experimental.pallas import tpu as pltpu
from jax.sharding import PartitionSpec as P

KW = 5

SQRT_TWO_PI = 0.7978845608028654
CUBIC = 0.044715

STEM_ROWS = 32
FIRST = 3
SIDE = 64
OUTER = 16
INNER = 8
F32 = jnp.float32
BF16 = jnp.bfloat16
MIB = 1024 * 1024


def gelu_value(value):
    inner = jnp.tanh(SQRT_TWO_PI * (value + CUBIC * value * value * value))
    return 0.5 * value * (1.0 + inner)


def gelu_slope(value):
    inner = jnp.tanh(SQRT_TWO_PI * (value + CUBIC * value * value * value))
    return 0.5 * (1.0 + inner) + 0.5 * value * (1.0 - inner * inner) * SQRT_TWO_PI * (
        1.0 + 3.0 * CUBIC * value * value
    )


def dot(a, b, contract):
    return lax.dot_general(a, b, (contract, ((), ())), preferred_element_type=F32)


def assemble(own, after, before, block, devices):
    side = 2 * SIDE
    pairs = own.shape[1]
    column = lax.broadcasted_iota(jnp.int32, (2, side), 1)
    after = jnp.where(block == devices - 1, -1, after[:, :side])
    before = jnp.where(block == 0, -1, before[:, pairs - side :])
    return jnp.concatenate([own, jnp.where(column < SIDE, after, before)], axis=1)


def split_parity(blocks):
    count = blocks[0].shape[1]
    row = lax.broadcasted_iota(jnp.int32, (count, count), 0)
    column = lax.broadcasted_iota(jnp.int32, (count, count), 1)
    source = jnp.where(column < count // 2, 2 * column, 2 * column - count + 1)
    chosen = jnp.where(row == source, 1.0, 0.0).astype(BF16)
    place = lax.broadcasted_iota(jnp.int32, (16, count), 0)
    wide = jnp.broadcast_to(blocks[0], (16, count))
    for i, block in enumerate(blocks[1:]):
        wide = jnp.where(place == i + 1, jnp.broadcast_to(block, (16, count)), wide)
    value = dot(wide.astype(F32).astype(BF16), chosen, ((1,), (0,))).astype(jnp.int32)
    return [
        jnp.concatenate([value[i : i + 1, : count // 2], value[i : i + 1, count // 2 :]], axis=0)
        for i in range(len(blocks))
    ]


def tap_onehots(bases, start, width):
    total = bases.shape[1]
    before = pltpu.roll(bases, (1 - start) % total, 1)[:, :width]
    here = bases[:, :width] if start == 0 else pltpu.roll(bases, -start % total, 1)[:, :width]
    after = pltpu.roll(bases, (-1 - start) % total, 1)[:, :width]
    taps = [before[0:1], before[1:2], here[0:1], here[1:2], after[0:1], after[1:2]]
    row = lax.broadcasted_iota(jnp.int32, (4 * KW, width), 0)
    tap, base = row >> 2, row & 3
    out = []
    for first in (0, 1):
        value = jnp.full((4 * KW, width), -1, jnp.int32)
        for k in range(KW):
            value = jnp.where(tap == k, jnp.broadcast_to(taps[first + k], value.shape), value)
        out.append(jnp.where(value == base, 1.0, 0.0).astype(BF16))
    return out


def valid_pairs(shape, dim, first, total):
    pair = lax.broadcasted_iota(jnp.int32, shape, dim) + first
    return (pair >= 0) & (pair < total)


def stem_kernel(
    place, own, after, before, stem_own, w_oth, w_own, acc, stem_out, lhs, lhs_oth, split, even, odd, *, pairs, devices
):
    seq = place[0]
    rows = pairs + 2 * INNER
    wide = pairs + 2 * OUTER
    swapped = lax.rem(seq, 2) == 1
    first, second = after[...], before[...]
    parts = split_parity([own[...], jnp.where(swapped, second, first), jnp.where(swapped, first, second)])
    for i, part in enumerate(parts):
        split[i] = part
    hots = tap_onehots(assemble(*parts, seq, devices), -OUTER, wide)
    gap = OUTER - INNER
    stem_oth = w_oth[: stem_own.shape[0], : stem_own.shape[1]]
    for weight, held_lhs in ((stem_own[...], lhs), (stem_oth, lhs_oth)):
        for hot, held in zip(hots, (even, odd)):
            raw = dot(hot, weight, ((0,), (0,)))
            ok = valid_pairs(raw.shape, 0, seq * pairs - OUTER, pairs * devices)
            held[...] = jnp.where(ok, gelu_value(raw), 0.0).astype(BF16).astype(F32)
        for k in range(6):
            source = even if k % 2 == 0 else odd
            held_lhs[k] = source[gap + k // 2 - 1 : gap + k // 2 - 1 + rows, :].astype(BF16)
    stem_out[0] = lhs[2]
    stem_out[1] = lhs[3]
    acc[...] = own_sums(lhs, w_own, 2 * (1 - place[1]) + place[2], acc.shape)


def own_sums(lhs, weight, index, shape):
    at = pl.ds(pl.multiple_of(index * shape[1], 128), shape[1])
    total = jnp.zeros(shape, F32)
    for k in range(KW):
        total = total + dot(lhs[k : k + 2].reshape(shape[0], -1), weight[k, :, at], ((1,), (0,)))
    return total


def other_sums(lhs, weight, index, total):
    rows, block = total.shape
    channels = lhs.shape[2]
    at = pl.ds(pl.multiple_of(index * block, 128), block)
    for k in range(KW):
        tap = weight[k * channels : (k + 1) * channels, at]
        total = total + dot(lhs[k : k + 2].reshape(rows, -1), tap, ((1,), (0,)))
    return total


def send_kernel(place, acc, lhs, w_oth, send):
    send[...] = other_sums(lhs, w_oth, 1 - place[1], acc[...]).astype(BF16)


def keep_kernel(place, lhs, lhs_oth, w_own, w_oth, keep):
    total = own_sums(lhs, w_own, 2 * place[1] + place[2], keep.shape)
    keep[...] = other_sums(lhs_oth, w_oth, place[1], total)


def pool_kernel(place, keep, came, pooled, centre, *, pairs, total):
    rows = pairs + 2 * INNER
    value = keep[...] + came[...].astype(F32)
    active = gelu_value(value).astype(BF16).astype(F32)
    both = 0.5 * (active[:rows] + active[rows:])
    ok = valid_pairs(both.shape, 0, place[0] * pairs - INNER, total)
    both = jnp.where(ok, both, 0.0).astype(BF16)
    pooled[...] = both
    centre[...] = both[INNER : INNER + pairs].astype(BF16)


def dec_kernel(own, oth, w_own, w_oth, stem, targets, part, send, held, *, pairs):
    rows = pairs + 2 * INNER
    held[:8] = jnp.zeros((8, held.shape[1]), F32)
    held[8 + rows :] = jnp.zeros((8, held.shape[1]), F32)
    acc = jnp.zeros(part.shape, F32)
    for source, weight in ((own, w_own), (oth, w_oth)):
        held[8 : 8 + rows] = source[...].astype(F32)
        for k in range(3):
            acc = acc + dot(held[7 + k : 7 + k + rows].astype(BF16), weight[k], ((1,), (1,)))
    half = part.shape[1] // 2
    for parity in range(2):
        value = acc[:, parity * half : (parity + 1) * half]
        value = value + stem[parity].astype(F32) - targets[parity].astype(F32)
        part[:, parity * half : (parity + 1) * half] = value
        send[:, parity * half : (parity + 1) * half] = value.astype(BF16)


def slope_kernel(place, part, came, targets, pred, sums, local, near, far, held, *, pairs, total, scale):
    rows = pairs + 2 * INNER
    half = part.shape[1] // 2
    quarter = half // 2
    ok = valid_pairs((rows, half), 0, place[0] * pairs - INNER, total)
    second = place[1] == 1
    slopes = []
    for parity in range(2):
        cols = slice(parity * half, (parity + 1) * half)
        value = part[:, cols] + came[:, cols].astype(F32)
        out = (value + targets[parity].astype(F32))[INNER : INNER + pairs]
        pred[parity] = jnp.where(second, out[:, quarter:], out[:, :quarter]).astype(BF16)
        slopes.append(jnp.where(ok, value * scale, 0.0).astype(BF16).astype(F32))
    held[:rows] = slopes[0]
    held[rows:] = jnp.zeros((8, half), F32)
    both = slopes[0] + slopes[1], slopes[1] + held[1 : 1 + rows]
    for i in range(2):
        for h in range(2):
            sums[h, i] = both[i][:, h * quarter : (h + 1) * quarter].astype(BF16)
    for out, step in ((local, 0), (near, 2 - place[3]), (far, 3)):
        out[...] = sums[lax.rem(place[0] + step, 4) // 2]


def lane_tiles(channels):
    return [(first, min(first + 128, channels)) for first in range(0, channels, 128)]


def targets_kernel(place, own, before, after, out, held):
    channels, count = own.shape
    side = before.shape[1]
    rows = count // 2 + 2 * INNER
    high = place[1] == 1
    for first, last in lane_tiles(channels):
        wide = last - first
        held[:side, :wide] = before[first:last].astype(F32).T
        held[side : side + count, :wide] = own[first:last].astype(F32).T
        held[side + count :, :wide] = after[first:last].astype(F32).T
        for parity in range(2):
            value = held[pl.ds(side - 2 * INNER + parity, rows, stride=2), :][:, :wide].astype(BF16)
            blank = jnp.zeros_like(value)
            out[parity, :, first:last] = jnp.where(high, blank, value)
            out[parity, :, channels + first : channels + last] = jnp.where(high, value, blank)


def pred_kernel(source, out, held):
    channels, count = out.shape
    for first, last in lane_tiles(channels):
        wide = last - first
        for parity in range(2):
            value = source[parity, :, first:last].astype(F32)
            if wide < 128:
                value = jnp.concatenate([value, jnp.zeros((count // 2, 128 - wide), F32)], axis=1)
            held[pl.ds(parity, count // 2, stride=2), :] = value
        out[first:last] = held[:, :wide].T.astype(BF16)


def shifted_sums(held, pairs):
    return [
        held[0, INNER + 1 : INNER + 1 + pairs].astype(BF16),
        held[1, INNER : INNER + pairs].astype(BF16),
        held[0, INNER : INNER + pairs].astype(BF16),
        held[1, INNER - 1 : INNER - 1 + pairs].astype(BF16),
        held[0, INNER - 1 : INNER - 1 + pairs].astype(BF16),
    ]


def back_kernel(place, own, oth, weight, out, held, *, pairs):
    acc = jnp.zeros(out.shape, F32)
    for source, core in ((own, place[2]), (oth, 1 - place[2])):
        for h in range(2):
            held[...] = source[h].astype(F32)
            for k, tap in enumerate(shifted_sums(held, pairs)):
                acc = acc + dot(tap, weight[k, 2 * h + core], ((1,), (0,)))
    out[...] = (0.5 * acc).astype(BF16)


def owner_slope_kernel(place, *refs, slot, pairs, devices):
    blocks, weights = refs[:devices], refs[devices : devices + 6]
    out, bases, even, odd, lhs = refs[devices + 6 :]
    for r in range(devices):
        bases[r] = blocks[r][...]
    wide = pairs + 2 * INNER
    step = 2 * slot + place[3]
    block = lax.rem(place[0] - step + devices, devices)
    before, after = lax.rem(step + 1, devices), lax.rem(step + devices - 1, devices)
    joined = assemble(bases[step], bases[after], bases[before], block, devices)
    hots = tap_onehots(joined, -INNER, wide)
    total = jnp.zeros(out.shape, F32)
    channels = lhs.shape[2]
    for some, others in ((0, None), (1, None), (2, 3), (4, 5)):
        count = KW if others is None else FIRST
        weight = weights[some][count * channels : count * channels + 4 * KW, :channels]
        for hot, held in zip(hots, (even, odd)):
            raw = dot(hot, weight, ((0,), (0,)))
            ok = valid_pairs(raw.shape, 0, block * pairs - INNER, pairs * devices)
            held[...] = jnp.where(ok, gelu_value(raw), 0.0).astype(BF16).astype(F32)
        for k in range(6):
            source = even if k % 2 == 0 else odd
            lhs[k] = source[INNER + k // 2 - 1 : INNER + k // 2 - 1 + pairs, :].astype(BF16)
        for k in range(KW):
            at, step = (some, k) if k < count else (others, k - count)
            tap = weights[at][step * channels : (step + 1) * channels, :]
            total = total + dot(lhs[k : k + 2].reshape(2 * pairs, -1), tap, ((1,), (0,)))
    out[...] = gelu_slope(total).astype(BF16)


def taps_kernel(place, *refs, pairs, devices):
    blocks, (stem_w, out) = refs[:devices], refs[devices:]
    channels = stem_w.shape[1]
    for r in range(devices):
        block = lax.rem(place[0] - r + devices, devices)
        bases = assemble(blocks[r][...], blocks[r - 1][...], blocks[(r + 1) % devices][...], block, devices)
        width = bases.shape[1]
        parts = []
        for hot in tap_onehots(bases, 0, width):
            raw = dot(stem_w[...], hot, ((0,), (0,)))
            column = lax.broadcasted_iota(jnp.int32, raw.shape, 1)
            pair = jnp.where(column >= width - SIDE, column - width, column) + block * pairs
            ok = (pair >= 0) & (pair < pairs * devices)
            parts.append(jnp.where(ok, gelu_value(raw), 0.0))
        taps = []
        for step in (-1, 0, 1):
            for held in parts:
                moved = held if step == 0 else pltpu.roll(held, -step % width, 1)
                taps.append(moved[:, :pairs].astype(BF16))
        at = 2 * r * pairs
        for k in range(KW):
            out[k * channels : (k + 1) * channels, at : at + pairs] = taps[k]
            out[k * channels : (k + 1) * channels, at + pairs : at + 2 * pairs] = taps[k + 1]


def picks_kernel(place, stem, enc, mine, mine0, mine1, enc_oth, sems):
    seq, core = place[0], 1 - place[2]
    taps, channels, _ = enc.shape
    block = mine0.shape[1]

    def columns(index):
        return pl.ds(pl.multiple_of(index * block, 128), block)

    copies = []
    for k in range(taps):
        rows = pl.ds(k * channels, channels)
        for h in range(2):
            copies.append((enc.at[k, :, columns(2 * h + core)], enc_oth.at[rows, h * block : (h + 1) * block]))
        copies.append((enc.at[k, :, columns(seq)], mine.at[rows]))
        if k < FIRST:
            copies.append((enc.at[k, :, columns(seq)], mine0.at[rows]))
        else:
            copies.append((enc.at[k, :, columns(seq)], mine1.at[pl.ds((k - FIRST) * channels, channels)]))
    copies = [pltpu.make_async_copy(*ends, sems.at[i]) for i, ends in enumerate(copies)]
    for copy in copies:
        copy.start()
    enc_oth[taps * channels :, : stem.shape[1]] = stem[...]
    mine0[FIRST * channels :, : stem.shape[1]] = stem[...]
    mine[taps * channels :, : stem.shape[1]] = stem[...]
    for copy in copies:
        copy.wait()


def pick_kernel(place, source, out):
    out[...] = source[...]


def comb_kernel(place, own, came, comb_own, comb_came):
    combine(own, comb_own)
    combine(came, comb_came)


def combine(weight, comb):
    comb[0, 0] = weight[0] + weight[1]
    comb[1, 0] = weight[2] + weight[3]
    comb[2, 0] = weight[4]
    comb[0, 1] = weight[0]
    comb[1, 1] = weight[1] + weight[2]
    comb[2, 1] = weight[3] + weight[4]


def dec_grad_kernel(place, own, came, pool0, pool1, pool2, pool3, out, held, taps, pooled, *, pairs):
    blocks = (pool0, pool1, pool2, pool3)
    parity = place[3]
    odd = lax.rem(place[0], 2)
    for block, step in zip(blocks, (0, 3 - 2 * odd, 2, 1 + 2 * odd)):
        pooled[pl.ds(pl.multiple_of(step * pairs, pairs), pairs), :] = block[...]
    for i in range(4):
        slots = own if i < 2 else came
        held[...] = slots[i % 2].astype(F32)
        step = 2 * (i % 2) + (parity if i < 2 else 1 - parity)
        at = pl.ds(pl.multiple_of(step * pairs, pairs), pairs)
        for k, tap in enumerate(shifted_sums(held, pairs)):
            taps[k, at, :] = tap
    for k in range(KW):
        out[k] = dot(taps[k], pooled[...], ((0,), (0,)))


def enc_grad_kernel(place, taps, slots, slope0, slope1, *refs, first):
    prior, (out, joined) = refs[:-2], refs[-2:]
    pairs = slots.shape[1]
    size = 2 * pairs
    offset = place[3] if first else 1 - place[3]

    @pl.when(pl.program_id(0) == 0)
    def _():
        for i, slope in enumerate((slope0, slope1)):
            grad = slots[i].astype(F32)
            for parity in range(2):
                at = i * size + parity * pairs
                value = grad * slope[parity * pairs : (parity + 1) * pairs].astype(F32)
                joined[at : at + pairs] = value.astype(BF16)

    used = [taps[:, pl.ds(pl.multiple_of((2 * i + offset) * size, 128), size)] for i in range(2)]
    value = dot(jnp.concatenate(used, axis=1), joined[...], ((1,), (0,)))
    out[...] = value if first else value + prior[0][...]


def whole(shape):
    return pl.BlockSpec(shape, lambda *_: (0,) * len(shape))


SCALARS = pl.BlockSpec(memory_space=pltpu.SMEM)


def call(kernel, ins, outs, scratch=(), limit=16, name=None, last=()):
    specs = [SCALARS if i.dtype == jnp.int32 and i.ndim == 1 else whole(i.shape) for i in ins]
    for at in last:
        shape = ins[at].shape
        specs[at] = pl.BlockSpec((STEM_ROWS,) + shape[1:], lambda *_: (shape[0] // STEM_ROWS - 1, 0))
    return pl.pallas_call(
        kernel,
        grid=(1,) if last else (),
        in_specs=specs,
        out_specs=[whole(s) for s, _ in outs],
        out_shape=[jax.ShapeDtypeStruct(s, d) for s, d in outs],
        scratch_shapes=[pltpu.VMEM(s, d) for s, d in scratch],
        compiler_params=pltpu.CompilerParams(vmem_limit_bytes=limit * MIB),
        name=name,
    )(*ins)


def gated(values, gates):
    return lax.optimization_barrier((values, gates))[0]


def shards(dna_bases, w_stem, w_enc, w_dec, targets):
    devices = lax.axis_size("seq")
    seq, chan = lax.axis_index("seq"), lax.axis_index("chan")
    hi, lo = chan // 2, chan % 2
    parity = (lo + seq) % 2
    pairs = dna_bases.shape[0] // 2
    total = pairs * devices
    rows = pairs + 2 * INNER
    stem_c = w_stem.shape[0]
    enc_c = w_dec.shape[2]
    across = [(c, c ^ 2) for c in range(4)]
    cores = [(c, c ^ 1) for c in range(4)]

    def ring(array, step):
        return lax.ppermute(array, "seq", [(i, (i + step) % devices) for i in range(devices)])

    def swap(array, distance):
        return lax.ppermute(array, "seq", [(i, i ^ distance) for i in range(devices)])

    place = jnp.stack([seq, hi, lo, parity]).astype(jnp.int32)
    first_chip, even = hi == 0, parity == 0
    target = [(seq + step) % devices // 2 == hi for step in (0, 2 - parity, 3)]
    own = dna_bases.reshape(1, 2 * pairs)
    stem_w = w_stem.transpose(1, 2, 0).reshape(4 * KW, stem_c)
    own, place, first_chip, even, target = lax.optimization_barrier((own, place, first_chip, even, target))

    first = swap(own, 1)
    second = lax.ppermute(own, "seq", [(i, (i + 1 - 2 * (1 - i % 2)) % devices) for i in range(devices)])
    enc_w = w_enc.transpose(1, 2, 0)
    dec_w = w_dec.transpose(1, 0, 2).reshape(KW, 4, stem_c, enc_c)
    picked = (KW, 1, stem_c, enc_c)
    stem_rows = jnp.concatenate([stem_w, jnp.zeros((STEM_ROWS - 4 * KW, stem_c), BF16)])
    mine, mine0, mine1, enc_send = pl.pallas_call(
        picks_kernel,
        in_specs=[SCALARS, whole(stem_rows.shape), pl.BlockSpec(memory_space=pl.ANY)],
        out_specs=[pl.BlockSpec(memory_space=pltpu.VMEM)] * 4,
        out_shape=[
            jax.ShapeDtypeStruct((KW * stem_c + STEM_ROWS, enc_c), BF16),
            jax.ShapeDtypeStruct((FIRST * stem_c + STEM_ROWS, enc_c), BF16),
            jax.ShapeDtypeStruct(((KW - FIRST) * stem_c, enc_c), BF16),
            jax.ShapeDtypeStruct((KW * stem_c + STEM_ROWS, 2 * enc_c), BF16),
        ],
        scratch_shapes=[pltpu.SemaphoreType.DMA((4 * KW,))],
        compiler_params=pltpu.CompilerParams(vmem_limit_bytes=6 * MIB),
        name="picks",
    )(place, stem_rows, enc_w)
    enc_oth = lax.ppermute(enc_send, "chan", cores)
    mine0_far = lax.ppermute(mine0, "chan", across)
    dec_send = pl.pallas_call(
        pick_kernel,
        grid_spec=pltpu.PrefetchScalarGridSpec(
            num_scalar_prefetch=1,
            grid=(2,),
            in_specs=[pl.BlockSpec(picked, lambda h, at: (0, 2 * h + 1 - at[2], 0, 0))],
            out_specs=pl.BlockSpec(picked, lambda h, at: (0, h, 0, 0)),
        ),
        out_shape=jax.ShapeDtypeStruct((KW, 2, stem_c, enc_c), BF16),
        compiler_params=pltpu.CompilerParams(vmem_limit_bytes=8 * MIB),
        name="dec_pick",
    )(place, dec_w)
    dec_came = lax.ppermute(dec_send, "chan", cores)

    held = (6, rows, stem_c)
    acc, stem, lhs, lhs_oth, split = call(
        functools.partial(stem_kernel, pairs=pairs, devices=devices),
        [place, own, first, second, stem_w, enc_oth, enc_w],
        [
            ((2 * rows, enc_c), F32),
            ((2, rows, stem_c), BF16),
            (held, BF16),
            (held, BF16),
            ((3, 2, pairs), jnp.int32),
        ],
        [((pairs + 2 * OUTER, stem_c), F32), ((pairs + 2 * OUTER, stem_c), F32)],
        limit=14,
        name="stem_conv",
        last=(5,),
    )
    (send,) = call(
        send_kernel,
        [place, acc, lhs_oth, enc_oth],
        [((2 * rows, enc_c), BF16)],
        limit=12,
        name="enc_conv",
    )
    came = lax.ppermute(send, "chan", across)

    (keep,) = call(
        keep_kernel,
        [gated(place, send), lhs, lhs_oth, enc_w, enc_oth],
        [((2 * rows, enc_c), F32)],
        limit=14,
        name="enc_keep",
    )
    targets_in, place_in = gated((targets, place), send)
    blocks = {0: split[0], 1: split[2], devices - 1: split[1]}
    for r in range(2, devices - 1):
        blocks[r] = ring(split[0], r)
    comb_own, comb_came = pl.pallas_call(
        comb_kernel,
        grid_spec=pltpu.PrefetchScalarGridSpec(
            num_scalar_prefetch=1,
            grid=(2,),
            in_specs=[
                pl.BlockSpec(picked, lambda h, at: (0, 2 * h + at[2], 0, 0)),
                pl.BlockSpec(picked, lambda h, at: (0, h, 0, 0)),
            ],
            out_specs=[pl.BlockSpec((3, 2, 1, stem_c, enc_c), lambda h, at: (0, 0, h, 0, 0))] * 2,
        ),
        out_shape=[jax.ShapeDtypeStruct((3, 2, 2, stem_c, enc_c), BF16)] * 2,
        compiler_params=pltpu.CompilerParams(vmem_limit_bytes=12 * MIB),
        name="dec_taps",
    )(place_in, dec_w, dec_came)
    targets_in = targets_in.T
    count, edge = 2 * pairs, 2 * SIDE
    below, above = ring(targets_in[:, count - edge :], 1), ring(targets_in[:, :edge], devices - 1)
    mine1_far = lax.ppermute(gated(mine1, (below, mine0_far)), "chan", across)
    (targets_at,) = call(
        targets_kernel,
        [place, targets_in, below, above],
        [((2, rows, 2 * stem_c), BF16)],
        [((count + 2 * edge, 128), F32)],
        limit=6,
        name="targets",
    )
    blank = jnp.zeros_like(stem)
    stem_at = jnp.where(
        first_chip, jnp.concatenate([stem, blank], axis=2), jnp.concatenate([blank, stem], axis=2)
    )
    place_in = gated(place, (comb_own, comb_came, targets_at, stem_at, list(blocks.values())))

    pooled, centre = call(
        functools.partial(pool_kernel, pairs=pairs, total=total),
        [place_in, keep, came],
        [((rows, enc_c), BF16), ((pairs, enc_c), BF16)],
        limit=8,
        name="gelu_pool",
    )
    pooled_oth = lax.ppermute(pooled, "chan", cores)
    part, send = call(
        functools.partial(dec_kernel, pairs=pairs),
        [
            pooled,
            pooled_oth,
            comb_own.reshape(3, 4 * stem_c, enc_c),
            comb_came.reshape(3, 4 * stem_c, enc_c),
            stem_at,
            targets_at,
        ],
        [((rows, 4 * stem_c), F32), ((rows, 4 * stem_c), BF16)],
        [((rows + 16, enc_c), F32)],
        limit=11,
        name="dec_conv",
    )
    came = lax.ppermute(gated(send, mine1_far), "chan", across)

    centre, place_in = gated((centre, place), send)
    beyond, beside = swap(centre, 2), swap(centre, 1)

    weights = [mine, lax.ppermute(gated(mine, keep), "chan", cores), mine0_far, mine1_far]
    weights += [lax.ppermute(w, "chan", cores) for w in weights[2:]]

    def owner_slope(slot, at):
        (out,) = call(
            functools.partial(owner_slope_kernel, slot=slot, pairs=pairs, devices=devices),
            [at] + [blocks[r] for r in range(devices)] + weights,
            [((2 * pairs, enc_c), BF16)],
            [
                ((devices, 2, pairs), jnp.int32),
                ((rows, stem_c), F32),
                ((rows, stem_c), F32),
                ((6, pairs, stem_c), BF16),
            ],
            limit=10,
            name="owner_slope",
        )
        return out, lax.ppermute(out, "chan", cores)

    slope0, slope0_came = owner_slope(0, gated(place, send))

    pred, sums, local, near, far = call(
        functools.partial(slope_kernel, pairs=pairs, total=total, scale=1.0 / math.sqrt(2 * total)),
        [gated(place, (beyond, beside, slope0)), part, came, targets_at],
        [((2, pairs, stem_c), BF16), ((2, 2, rows, stem_c), BF16)] + [((2, rows, stem_c), BF16)] * 3,
        [((rows + 8, 2 * stem_c), F32)],
        limit=7,
        name="out_slope",
    )
    sums_oth = lax.ppermute(sums, "chan", cores)
    (pre,) = call(
        functools.partial(back_kernel, pairs=pairs),
        [place, sums, sums_oth, dec_w],
        [((pairs, enc_c), BF16)],
        [((2, rows, stem_c), F32)],
        limit=11,
        name="up_grad",
    )

    def link(steps):
        out = []
        for s in range(devices):
            for step in steps:
                t = (s + step) % devices
                for x in range(2):
                    out.append((s * 4 + 2 * x + t % 2, t * 4 + 2 * x + (t + step) % 2))
        return out

    def to_owner(local, near, far):
        near = lax.ppermute(near, ("seq", "chan"), link((1, 2)))
        far = lax.ppermute(far, ("seq", "chan"), link((3,)))
        return local, near, far

    def slots(local, near, far):
        return jnp.stack([jnp.where(even, local, near), jnp.where(even, near, far)])

    local, near, far = to_owner(local, near, far)
    pre_oth = lax.ppermute(pre, "chan", across)
    slope1, slope1_came = owner_slope(1, gated(place, pre))
    (taps,) = call(
        functools.partial(taps_kernel, pairs=pairs, devices=devices),
        [gated(place, slope1)] + [blocks[r] for r in range(devices)] + [stem_w],
        [((KW * stem_c, 2 * pairs * devices), BF16)],
        limit=12,
        name="stem_taps",
    )
    near, far = gated((near, far), taps)
    far_pooled = swap(gated(beyond, taps), 1)
    sums_pieces = local, near, far
    pre_oth = gated(pre_oth, (near, far, slope1, taps))
    pieces = [jnp.where(own_block, pre, pre_oth) for own_block in target]
    local, near, far = to_owner(*pieces)
    sums_mine = gated(slots(*sums_pieces), pieces)
    sums_came = lax.ppermute(sums_mine, "chan", cores)

    (pred,) = call(
        pred_kernel,
        [pred],
        [((stem_c, 2 * pairs), BF16)],
        [((2 * pairs, 128), F32)],
        limit=5,
        name="pred",
    )
    pred = pred.T
    (g_dec,) = call(
        functools.partial(dec_grad_kernel, pairs=pairs),
        [place, sums_mine, sums_came, centre, beside, beyond, far_pooled],
        [((KW, stem_c, enc_c), F32)],
        [
            ((2, rows, stem_c), F32),
            ((KW, devices * pairs, stem_c), BF16),
            ((devices * pairs, enc_c), BF16),
        ],
        limit=12,
        name="dec_grad",
    )
    near, far = gated((near, far), (g_dec, pred))
    pre_mine = slots(local, near, far)
    pre_came = lax.ppermute(pre_mine, "chan", cores)

    def enc_grad(first, *arrays):
        half = (KW * stem_c // 2, enc_c)
        return pl.pallas_call(
            functools.partial(enc_grad_kernel, first=first),
            grid=(2,),
            in_specs=[SCALARS, pl.BlockSpec((half[0], 2 * pairs * devices), lambda k: (k, 0))]
            + [whole(p.shape) for p in arrays[:3]]
            + [pl.BlockSpec(half, lambda k: (k, 0))] * len(arrays[3:]),
            out_specs=pl.BlockSpec(half, lambda k: (k, 0)),
            out_shape=jax.ShapeDtypeStruct((KW * stem_c, enc_c), F32),
            scratch_shapes=[pltpu.VMEM((4 * pairs, enc_c), BF16)],
            compiler_params=pltpu.CompilerParams(vmem_limit_bytes=13 * MIB),
            name="enc_grad",
        )(place, taps, *arrays)

    g_enc = enc_grad(True, pre_mine, slope0, slope1)
    g_enc = enc_grad(False, pre_came, slope0_came, slope1_came, g_enc)
    g_enc = g_enc.reshape(KW, stem_c, enc_c).transpose(2, 0, 1)
    return (pred, g_enc, g_dec.transpose(1, 0, 2))


def extended(block, sides, width):
    for axis, dim in sides:
        count = lax.axis_size(axis)
        forward = [(i, i + 1) for i in range(count - 1)]
        backward = [(target, source) for source, target in forward]
        low = lax.ppermute(
            lax.slice_in_dim(block, block.shape[dim] - width, None, axis=dim), axis, forward
        )
        high = lax.ppermute(lax.slice_in_dim(block, 0, width, axis=dim), axis, backward)
        block = jnp.concatenate([low, block, high], axis=dim)
    return block


def rim_cells(block, margin):
    return extended(block, (("seq", 0),), margin)


def channel_sum(partial_value):
    return lax.psum_scatter(partial_value, "chan", scatter_dimension=1, tiled=True)


def channel_gather(block):
    return lax.all_gather(block, "chan", axis=1, tiled=True)


def conv_rows(padded, weight):
    row_count = padded.shape[0] - 4
    total = jnp.zeros((row_count, weight.shape[0]), jnp.float32)
    for k in range(KW):
        total = total + lax.dot_general(
            padded[k : k + row_count],
            weight[:, k, :],
            (((1,), (1,)), ((), ())),
            preferred_element_type=jnp.float32,
        )
    return total


def grad_taps(picked, padded):
    row_count = picked.shape[0]
    pieces = [
        lax.dot_general(
            picked,
            padded[k : k + row_count],
            (((0,), (0,)), ((), ())),
            preferred_element_type=jnp.float32,
        )
        for k in range(KW)
    ]
    return jnp.stack(pieces, axis=1)


def weight_grad(cotangent, padded):
    rounded = grad_taps(cotangent, padded).astype(jnp.bfloat16)
    return lax.psum_scatter(
        lax.optimization_barrier(rounded).astype(jnp.float32),
        "seq",
        scatter_dimension=0,
        tiled=True,
    )


def general_shards(dna_bases, w_stem, w_enc, w_dec, targets):
    row_count = dna_bases.shape[0]
    devices = lax.axis_size("seq")
    length = row_count * devices
    onehot = (dna_bases[:, None] == jnp.arange(4, dtype=jnp.int32)[None, :]).astype(jnp.bfloat16)
    onehot_pad = rim_cells(onehot, 2)
    stem_out = gelu_value(conv_rows(onehot_pad, w_stem)).astype(jnp.bfloat16)
    stem_pad = rim_cells(stem_out, 2)
    enc_pre = channel_sum(conv_rows(stem_pad, w_enc))
    active = gelu_value(enc_pre).astype(jnp.bfloat16).astype(jnp.float32)
    pooled = (0.5 * active.reshape(row_count // 2, 2, -1).sum(axis=1)).astype(jnp.bfloat16)
    pooled_pad = rim_cells(pooled, 1)
    up_pad = jnp.repeat(pooled_pad, 2, axis=0)
    output = channel_sum(conv_rows(up_pad, w_dec)) + stem_out.astype(jnp.float32)
    pred = output.astype(jnp.bfloat16)
    scale = 1.0 / math.sqrt(length)
    slope_out = ((output - targets.astype(jnp.float32)) * scale).astype(jnp.bfloat16)
    slope_all = channel_gather(slope_out)
    g_dec = weight_grad(slope_all, up_pad)
    slope_pad = rim_cells(slope_all, 2)
    up_grad = jnp.zeros((row_count, w_dec.shape[2]), jnp.float32)
    for k in range(KW):
        up_grad = up_grad + jnp.dot(
            slope_pad[4 - k : 4 - k + row_count], w_dec[:, k, :], preferred_element_type=jnp.float32
        )
    pool_grad = up_grad.reshape(row_count // 2, 2, -1).sum(axis=1)
    act_grad = 0.5 * jnp.repeat(pool_grad, 2, axis=0)
    pre_grad = (act_grad * gelu_slope(enc_pre)).astype(jnp.bfloat16)
    pre_all = channel_gather(pre_grad)
    g_enc = weight_grad(pre_all, stem_pad)
    return (pred, g_enc, g_dec)


def solution(mesh):
    sizes = mesh.shape["seq"], mesh.shape["chan"]
    return jax.shard_map(
        shards if sizes == (4, 4) else general_shards,
        mesh=mesh,
        in_specs=(
            P(("groups", "seq")),
            P("chan", None, None),
            P(None, None, "chan"),
            P(None, None, "chan"),
            P(("groups", "seq"), "chan"),
        ),
        out_specs=(
            P(("groups", "seq"), "chan"),
            P(("groups", "seq"), None, "chan"),
            P(("groups", "seq"), None, "chan"),
        ),
        check_vma=False,
    )
```

```python
import functools
import math

import jax
import jax.numpy as jnp
from jax import lax
from jax.experimental import pallas as pl
from jax.experimental.pallas import tpu as pltpu
from jax.sharding import PartitionSpec as P

KW = 5

SQRT_TWO_PI = 0.7978845608028654
CUBIC = 0.044715

STEM_ROWS = 32
FIRST = 3
SIDE = 64
OUTER = 16
INNER = 8
F32 = jnp.float32
BF16 = jnp.bfloat16
MIB = 1024 * 1024


def gelu_value(value):
    inner = jnp.tanh(SQRT_TWO_PI * (value + CUBIC * value * value * value))
    return 0.5 * value * (1.0 + inner)


def gelu_slope(value):
    inner = jnp.tanh(SQRT_TWO_PI * (value + CUBIC * value * value * value))
    return 0.5 * (1.0 + inner) + 0.5 * value * (1.0 - inner * inner) * SQRT_TWO_PI * (
        1.0 + 3.0 * CUBIC * value * value
    )


def dot(a, b, contract):
    return lax.dot_general(a, b, (contract, ((), ())), preferred_element_type=F32)


def assemble(own, after, before, block, devices):
    side = 2 * SIDE
    pairs = own.shape[1]
    column = lax.broadcasted_iota(jnp.int32, (2, side), 1)
    after = jnp.where(block == devices - 1, -1, after[:, :side])
    before = jnp.where(block == 0, -1, before[:, pairs - side :])
    return jnp.concatenate([own, jnp.where(column < SIDE, after, before)], axis=1)


def split_parity(blocks):
    count = blocks[0].shape[1]
    row = lax.broadcasted_iota(jnp.int32, (count, count), 0)
    column = lax.broadcasted_iota(jnp.int32, (count, count), 1)
    source = jnp.where(column < count // 2, 2 * column, 2 * column - count + 1)
    chosen = jnp.where(row == source, 1.0, 0.0).astype(BF16)
    place = lax.broadcasted_iota(jnp.int32, (16, count), 0)
    wide = jnp.broadcast_to(blocks[0], (16, count))
    for i, block in enumerate(blocks[1:]):
        wide = jnp.where(place == i + 1, jnp.broadcast_to(block, (16, count)), wide)
    value = dot(wide.astype(F32).astype(BF16), chosen, ((1,), (0,))).astype(jnp.int32)
    return [
        jnp.concatenate([value[i : i + 1, : count // 2], value[i : i + 1, count // 2 :]], axis=0)
        for i in range(len(blocks))
    ]


def tap_onehots(bases, start, width):
    total = bases.shape[1]
    before = pltpu.roll(bases, (1 - start) % total, 1)[:, :width]
    here = bases[:, :width] if start == 0 else pltpu.roll(bases, -start % total, 1)[:, :width]
    after = pltpu.roll(bases, (-1 - start) % total, 1)[:, :width]
    taps = [before[0:1], before[1:2], here[0:1], here[1:2], after[0:1], after[1:2]]
    row = lax.broadcasted_iota(jnp.int32, (4 * KW, width), 0)
    tap, base = row >> 2, row & 3
    out = []
    for first in (0, 1):
        value = jnp.full((4 * KW, width), -1, jnp.int32)
        for k in range(KW):
            value = jnp.where(tap == k, jnp.broadcast_to(taps[first + k], value.shape), value)
        out.append(jnp.where(value == base, 1.0, 0.0).astype(BF16))
    return out


def valid_pairs(shape, dim, first, total):
    pair = lax.broadcasted_iota(jnp.int32, shape, dim) + first
    return (pair >= 0) & (pair < total)


def stem_kernel(
    place, own, after, before, stem_own, w_oth, w_own, acc, stem_out, lhs, lhs_oth, split, even, odd, *, pairs, devices
):
    seq = place[0]
    rows = pairs + 2 * INNER
    wide = pairs + 2 * OUTER
    swapped = lax.rem(seq, 2) == 1
    first, second = after[...], before[...]
    parts = split_parity([own[...], jnp.where(swapped, second, first), jnp.where(swapped, first, second)])
    for i, part in enumerate(parts):
        split[i] = part
    hots = tap_onehots(assemble(*parts, seq, devices), -OUTER, wide)
    gap = OUTER - INNER
    stem_oth = w_oth[: stem_own.shape[0], : stem_own.shape[1]]
    for weight, held_lhs in ((stem_own[...], lhs), (stem_oth, lhs_oth)):
        for hot, held in zip(hots, (even, odd)):
            raw = dot(hot, weight, ((0,), (0,)))
            ok = valid_pairs(raw.shape, 0, seq * pairs - OUTER, pairs * devices)
            held[...] = jnp.where(ok, gelu_value(raw), 0.0).astype(BF16).astype(F32)
        for k in range(6):
            source = even if k % 2 == 0 else odd
            held_lhs[k] = source[gap + k // 2 - 1 : gap + k // 2 - 1 + rows, :].astype(BF16)
    stem_out[0] = lhs[2]
    stem_out[1] = lhs[3]
    acc[...] = own_sums(lhs, w_own, 2 * (1 - place[1]) + place[2], acc.shape)


def own_sums(lhs, weight, index, shape):
    at = pl.ds(pl.multiple_of(index * shape[1], 128), shape[1])
    total = jnp.zeros(shape, F32)
    for k in range(KW):
        total = total + dot(lhs[k : k + 2].reshape(shape[0], -1), weight[k, :, at], ((1,), (0,)))
    return total


def other_sums(lhs, weight, index, total):
    rows, block = total.shape
    channels = lhs.shape[2]
    at = pl.ds(pl.multiple_of(index * block, 128), block)
    for k in range(KW):
        tap = weight[k * channels : (k + 1) * channels, at]
        total = total + dot(lhs[k : k + 2].reshape(rows, -1), tap, ((1,), (0,)))
    return total


def send_kernel(place, acc, lhs, w_oth, send):
    send[...] = other_sums(lhs, w_oth, 1 - place[1], acc[...]).astype(BF16)


def keep_kernel(place, lhs, lhs_oth, w_own, w_oth, keep):
    total = own_sums(lhs, w_own, 2 * place[1] + place[2], keep.shape)
    keep[...] = other_sums(lhs_oth, w_oth, place[1], total)


def pool_kernel(place, keep, came, pooled, centre, *, pairs, total):
    rows = pairs + 2 * INNER
    value = keep[...] + came[...].astype(F32)
    active = gelu_value(value).astype(BF16).astype(F32)
    both = 0.5 * (active[:rows] + active[rows:])
    ok = valid_pairs(both.shape, 0, place[0] * pairs - INNER, total)
    both = jnp.where(ok, both, 0.0).astype(BF16)
    pooled[...] = both
    centre[...] = both[INNER : INNER + pairs].astype(BF16)


def dec_kernel(own, oth, w_own, w_oth, stem, targets, part, send, held, *, pairs):
    rows = pairs + 2 * INNER
    held[:8] = jnp.zeros((8, held.shape[1]), F32)
    held[8 + rows :] = jnp.zeros((8, held.shape[1]), F32)
    acc = jnp.zeros(part.shape, F32)
    for source, weight in ((own, w_own), (oth, w_oth)):
        held[8 : 8 + rows] = source[...].astype(F32)
        for k in range(3):
            acc = acc + dot(held[7 + k : 7 + k + rows].astype(BF16), weight[k], ((1,), (1,)))
    half = part.shape[1] // 2
    for parity in range(2):
        value = acc[:, parity * half : (parity + 1) * half]
        value = value + stem[parity].astype(F32) - targets[parity].astype(F32)
        part[:, parity * half : (parity + 1) * half] = value
        send[:, parity * half : (parity + 1) * half] = value.astype(BF16)


def slope_kernel(place, part, came, targets, pred, sums, local, near, far, held, *, pairs, total, scale):
    rows = pairs + 2 * INNER
    half = part.shape[1] // 2
    quarter = half // 2
    ok = valid_pairs((rows, half), 0, place[0] * pairs - INNER, total)
    second = place[1] == 1
    slopes = []
    for parity in range(2):
        cols = slice(parity * half, (parity + 1) * half)
        value = part[:, cols] + came[:, cols].astype(F32)
        out = (value + targets[parity].astype(F32))[INNER : INNER + pairs]
        pred[parity] = jnp.where(second, out[:, quarter:], out[:, :quarter]).astype(BF16)
        slopes.append(jnp.where(ok, value * scale, 0.0).astype(BF16).astype(F32))
    held[:rows] = slopes[0]
    held[rows:] = jnp.zeros((8, half), F32)
    both = slopes[0] + slopes[1], slopes[1] + held[1 : 1 + rows]
    for i in range(2):
        for h in range(2):
            sums[h, i] = both[i][:, h * quarter : (h + 1) * quarter].astype(BF16)
    for out, step in ((local, 0), (near, 2 - place[3]), (far, 3)):
        out[...] = sums[lax.rem(place[0] + step, 4) // 2]


def lane_tiles(channels):
    return [(first, min(first + 128, channels)) for first in range(0, channels, 128)]


def targets_kernel(place, own, before, after, out, held):
    channels, count = own.shape
    side = before.shape[1]
    rows = count // 2 + 2 * INNER
    high = place[1] == 1
    for first, last in lane_tiles(channels):
        wide = last - first
        held[:side, :wide] = before[first:last].astype(F32).T
        held[side : side + count, :wide] = own[first:last].astype(F32).T
        held[side + count :, :wide] = after[first:last].astype(F32).T
        for parity in range(2):
            value = held[pl.ds(side - 2 * INNER + parity, rows, stride=2), :][:, :wide].astype(BF16)
            blank = jnp.zeros_like(value)
            out[parity, :, first:last] = jnp.where(high, blank, value)
            out[parity, :, channels + first : channels + last] = jnp.where(high, value, blank)


def pred_kernel(source, out, held):
    channels, count = out.shape
    for first, last in lane_tiles(channels):
        wide = last - first
        for parity in range(2):
            value = source[parity, :, first:last].astype(F32)
            if wide < 128:
                value = jnp.concatenate([value, jnp.zeros((count // 2, 128 - wide), F32)], axis=1)
            held[pl.ds(parity, count // 2, stride=2), :] = value
        out[first:last] = held[:, :wide].T.astype(BF16)


def shifted_sums(held, pairs):
    return [
        held[0, INNER + 1 : INNER + 1 + pairs].astype(BF16),
        held[1, INNER : INNER + pairs].astype(BF16),
        held[0, INNER : INNER + pairs].astype(BF16),
        held[1, INNER - 1 : INNER - 1 + pairs].astype(BF16),
        held[0, INNER - 1 : INNER - 1 + pairs].astype(BF16),
    ]


def back_kernel(place, own, oth, weight, out, held, *, pairs):
    acc = jnp.zeros(out.shape, F32)
    for source, core in ((own, place[2]), (oth, 1 - place[2])):
        for h in range(2):
            held[...] = source[h].astype(F32)
            for k, tap in enumerate(shifted_sums(held, pairs)):
                acc = acc + dot(tap, weight[k, 2 * h + core], ((1,), (0,)))
    out[...] = (0.5 * acc).astype(BF16)


def owner_slope_kernel(place, *refs, slot, pairs, devices):
    blocks, weights = refs[:devices], refs[devices : devices + 6]
    out, bases, even, odd, lhs = refs[devices + 6 :]
    for r in range(devices):
        bases[r] = blocks[r][...]
    wide = pairs + 2 * INNER
    step = 2 * slot + place[3]
    block = lax.rem(place[0] - step + devices, devices)
    before, after = lax.rem(step + 1, devices), lax.rem(step + devices - 1, devices)
    joined = assemble(bases[step], bases[after], bases[before], block, devices)
    hots = tap_onehots(joined, -INNER, wide)
    total = jnp.zeros(out.shape, F32)
    channels = lhs.shape[2]
    for some, others in ((0, None), (1, None), (2, 3), (4, 5)):
        count = KW if others is None else FIRST
        weight = weights[some][count * channels : count * channels + 4 * KW, :channels]
        for hot, held in zip(hots, (even, odd)):
            raw = dot(hot, weight, ((0,), (0,)))
            ok = valid_pairs(raw.shape, 0, block * pairs - INNER, pairs * devices)
            held[...] = jnp.where(ok, gelu_value(raw), 0.0).astype(BF16).astype(F32)
        for k in range(6):
            source = even if k % 2 == 0 else odd
            lhs[k] = source[INNER + k // 2 - 1 : INNER + k // 2 - 1 + pairs, :].astype(BF16)
        for k in range(KW):
            at, step = (some, k) if k < count else (others, k - count)
            tap = weights[at][step * channels : (step + 1) * channels, :]
            total = total + dot(lhs[k : k + 2].reshape(2 * pairs, -1), tap, ((1,), (0,)))
    out[...] = gelu_slope(total).astype(BF16)


def taps_kernel(place, *refs, pairs, devices):
    blocks, (stem_w, out) = refs[:devices], refs[devices:]
    channels = stem_w.shape[1]
    for r in range(devices):
        block = lax.rem(place[0] - r + devices, devices)
        bases = assemble(blocks[r][...], blocks[r - 1][...], blocks[(r + 1) % devices][...], block, devices)
        width = bases.shape[1]
        parts = []
        for hot in tap_onehots(bases, 0, width):
            raw = dot(stem_w[...], hot, ((0,), (0,)))
            column = lax.broadcasted_iota(jnp.int32, raw.shape, 1)
            pair = jnp.where(column >= width - SIDE, column - width, column) + block * pairs
            ok = (pair >= 0) & (pair < pairs * devices)
            parts.append(jnp.where(ok, gelu_value(raw), 0.0))
        taps = []
        for step in (-1, 0, 1):
            for held in parts:
                moved = held if step == 0 else pltpu.roll(held, -step % width, 1)
                taps.append(moved[:, :pairs].astype(BF16))
        at = 2 * r * pairs
        for k in range(KW):
            out[k * channels : (k + 1) * channels, at : at + pairs] = taps[k]
            out[k * channels : (k + 1) * channels, at + pairs : at + 2 * pairs] = taps[k + 1]


def picks_kernel(place, stem, enc, mine, mine0, mine1, enc_oth, sems):
    seq, core = place[0], 1 - place[2]
    taps, channels, _ = enc.shape
    block = mine0.shape[1]

    def columns(index):
        return pl.ds(pl.multiple_of(index * block, 128), block)

    copies = []
    for k in range(taps):
        rows = pl.ds(k * channels, channels)
        for h in range(2):
            copies.append((enc.at[k, :, columns(2 * h + core)], enc_oth.at[rows, h * block : (h + 1) * block]))
        copies.append((enc.at[k, :, columns(seq)], mine.at[rows]))
        if k < FIRST:
            copies.append((enc.at[k, :, columns(seq)], mine0.at[rows]))
        else:
            copies.append((enc.at[k, :, columns(seq)], mine1.at[pl.ds((k - FIRST) * channels, channels)]))
    copies = [pltpu.make_async_copy(*ends, sems.at[i]) for i, ends in enumerate(copies)]
    for copy in copies:
        copy.start()
    enc_oth[taps * channels :, : stem.shape[1]] = stem[...]
    mine0[FIRST * channels :, : stem.shape[1]] = stem[...]
    mine[taps * channels :, : stem.shape[1]] = stem[...]
    for copy in copies:
        copy.wait()


def pick_kernel(place, source, out):
    out[...] = source[...]


def comb_kernel(place, own, came, comb_own, comb_came):
    combine(own, comb_own)
    combine(came, comb_came)


def combine(weight, comb):
    comb[0, 0] = weight[0] + weight[1]
    comb[1, 0] = weight[2] + weight[3]
    comb[2, 0] = weight[4]
    comb[0, 1] = weight[0]
    comb[1, 1] = weight[1] + weight[2]
    comb[2, 1] = weight[3] + weight[4]


def dec_grad_kernel(place, own, came, pool0, pool1, pool2, pool3, out, held, taps, pooled, *, pairs):
    blocks = (pool0, pool1, pool2, pool3)
    parity = place[3]
    odd = lax.rem(place[0], 2)
    for block, step in zip(blocks, (0, 3 - 2 * odd, 2, 1 + 2 * odd)):
        pooled[pl.ds(pl.multiple_of(step * pairs, pairs), pairs), :] = block[...]
    for i in range(4):
        slots = own if i < 2 else came
        held[...] = slots[i % 2].astype(F32)
        step = 2 * (i % 2) + (parity if i < 2 else 1 - parity)
        at = pl.ds(pl.multiple_of(step * pairs, pairs), pairs)
        for k, tap in enumerate(shifted_sums(held, pairs)):
            taps[k, at, :] = tap
    for k in range(KW):
        out[k] = dot(taps[k], pooled[...], ((0,), (0,)))


def enc_grad_kernel(place, taps, slots, slope0, slope1, *refs, first):
    prior, (out, joined) = refs[:-2], refs[-2:]
    pairs = slots.shape[1]
    size = 2 * pairs
    offset = place[3] if first else 1 - place[3]

    @pl.when(pl.program_id(0) == 0)
    def _():
        for i, slope in enumerate((slope0, slope1)):
            grad = slots[i].astype(F32)
            for parity in range(2):
                at = i * size + parity * pairs
                value = grad * slope[parity * pairs : (parity + 1) * pairs].astype(F32)
                joined[at : at + pairs] = value.astype(BF16)

    used = [taps[:, pl.ds(pl.multiple_of((2 * i + offset) * size, 128), size)] for i in range(2)]
    value = dot(jnp.concatenate(used, axis=1), joined[...], ((1,), (0,)))
    out[...] = value if first else value + prior[0][...]


def whole(shape):
    return pl.BlockSpec(shape, lambda *_: (0,) * len(shape))


SCALARS = pl.BlockSpec(memory_space=pltpu.SMEM)


def call(kernel, ins, outs, scratch=(), limit=16, name=None, last=()):
    specs = [SCALARS if i.dtype == jnp.int32 and i.ndim == 1 else whole(i.shape) for i in ins]
    for at in last:
        shape = ins[at].shape
        specs[at] = pl.BlockSpec((STEM_ROWS,) + shape[1:], lambda *_: (shape[0] // STEM_ROWS - 1, 0))
    return pl.pallas_call(
        kernel,
        grid=(1,) if last else (),
        in_specs=specs,
        out_specs=[whole(s) for s, _ in outs],
        out_shape=[jax.ShapeDtypeStruct(s, d) for s, d in outs],
        scratch_shapes=[pltpu.VMEM(s, d) for s, d in scratch],
        compiler_params=pltpu.CompilerParams(vmem_limit_bytes=limit * MIB),
        name=name,
    )(*ins)


def gated(values, gates):
    return lax.optimization_barrier((values, gates))[0]


def shards(dna_bases, w_stem, w_enc, w_dec, targets):
    devices = lax.axis_size("seq")
    seq, chan = lax.axis_index("seq"), lax.axis_index("chan")
    hi, lo = chan // 2, chan % 2
    parity = (lo + seq) % 2
    pairs = dna_bases.shape[0] // 2
    total = pairs * devices
    rows = pairs + 2 * INNER
    stem_c = w_stem.shape[0]
    enc_c = w_dec.shape[2]
    across = [(c, c ^ 2) for c in range(4)]
    cores = [(c, c ^ 1) for c in range(4)]

    def ring(array, step):
        return lax.ppermute(array, "seq", [(i, (i + step) % devices) for i in range(devices)])

    def swap(array, distance):
        return lax.ppermute(array, "seq", [(i, i ^ distance) for i in range(devices)])

    place = jnp.stack([seq, hi, lo, parity]).astype(jnp.int32)
    first_chip, even = hi == 0, parity == 0
    target = [(seq + step) % devices // 2 == hi for step in (0, 2 - parity, 3)]
    own = dna_bases.reshape(1, 2 * pairs)
    stem_w = w_stem.transpose(1, 2, 0).reshape(4 * KW, stem_c)
    own, place, first_chip, even, target = lax.optimization_barrier((own, place, first_chip, even, target))

    first = swap(own, 1)
    second = lax.ppermute(own, "seq", [(i, (i + 1 - 2 * (1 - i % 2)) % devices) for i in range(devices)])
    enc_w = w_enc.transpose(1, 2, 0)
    dec_w = w_dec.transpose(1, 0, 2).reshape(KW, 4, stem_c, enc_c)
    picked = (KW, 1, stem_c, enc_c)
    stem_rows = jnp.concatenate([stem_w, jnp.zeros((STEM_ROWS - 4 * KW, stem_c), BF16)])
    mine, mine0, mine1, enc_send = pl.pallas_call(
        picks_kernel,
        in_specs=[SCALARS, whole(stem_rows.shape), pl.BlockSpec(memory_space=pl.ANY)],
        out_specs=[pl.BlockSpec(memory_space=pltpu.VMEM)] * 4,
        out_shape=[
            jax.ShapeDtypeStruct((KW * stem_c + STEM_ROWS, enc_c), BF16),
            jax.ShapeDtypeStruct((FIRST * stem_c + STEM_ROWS, enc_c), BF16),
            jax.ShapeDtypeStruct(((KW - FIRST) * stem_c, enc_c), BF16),
            jax.ShapeDtypeStruct((KW * stem_c + STEM_ROWS, 2 * enc_c), BF16),
        ],
        scratch_shapes=[pltpu.SemaphoreType.DMA((4 * KW,))],
        compiler_params=pltpu.CompilerParams(vmem_limit_bytes=6 * MIB),
        name="picks",
    )(place, stem_rows, enc_w)
    enc_oth = lax.ppermute(enc_send, "chan", cores)
    mine0_far = lax.ppermute(mine0, "chan", across)
    dec_send = pl.pallas_call(
        pick_kernel,
        grid_spec=pltpu.PrefetchScalarGridSpec(
            num_scalar_prefetch=1,
            grid=(2,),
            in_specs=[pl.BlockSpec(picked, lambda h, at: (0, 2 * h + 1 - at[2], 0, 0))],
            out_specs=pl.BlockSpec(picked, lambda h, at: (0, h, 0, 0)),
        ),
        out_shape=jax.ShapeDtypeStruct((KW, 2, stem_c, enc_c), BF16),
        compiler_params=pltpu.CompilerParams(vmem_limit_bytes=8 * MIB),
        name="dec_pick",
    )(place, dec_w)
    dec_came = lax.ppermute(dec_send, "chan", cores)

    held = (6, rows, stem_c)
    acc, stem, lhs, lhs_oth, split = call(
        functools.partial(stem_kernel, pairs=pairs, devices=devices),
        [place, own, first, second, stem_w, enc_oth, enc_w],
        [
            ((2 * rows, enc_c), F32),
            ((2, rows, stem_c), BF16),
            (held, BF16),
            (held, BF16),
            ((3, 2, pairs), jnp.int32),
        ],
        [((pairs + 2 * OUTER, stem_c), F32), ((pairs + 2 * OUTER, stem_c), F32)],
        limit=14,
        name="stem_conv",
        last=(5,),
    )
    (send,) = call(
        send_kernel,
        [place, acc, lhs_oth, enc_oth],
        [((2 * rows, enc_c), BF16)],
        limit=12,
        name="enc_conv",
    )
    came = lax.ppermute(send, "chan", across)

    (keep,) = call(
        keep_kernel,
        [gated(place, send), lhs, lhs_oth, enc_w, enc_oth],
        [((2 * rows, enc_c), F32)],
        limit=14,
        name="enc_keep",
    )
    targets_in, place_in = gated((targets, place), send)
    blocks = {0: split[0], 1: split[2], devices - 1: split[1]}
    for r in range(2, devices - 1):
        blocks[r] = ring(split[0], r)
    comb_own, comb_came = pl.pallas_call(
        comb_kernel,
        grid_spec=pltpu.PrefetchScalarGridSpec(
            num_scalar_prefetch=1,
            grid=(2,),
            in_specs=[
                pl.BlockSpec(picked, lambda h, at: (0, 2 * h + at[2], 0, 0)),
                pl.BlockSpec(picked, lambda h, at: (0, h, 0, 0)),
            ],
            out_specs=[pl.BlockSpec((3, 2, 1, stem_c, enc_c), lambda h, at: (0, 0, h, 0, 0))] * 2,
        ),
        out_shape=[jax.ShapeDtypeStruct((3, 2, 2, stem_c, enc_c), BF16)] * 2,
        compiler_params=pltpu.CompilerParams(vmem_limit_bytes=12 * MIB),
        name="dec_taps",
    )(place_in, dec_w, dec_came)
    targets_in = targets_in.T
    count, edge = 2 * pairs, 2 * SIDE
    below, above = ring(targets_in[:, count - edge :], 1), ring(targets_in[:, :edge], devices - 1)
    mine1_far = lax.ppermute(gated(mine1, (below, mine0_far)), "chan", across)
    (targets_at,) = call(
        targets_kernel,
        [place, targets_in, below, above],
        [((2, rows, 2 * stem_c), BF16)],
        [((count + 2 * edge, 128), F32)],
        limit=6,
        name="targets",
    )
    blank = jnp.zeros_like(stem)
    stem_at = jnp.where(
        first_chip, jnp.concatenate([stem, blank], axis=2), jnp.concatenate([blank, stem], axis=2)
    )
    place_in = gated(place, (comb_own, comb_came, targets_at, stem_at, list(blocks.values())))

    pooled, centre = call(
        functools.partial(pool_kernel, pairs=pairs, total=total),
        [place_in, keep, came],
        [((rows, enc_c), BF16), ((pairs, enc_c), BF16)],
        limit=8,
        name="gelu_pool",
    )
    pooled_oth = lax.ppermute(pooled, "chan", cores)
    part, send = call(
        functools.partial(dec_kernel, pairs=pairs),
        [
            pooled,
            pooled_oth,
            comb_own.reshape(3, 4 * stem_c, enc_c),
            comb_came.reshape(3, 4 * stem_c, enc_c),
            stem_at,
            targets_at,
        ],
        [((rows, 4 * stem_c), F32), ((rows, 4 * stem_c), BF16)],
        [((rows + 16, enc_c), F32)],
        limit=11,
        name="dec_conv",
    )
    came = lax.ppermute(gated(send, mine1_far), "chan", across)

    centre, place_in = gated((centre, place), send)
    beyond, beside = swap(centre, 2), swap(centre, 1)

    weights = [mine, lax.ppermute(gated(mine, keep), "chan", cores), mine0_far, mine1_far]
    weights += [lax.ppermute(w, "chan", cores) for w in weights[2:]]

    def owner_slope(slot, at):
        (out,) = call(
            functools.partial(owner_slope_kernel, slot=slot, pairs=pairs, devices=devices),
            [at] + [blocks[r] for r in range(devices)] + weights,
            [((2 * pairs, enc_c), BF16)],
            [
                ((devices, 2, pairs), jnp.int32),
                ((rows, stem_c), F32),
                ((rows, stem_c), F32),
                ((6, pairs, stem_c), BF16),
            ],
            limit=10,
            name="owner_slope",
        )
        return out, lax.ppermute(out, "chan", cores)

    slope0, slope0_came = owner_slope(0, gated(place, send))
    (taps,) = call(
        functools.partial(taps_kernel, pairs=pairs, devices=devices),
        [gated(place, slope0)] + [blocks[r] for r in range(devices)] + [stem_w],
        [((KW * stem_c, 2 * pairs * devices), BF16)],
        limit=12,
        name="stem_taps",
    )

    pred, sums, local, near, far = call(
        functools.partial(slope_kernel, pairs=pairs, total=total, scale=1.0 / math.sqrt(2 * total)),
        [gated(place, (beyond, beside, slope0, taps)), part, came, targets_at],
        [((2, pairs, stem_c), BF16), ((2, 2, rows, stem_c), BF16)] + [((2, rows, stem_c), BF16)] * 3,
        [((rows + 8, 2 * stem_c), F32)],
        limit=7,
        name="out_slope",
    )
    sums_oth = lax.ppermute(sums, "chan", cores)
    (pre,) = call(
        functools.partial(back_kernel, pairs=pairs),
        [place, sums, sums_oth, dec_w],
        [((pairs, enc_c), BF16)],
        [((2, rows, stem_c), F32)],
        limit=11,
        name="up_grad",
    )

    def link(steps):
        out = []
        for s in range(devices):
            for step in steps:
                t = (s + step) % devices
                for x in range(2):
                    out.append((s * 4 + 2 * x + t % 2, t * 4 + 2 * x + (t + step) % 2))
        return out

    def to_owner(local, near, far):
        near = lax.ppermute(near, ("seq", "chan"), link((1, 2)))
        far = lax.ppermute(far, ("seq", "chan"), link((3,)))
        return local, near, far

    def slots(local, near, far):
        return jnp.stack([jnp.where(even, local, near), jnp.where(even, near, far)])

    local, near, far = to_owner(local, near, far)
    pre_oth = lax.ppermute(pre, "chan", across)
    slope1, slope1_came = owner_slope(1, gated(place, pre))
    near, far = gated((near, far), slope1)
    far_pooled = swap(gated(beyond, pre), 1)
    sums_pieces = local, near, far
    pre_oth = gated(pre_oth, (near, far, slope1))
    pieces = [jnp.where(own_block, pre, pre_oth) for own_block in target]
    local, near, far = to_owner(*pieces)
    sums_mine = gated(slots(*sums_pieces), pieces)
    sums_came = lax.ppermute(sums_mine, "chan", cores)

    (pred,) = call(
        pred_kernel,
        [pred],
        [((stem_c, 2 * pairs), BF16)],
        [((2 * pairs, 128), F32)],
        limit=5,
        name="pred",
    )
    pred = pred.T
    (g_dec,) = call(
        functools.partial(dec_grad_kernel, pairs=pairs),
        [place, sums_mine, sums_came, centre, beside, beyond, far_pooled],
        [((KW, stem_c, enc_c), F32)],
        [
            ((2, rows, stem_c), F32),
            ((KW, devices * pairs, stem_c), BF16),
            ((devices * pairs, enc_c), BF16),
        ],
        limit=12,
        name="dec_grad",
    )
    near, far = gated((near, far), (g_dec, pred))
    pre_mine = slots(local, near, far)
    pre_came = lax.ppermute(pre_mine, "chan", cores)

    def enc_grad(first, *arrays):
        half = (KW * stem_c // 2, enc_c)
        return pl.pallas_call(
            functools.partial(enc_grad_kernel, first=first),
            grid=(2,),
            in_specs=[SCALARS, pl.BlockSpec((half[0], 2 * pairs * devices), lambda k: (k, 0))]
            + [whole(p.shape) for p in arrays[:3]]
            + [pl.BlockSpec(half, lambda k: (k, 0))] * len(arrays[3:]),
            out_specs=pl.BlockSpec(half, lambda k: (k, 0)),
            out_shape=jax.ShapeDtypeStruct((KW * stem_c, enc_c), F32),
            scratch_shapes=[pltpu.VMEM((4 * pairs, enc_c), BF16)],
            compiler_params=pltpu.CompilerParams(vmem_limit_bytes=13 * MIB),
            name="enc_grad",
        )(place, taps, *arrays)

    g_enc = enc_grad(True, pre_mine, slope0, slope1)
    g_enc = enc_grad(False, pre_came, slope0_came, slope1_came, g_enc)
    g_enc = g_enc.reshape(KW, stem_c, enc_c).transpose(2, 0, 1)
    return (pred, g_enc, g_dec.transpose(1, 0, 2))


def extended(block, sides, width):
    for axis, dim in sides:
        count = lax.axis_size(axis)
        forward = [(i, i + 1) for i in range(count - 1)]
        backward = [(target, source) for source, target in forward]
        low = lax.ppermute(
            lax.slice_in_dim(block, block.shape[dim] - width, None, axis=dim), axis, forward
        )
        high = lax.ppermute(lax.slice_in_dim(block, 0, width, axis=dim), axis, backward)
        block = jnp.concatenate([low, block, high], axis=dim)
    return block


def rim_cells(block, margin):
    return extended(block, (("seq", 0),), margin)


def channel_sum(partial_value):
    return lax.psum_scatter(partial_value, "chan", scatter_dimension=1, tiled=True)


def channel_gather(block):
    return lax.all_gather(block, "chan", axis=1, tiled=True)


def conv_rows(padded, weight):
    row_count = padded.shape[0] - 4
    total = jnp.zeros((row_count, weight.shape[0]), jnp.float32)
    for k in range(KW):
        total = total + lax.dot_general(
            padded[k : k + row_count],
            weight[:, k, :],
            (((1,), (1,)), ((), ())),
            preferred_element_type=jnp.float32,
        )
    return total


def grad_taps(picked, padded):
    row_count = picked.shape[0]
    pieces = [
        lax.dot_general(
            picked,
            padded[k : k + row_count],
            (((0,), (0,)), ((), ())),
            preferred_element_type=jnp.float32,
        )
        for k in range(KW)
    ]
    return jnp.stack(pieces, axis=1)


def weight_grad(cotangent, padded):
    rounded = grad_taps(cotangent, padded).astype(jnp.bfloat16)
    return lax.psum_scatter(
        lax.optimization_barrier(rounded).astype(jnp.float32),
        "seq",
        scatter_dimension=0,
        tiled=True,
    )


def general_shards(dna_bases, w_stem, w_enc, w_dec, targets):
    row_count = dna_bases.shape[0]
    devices = lax.axis_size("seq")
    length = row_count * devices
    onehot = (dna_bases[:, None] == jnp.arange(4, dtype=jnp.int32)[None, :]).astype(jnp.bfloat16)
    onehot_pad = rim_cells(onehot, 2)
    stem_out = gelu_value(conv_rows(onehot_pad, w_stem)).astype(jnp.bfloat16)
    stem_pad = rim_cells(stem_out, 2)
    enc_pre = channel_sum(conv_rows(stem_pad, w_enc))
    active = gelu_value(enc_pre).astype(jnp.bfloat16).astype(jnp.float32)
    pooled = (0.5 * active.reshape(row_count // 2, 2, -1).sum(axis=1)).astype(jnp.bfloat16)
    pooled_pad = rim_cells(pooled, 1)
    up_pad = jnp.repeat(pooled_pad, 2, axis=0)
    output = channel_sum(conv_rows(up_pad, w_dec)) + stem_out.astype(jnp.float32)
    pred = output.astype(jnp.bfloat16)
    scale = 1.0 / math.sqrt(length)
    slope_out = ((output - targets.astype(jnp.float32)) * scale).astype(jnp.bfloat16)
    slope_all = channel_gather(slope_out)
    g_dec = weight_grad(slope_all, up_pad)
    slope_pad = rim_cells(slope_all, 2)
    up_grad = jnp.zeros((row_count, w_dec.shape[2]), jnp.float32)
    for k in range(KW):
        up_grad = up_grad + jnp.dot(
            slope_pad[4 - k : 4 - k + row_count], w_dec[:, k, :], preferred_element_type=jnp.float32
        )
    pool_grad = up_grad.reshape(row_count // 2, 2, -1).sum(axis=1)
    act_grad = 0.5 * jnp.repeat(pool_grad, 2, axis=0)
    pre_grad = (act_grad * gelu_slope(enc_pre)).astype(jnp.bfloat16)
    pre_all = channel_gather(pre_grad)
    g_enc = weight_grad(pre_all, stem_pad)
    return (pred, g_enc, g_dec)


def solution(mesh):
    sizes = mesh.shape["seq"], mesh.shape["chan"]
    return jax.shard_map(
        shards if sizes == (4, 4) else general_shards,
        mesh=mesh,
        in_specs=(
            P(("groups", "seq")),
            P("chan", None, None),
            P(None, None, "chan"),
            P(None, None, "chan"),
            P(("groups", "seq"), "chan"),
        ),
        out_specs=(
            P(("groups", "seq"), "chan"),
            P(("groups", "seq"), None, "chan"),
            P(("groups", "seq"), None, "chan"),
        ),
        check_vma=False,
    )
```

```python
import functools
import math

import jax
import jax.numpy as jnp
from jax import lax
from jax.experimental import pallas as pl
from jax.experimental.pallas import tpu as pltpu
from jax.sharding import PartitionSpec as P

KW = 5

SQRT_TWO_PI = 0.7978845608028654
CUBIC = 0.044715

STEM_ROWS = 32
FIRST = 3
SIDE = 64
OUTER = 16
INNER = 8
F32 = jnp.float32
BF16 = jnp.bfloat16
MIB = 1024 * 1024


def gelu_value(value):
    inner = jnp.tanh(SQRT_TWO_PI * (value + CUBIC * value * value * value))
    return 0.5 * value * (1.0 + inner)


def gelu_slope(value):
    inner = jnp.tanh(SQRT_TWO_PI * (value + CUBIC * value * value * value))
    return 0.5 * (1.0 + inner) + 0.5 * value * (1.0 - inner * inner) * SQRT_TWO_PI * (
        1.0 + 3.0 * CUBIC * value * value
    )


def dot(a, b, contract):
    return lax.dot_general(a, b, (contract, ((), ())), preferred_element_type=F32)


def assemble(own, after, before, block, devices):
    side = 2 * SIDE
    pairs = own.shape[1]
    column = lax.broadcasted_iota(jnp.int32, (2, side), 1)
    after = jnp.where(block == devices - 1, -1, after[:, :side])
    before = jnp.where(block == 0, -1, before[:, pairs - side :])
    return jnp.concatenate([own, jnp.where(column < SIDE, after, before)], axis=1)


def split_parity(blocks):
    count = blocks[0].shape[1]
    row = lax.broadcasted_iota(jnp.int32, (count, count), 0)
    column = lax.broadcasted_iota(jnp.int32, (count, count), 1)
    source = jnp.where(column < count // 2, 2 * column, 2 * column - count + 1)
    chosen = jnp.where(row == source, 1.0, 0.0).astype(BF16)
    place = lax.broadcasted_iota(jnp.int32, (16, count), 0)
    wide = jnp.broadcast_to(blocks[0], (16, count))
    for i, block in enumerate(blocks[1:]):
        wide = jnp.where(place == i + 1, jnp.broadcast_to(block, (16, count)), wide)
    value = dot(wide.astype(F32).astype(BF16), chosen, ((1,), (0,))).astype(jnp.int32)
    return [
        jnp.concatenate([value[i : i + 1, : count // 2], value[i : i + 1, count // 2 :]], axis=0)
        for i in range(len(blocks))
    ]


def tap_onehots(bases, start, width):
    total = bases.shape[1]
    before = pltpu.roll(bases, (1 - start) % total, 1)[:, :width]
    here = bases[:, :width] if start == 0 else pltpu.roll(bases, -start % total, 1)[:, :width]
    after = pltpu.roll(bases, (-1 - start) % total, 1)[:, :width]
    taps = [before[0:1], before[1:2], here[0:1], here[1:2], after[0:1], after[1:2]]
    row = lax.broadcasted_iota(jnp.int32, (4 * KW, width), 0)
    tap, base = row >> 2, row & 3
    out = []
    for first in (0, 1):
        value = jnp.full((4 * KW, width), -1, jnp.int32)
        for k in range(KW):
            value = jnp.where(tap == k, jnp.broadcast_to(taps[first + k], value.shape), value)
        out.append(jnp.where(value == base, 1.0, 0.0).astype(BF16))
    return out


def valid_pairs(shape, dim, first, total):
    pair = lax.broadcasted_iota(jnp.int32, shape, dim) + first
    return (pair >= 0) & (pair < total)


def stem_kernel(
    place, own, after, before, stem_own, w_oth, w_own, acc, stem_out, lhs, lhs_oth, split, even, odd, *, pairs, devices
):
    seq = place[0]
    rows = pairs + 2 * INNER
    wide = pairs + 2 * OUTER
    swapped = lax.rem(seq, 2) == 1
    first, second = after[...], before[...]
    parts = split_parity([own[...], jnp.where(swapped, second, first), jnp.where(swapped, first, second)])
    for i, part in enumerate(parts):
        split[i] = part
    hots = tap_onehots(assemble(*parts, seq, devices), -OUTER, wide)
    gap = OUTER - INNER
    stem_oth = w_oth[: stem_own.shape[0], : stem_own.shape[1]]
    for weight, held_lhs in ((stem_own[...], lhs), (stem_oth, lhs_oth)):
        for hot, held in zip(hots, (even, odd)):
            raw = dot(hot, weight, ((0,), (0,)))
            ok = valid_pairs(raw.shape, 0, seq * pairs - OUTER, pairs * devices)
            held[...] = jnp.where(ok, gelu_value(raw), 0.0).astype(BF16).astype(F32)
        for k in range(6):
            source = even if k % 2 == 0 else odd
            held_lhs[k] = source[gap + k // 2 - 1 : gap + k // 2 - 1 + rows, :].astype(BF16)
    stem_out[0] = lhs[2]
    stem_out[1] = lhs[3]
    acc[...] = own_sums(lhs, w_own, 2 * (1 - place[1]) + place[2], acc.shape)


def own_sums(lhs, weight, index, shape):
    at = pl.ds(pl.multiple_of(index * shape[1], 128), shape[1])
    total = jnp.zeros(shape, F32)
    for k in range(KW):
        total = total + dot(lhs[k : k + 2].reshape(shape[0], -1), weight[k, :, at], ((1,), (0,)))
    return total


def other_sums(lhs, weight, index, total):
    rows, block = total.shape
    channels = lhs.shape[2]
    at = pl.ds(pl.multiple_of(index * block, 128), block)
    for k in range(KW):
        tap = weight[k * channels : (k + 1) * channels, at]
        total = total + dot(lhs[k : k + 2].reshape(rows, -1), tap, ((1,), (0,)))
    return total


def send_kernel(place, acc, lhs, w_oth, send):
    send[...] = other_sums(lhs, w_oth, 1 - place[1], acc[...]).astype(BF16)


def keep_kernel(place, lhs, lhs_oth, w_own, w_oth, keep):
    total = own_sums(lhs, w_own, 2 * place[1] + place[2], keep.shape)
    keep[...] = other_sums(lhs_oth, w_oth, place[1], total)


def pool_kernel(place, keep, came, pooled, centre, *, pairs, total):
    rows = pairs + 2 * INNER
    value = keep[...] + came[...].astype(F32)
    active = gelu_value(value).astype(BF16).astype(F32)
    both = 0.5 * (active[:rows] + active[rows:])
    ok = valid_pairs(both.shape, 0, place[0] * pairs - INNER, total)
    both = jnp.where(ok, both, 0.0).astype(BF16)
    pooled[...] = both
    centre[...] = both[INNER : INNER + pairs].astype(BF16)


def dec_kernel(own, oth, w_own, w_oth, stem, targets, part, send, held, *, pairs):
    rows = pairs + 2 * INNER
    held[:8] = jnp.zeros((8, held.shape[1]), F32)
    held[8 + rows :] = jnp.zeros((8, held.shape[1]), F32)
    acc = jnp.zeros(part.shape, F32)
    for source, weight in ((own, w_own), (oth, w_oth)):
        held[8 : 8 + rows] = source[...].astype(F32)
        for k in range(3):
            acc = acc + dot(held[7 + k : 7 + k + rows].astype(BF16), weight[k], ((1,), (1,)))
    half = part.shape[1] // 2
    for parity in range(2):
        value = acc[:, parity * half : (parity + 1) * half]
        value = value + stem[parity].astype(F32) - targets[parity].astype(F32)
        part[:, parity * half : (parity + 1) * half] = value
        send[:, parity * half : (parity + 1) * half] = value.astype(BF16)


def slope_kernel(place, part, came, targets, pred, sums, local, near, far, held, *, pairs, total, scale):
    rows = pairs + 2 * INNER
    half = part.shape[1] // 2
    quarter = half // 2
    ok = valid_pairs((rows, half), 0, place[0] * pairs - INNER, total)
    second = place[1] == 1
    slopes = []
    for parity in range(2):
        cols = slice(parity * half, (parity + 1) * half)
        value = part[:, cols] + came[:, cols].astype(F32)
        out = (value + targets[parity].astype(F32))[INNER : INNER + pairs]
        pred[parity] = jnp.where(second, out[:, quarter:], out[:, :quarter]).astype(BF16)
        slopes.append(jnp.where(ok, value * scale, 0.0).astype(BF16).astype(F32))
    held[:rows] = slopes[0]
    held[rows:] = jnp.zeros((8, half), F32)
    both = slopes[0] + slopes[1], slopes[1] + held[1 : 1 + rows]
    for i in range(2):
        sums[i] = both[i].astype(BF16)
    for out, step in ((local, 0), (near, 2 - place[3]), (far, 3)):
        low = lax.rem(place[0] + step, 4) < 2
        for i in range(2):
            out[i] = jnp.where(low, both[i][:, :quarter], both[i][:, quarter:]).astype(BF16)


def lane_tiles(channels):
    return [(first, min(first + 128, channels)) for first in range(0, channels, 128)]


def targets_kernel(place, own, before, after, out, held):
    channels, count = own.shape
    side = before.shape[1]
    rows = count // 2 + 2 * INNER
    high = place[1] == 1
    for first, last in lane_tiles(channels):
        wide = last - first
        held[:side, :wide] = before[first:last].astype(F32).T
        held[side : side + count, :wide] = own[first:last].astype(F32).T
        held[side + count :, :wide] = after[first:last].astype(F32).T
        for parity in range(2):
            value = held[pl.ds(side - 2 * INNER + parity, rows, stride=2), :][:, :wide].astype(BF16)
            blank = jnp.zeros_like(value)
            out[parity, :, first:last] = jnp.where(high, blank, value)
            out[parity, :, channels + first : channels + last] = jnp.where(high, value, blank)


def pred_kernel(source, out, held):
    channels, count = out.shape
    for first, last in lane_tiles(channels):
        wide = last - first
        for parity in range(2):
            value = source[parity, :, first:last].astype(F32)
            if wide < 128:
                value = jnp.concatenate([value, jnp.zeros((count // 2, 128 - wide), F32)], axis=1)
            held[pl.ds(parity, count // 2, stride=2), :] = value
        out[first:last] = held[:, :wide].T.astype(BF16)


def shifted_sums(held, pairs):
    return [
        held[0, INNER + 1 : INNER + 1 + pairs].astype(BF16),
        held[1, INNER : INNER + pairs].astype(BF16),
        held[0, INNER : INNER + pairs].astype(BF16),
        held[1, INNER - 1 : INNER - 1 + pairs].astype(BF16),
        held[0, INNER - 1 : INNER - 1 + pairs].astype(BF16),
    ]


def back_kernel(place, own, oth, weight, out, held, *, pairs):
    core = place[2]
    sides = []
    for source in (own, oth):
        held[...] = source[...].astype(F32)
        sides.append(shifted_sums(held, pairs))
    acc = jnp.zeros(out.shape, F32)
    for k in range(KW):
        kernel = [weight[k, 2 * h + c] for c in (core, 1 - core) for h in range(2)]
        acc = acc + dot(
            jnp.concatenate([sides[0][k], sides[1][k]], axis=1), jnp.concatenate(kernel, axis=0), ((1,), (0,))
        )
    out[...] = (0.5 * acc).astype(BF16)


def owner_slope_kernel(place, *refs, slot, pairs, devices):
    blocks, weights = refs[:devices], refs[devices : devices + 6]
    out, bases, even, odd, lhs = refs[devices + 6 :]
    for r in range(devices):
        bases[r] = blocks[r][...]
    wide = pairs + 2 * INNER
    step = 2 * slot + place[3]
    block = lax.rem(place[0] - step + devices, devices)
    before, after = lax.rem(step + 1, devices), lax.rem(step + devices - 1, devices)
    joined = assemble(bases[step], bases[after], bases[before], block, devices)
    hots = tap_onehots(joined, -INNER, wide)
    total = jnp.zeros(out.shape, F32)
    channels = lhs.shape[2]
    for some, others in ((0, None), (1, None), (2, 3), (4, 5)):
        count = KW if others is None else FIRST
        weight = weights[some][count * channels : count * channels + 4 * KW, :channels]
        for hot, held in zip(hots, (even, odd)):
            raw = dot(hot, weight, ((0,), (0,)))
            ok = valid_pairs(raw.shape, 0, block * pairs - INNER, pairs * devices)
            held[...] = jnp.where(ok, gelu_value(raw), 0.0).astype(BF16).astype(F32)
        for k in range(6):
            source = even if k % 2 == 0 else odd
            lhs[k] = source[INNER + k // 2 - 1 : INNER + k // 2 - 1 + pairs, :].astype(BF16)
        for k in range(KW):
            at, step = (some, k) if k < count else (others, k - count)
            tap = weights[at][step * channels : (step + 1) * channels, :]
            total = total + dot(lhs[k : k + 2].reshape(2 * pairs, -1), tap, ((1,), (0,)))
    out[...] = gelu_slope(total).astype(BF16)


def taps_kernel(place, *refs, pairs, devices):
    blocks, (stem_w, out) = refs[:devices], refs[devices:]
    channels = stem_w.shape[1]
    for r in range(devices):
        block = lax.rem(place[0] - r + devices, devices)
        bases = assemble(blocks[r][...], blocks[r - 1][...], blocks[(r + 1) % devices][...], block, devices)
        width = bases.shape[1]
        parts = []
        for hot in tap_onehots(bases, 0, width):
            raw = dot(stem_w[...], hot, ((0,), (0,)))
            column = lax.broadcasted_iota(jnp.int32, raw.shape, 1)
            pair = jnp.where(column >= width - SIDE, column - width, column) + block * pairs
            ok = (pair >= 0) & (pair < pairs * devices)
            parts.append(jnp.where(ok, gelu_value(raw), 0.0))
        taps = []
        for step in (-1, 0, 1):
            for held in parts:
                moved = held if step == 0 else pltpu.roll(held, -step % width, 1)
                taps.append(moved[:, :pairs].astype(BF16))
        at = 2 * r * pairs
        for k in range(KW):
            out[k * channels : (k + 1) * channels, at : at + pairs] = taps[k]
            out[k * channels : (k + 1) * channels, at + pairs : at + 2 * pairs] = taps[k + 1]


def picks_kernel(place, stem, enc, mine, mine0, mine1, enc_oth, sems):
    seq, core = place[0], 1 - place[2]
    taps, channels, _ = enc.shape
    block = mine0.shape[1]

    def columns(index):
        return pl.ds(pl.multiple_of(index * block, 128), block)

    copies = []
    for k in range(taps):
        rows = pl.ds(k * channels, channels)
        for h in range(2):
            copies.append((enc.at[k, :, columns(2 * h + core)], enc_oth.at[rows, h * block : (h + 1) * block]))
        copies.append((enc.at[k, :, columns(seq)], mine.at[rows]))
        if k < FIRST:
            copies.append((enc.at[k, :, columns(seq)], mine0.at[rows]))
        else:
            copies.append((enc.at[k, :, columns(seq)], mine1.at[pl.ds((k - FIRST) * channels, channels)]))
    copies = [pltpu.make_async_copy(*ends, sems.at[i]) for i, ends in enumerate(copies)]
    for copy in copies:
        copy.start()
    enc_oth[taps * channels :, : stem.shape[1]] = stem[...]
    mine0[FIRST * channels :, : stem.shape[1]] = stem[...]
    mine[taps * channels :, : stem.shape[1]] = stem[...]
    for copy in copies:
        copy.wait()


def pick_kernel(place, source, out):
    out[...] = source[...]


def comb_kernel(place, own, came, comb_own, comb_came):
    combine(own, comb_own)
    combine(came, comb_came)


def combine(weight, comb):
    comb[0, 0] = weight[0] + weight[1]
    comb[1, 0] = weight[2] + weight[3]
    comb[2, 0] = weight[4]
    comb[0, 1] = weight[0]
    comb[1, 1] = weight[1] + weight[2]
    comb[2, 1] = weight[3] + weight[4]


def dec_grad_kernel(place, own, came, pool0, pool1, pool2, pool3, out, held, taps, pooled, *, pairs):
    blocks = (pool0, pool1, pool2, pool3)
    parity = place[3]
    odd = lax.rem(place[0], 2)
    for block, step in zip(blocks, (0, 3 - 2 * odd, 2, 1 + 2 * odd)):
        pooled[pl.ds(pl.multiple_of(step * pairs, pairs), pairs), :] = block[...]
    for i in range(4):
        slots = own if i < 2 else came
        held[...] = slots[i % 2].astype(F32)
        step = 2 * (i % 2) + (parity if i < 2 else 1 - parity)
        at = pl.ds(pl.multiple_of(step * pairs, pairs), pairs)
        for k, tap in enumerate(shifted_sums(held, pairs)):
            taps[k, at, :] = tap
    for k in range(KW):
        out[k] = dot(taps[k], pooled[...], ((0,), (0,)))


def enc_grad_kernel(place, taps, slots, slope0, slope1, *refs, first):
    prior, (out, joined) = refs[:-2], refs[-2:]
    pairs = slots.shape[1]
    size = 2 * pairs
    offset = place[3] if first else 1 - place[3]

    @pl.when(pl.program_id(0) == 0)
    def _():
        for i, slope in enumerate((slope0, slope1)):
            grad = slots[i].astype(F32)
            for parity in range(2):
                at = i * size + parity * pairs
                value = grad * slope[parity * pairs : (parity + 1) * pairs].astype(F32)
                joined[at : at + pairs] = value.astype(BF16)

    used = [taps[:, pl.ds(pl.multiple_of((2 * i + offset) * size, 128), size)] for i in range(2)]
    value = dot(jnp.concatenate(used, axis=1), joined[...], ((1,), (0,)))
    out[...] = value if first else value + prior[0][...]


def whole(shape):
    return pl.BlockSpec(shape, lambda *_: (0,) * len(shape))


SCALARS = pl.BlockSpec(memory_space=pltpu.SMEM)


def call(kernel, ins, outs, scratch=(), limit=16, name=None, last=()):
    specs = [SCALARS if i.dtype == jnp.int32 and i.ndim == 1 else whole(i.shape) for i in ins]
    for at in last:
        shape = ins[at].shape
        specs[at] = pl.BlockSpec((STEM_ROWS,) + shape[1:], lambda *_: (shape[0] // STEM_ROWS - 1, 0))
    return pl.pallas_call(
        kernel,
        grid=(1,) if last else (),
        in_specs=specs,
        out_specs=[whole(s) for s, _ in outs],
        out_shape=[jax.ShapeDtypeStruct(s, d) for s, d in outs],
        scratch_shapes=[pltpu.VMEM(s, d) for s, d in scratch],
        compiler_params=pltpu.CompilerParams(vmem_limit_bytes=limit * MIB),
        name=name,
    )(*ins)


def gated(values, gates):
    return lax.optimization_barrier((values, gates))[0]


def shards(dna_bases, w_stem, w_enc, w_dec, targets):
    devices = lax.axis_size("seq")
    seq, chan = lax.axis_index("seq"), lax.axis_index("chan")
    hi, lo = chan // 2, chan % 2
    parity = (lo + seq) % 2
    pairs = dna_bases.shape[0] // 2
    total = pairs * devices
    rows = pairs + 2 * INNER
    stem_c = w_stem.shape[0]
    enc_c = w_dec.shape[2]
    across = [(c, c ^ 2) for c in range(4)]
    cores = [(c, c ^ 1) for c in range(4)]

    def ring(array, step):
        return lax.ppermute(array, "seq", [(i, (i + step) % devices) for i in range(devices)])

    def swap(array, distance):
        return lax.ppermute(array, "seq", [(i, i ^ distance) for i in range(devices)])

    place = jnp.stack([seq, hi, lo, parity]).astype(jnp.int32)
    first_chip, even = hi == 0, parity == 0
    target = [(seq + step) % devices // 2 == hi for step in (0, 2 - parity, 3)]
    own = dna_bases.reshape(1, 2 * pairs)
    stem_w = w_stem.transpose(1, 2, 0).reshape(4 * KW, stem_c)
    own, place, first_chip, even, target = lax.optimization_barrier((own, place, first_chip, even, target))

    first = swap(own, 1)
    second = lax.ppermute(own, "seq", [(i, (i + 1 - 2 * (1 - i % 2)) % devices) for i in range(devices)])
    enc_w = w_enc.transpose(1, 2, 0)
    dec_w = w_dec.transpose(1, 0, 2).reshape(KW, 4, stem_c, enc_c)
    picked = (KW, 1, stem_c, enc_c)
    stem_rows = jnp.concatenate([stem_w, jnp.zeros((STEM_ROWS - 4 * KW, stem_c), BF16)])
    mine, mine0, mine1, enc_send = pl.pallas_call(
        picks_kernel,
        in_specs=[SCALARS, whole(stem_rows.shape), pl.BlockSpec(memory_space=pl.ANY)],
        out_specs=[pl.BlockSpec(memory_space=pltpu.VMEM)] * 4,
        out_shape=[
            jax.ShapeDtypeStruct((KW * stem_c + STEM_ROWS, enc_c), BF16),
            jax.ShapeDtypeStruct((FIRST * stem_c + STEM_ROWS, enc_c), BF16),
            jax.ShapeDtypeStruct(((KW - FIRST) * stem_c, enc_c), BF16),
            jax.ShapeDtypeStruct((KW * stem_c + STEM_ROWS, 2 * enc_c), BF16),
        ],
        scratch_shapes=[pltpu.SemaphoreType.DMA((4 * KW,))],
        compiler_params=pltpu.CompilerParams(vmem_limit_bytes=6 * MIB),
        name="picks",
    )(place, stem_rows, enc_w)
    enc_oth = lax.ppermute(enc_send, "chan", cores)
    mine0_far = lax.ppermute(mine0, "chan", across)
    dec_send = pl.pallas_call(
        pick_kernel,
        grid_spec=pltpu.PrefetchScalarGridSpec(
            num_scalar_prefetch=1,
            grid=(2,),
            in_specs=[pl.BlockSpec(picked, lambda h, at: (0, 2 * h + 1 - at[2], 0, 0))],
            out_specs=pl.BlockSpec(picked, lambda h, at: (0, h, 0, 0)),
        ),
        out_shape=jax.ShapeDtypeStruct((KW, 2, stem_c, enc_c), BF16),
        compiler_params=pltpu.CompilerParams(vmem_limit_bytes=8 * MIB),
        name="dec_pick",
    )(place, dec_w)
    dec_came = lax.ppermute(dec_send, "chan", cores)

    held = (6, rows, stem_c)
    acc, stem, lhs, lhs_oth, split = call(
        functools.partial(stem_kernel, pairs=pairs, devices=devices),
        [place, own, first, second, stem_w, enc_oth, enc_w],
        [
            ((2 * rows, enc_c), F32),
            ((2, rows, stem_c), BF16),
            (held, BF16),
            (held, BF16),
            ((3, 2, pairs), jnp.int32),
        ],
        [((pairs + 2 * OUTER, stem_c), F32), ((pairs + 2 * OUTER, stem_c), F32)],
        limit=14,
        name="stem_conv",
        last=(5,),
    )
    (send,) = call(
        send_kernel,
        [place, acc, lhs_oth, enc_oth],
        [((2 * rows, enc_c), BF16)],
        limit=12,
        name="enc_conv",
    )
    came = lax.ppermute(send, "chan", across)

    (keep,) = call(
        keep_kernel,
        [gated(place, send), lhs, lhs_oth, enc_w, enc_oth],
        [((2 * rows, enc_c), F32)],
        limit=14,
        name="enc_keep",
    )
    targets_in, place_in = gated((targets, place), send)
    blocks = {0: split[0], 1: split[2], devices - 1: split[1]}
    for r in range(2, devices - 1):
        blocks[r] = ring(split[0], r)
    comb_own, comb_came = pl.pallas_call(
        comb_kernel,
        grid_spec=pltpu.PrefetchScalarGridSpec(
            num_scalar_prefetch=1,
            grid=(2,),
            in_specs=[
                pl.BlockSpec(picked, lambda h, at: (0, 2 * h + at[2], 0, 0)),
                pl.BlockSpec(picked, lambda h, at: (0, h, 0, 0)),
            ],
            out_specs=[pl.BlockSpec((3, 2, 1, stem_c, enc_c), lambda h, at: (0, 0, h, 0, 0))] * 2,
        ),
        out_shape=[jax.ShapeDtypeStruct((3, 2, 2, stem_c, enc_c), BF16)] * 2,
        compiler_params=pltpu.CompilerParams(vmem_limit_bytes=12 * MIB),
        name="dec_taps",
    )(place_in, dec_w, dec_came)
    targets_in = targets_in.T
    count, edge = 2 * pairs, 2 * SIDE
    below, above = ring(targets_in[:, count - edge :], 1), ring(targets_in[:, :edge], devices - 1)
    mine1_far = lax.ppermute(gated(mine1, (below, mine0_far)), "chan", across)
    (targets_at,) = call(
        targets_kernel,
        [place, targets_in, below, above],
        [((2, rows, 2 * stem_c), BF16)],
        [((count + 2 * edge, 128), F32)],
        limit=6,
        name="targets",
    )
    blank = jnp.zeros_like(stem)
    stem_at = jnp.where(
        first_chip, jnp.concatenate([stem, blank], axis=2), jnp.concatenate([blank, stem], axis=2)
    )
    place_in = gated(place, (comb_own, comb_came, targets_at, stem_at, list(blocks.values())))

    pooled, centre = call(
        functools.partial(pool_kernel, pairs=pairs, total=total),
        [place_in, keep, came],
        [((rows, enc_c), BF16), ((pairs, enc_c), BF16)],
        limit=8,
        name="gelu_pool",
    )
    pooled_oth = lax.ppermute(pooled, "chan", cores)
    part, send = call(
        functools.partial(dec_kernel, pairs=pairs),
        [
            pooled,
            pooled_oth,
            comb_own.reshape(3, 4 * stem_c, enc_c),
            comb_came.reshape(3, 4 * stem_c, enc_c),
            stem_at,
            targets_at,
        ],
        [((rows, 4 * stem_c), F32), ((rows, 4 * stem_c), BF16)],
        [((rows + 16, enc_c), F32)],
        limit=11,
        name="dec_conv",
    )
    came = lax.ppermute(gated(send, mine1_far), "chan", across)

    centre, place_in = gated((centre, place), send)
    beyond, beside = swap(centre, 2), swap(centre, 1)

    weights = [mine, lax.ppermute(gated(mine, keep), "chan", cores), mine0_far, mine1_far]
    weights += [lax.ppermute(w, "chan", cores) for w in weights[2:]]

    def owner_slope(slot, at):
        (out,) = call(
            functools.partial(owner_slope_kernel, slot=slot, pairs=pairs, devices=devices),
            [at] + [blocks[r] for r in range(devices)] + weights,
            [((2 * pairs, enc_c), BF16)],
            [
                ((devices, 2, pairs), jnp.int32),
                ((rows, stem_c), F32),
                ((rows, stem_c), F32),
                ((6, pairs, stem_c), BF16),
            ],
            limit=10,
            name="owner_slope",
        )
        return out, lax.ppermute(out, "chan", cores)

    slope0, slope0_came = owner_slope(0, gated(place, send))
    (taps,) = call(
        functools.partial(taps_kernel, pairs=pairs, devices=devices),
        [gated(place, slope0)] + [blocks[r] for r in range(devices)] + [stem_w],
        [((KW * stem_c, 2 * pairs * devices), BF16)],
        limit=12,
        name="stem_taps",
    )

    pred, sums, local, near, far = call(
        functools.partial(slope_kernel, pairs=pairs, total=total, scale=1.0 / math.sqrt(2 * total)),
        [gated(place, (beyond, beside, slope0, taps)), part, came, targets_at],
        [((2, pairs, stem_c), BF16), ((2, rows, 2 * stem_c), BF16)] + [((2, rows, stem_c), BF16)] * 3,
        [((rows + 8, 2 * stem_c), F32)],
        limit=7,
        name="out_slope",
    )
    sums_oth = lax.ppermute(sums, "chan", cores)
    (pre,) = call(
        functools.partial(back_kernel, pairs=pairs),
        [place, sums, sums_oth, dec_w],
        [((pairs, enc_c), BF16)],
        [((2, rows, 2 * stem_c), F32)],
        limit=11,
        name="up_grad",
    )

    def link(steps):
        out = []
        for s in range(devices):
            for step in steps:
                t = (s + step) % devices
                for x in range(2):
                    out.append((s * 4 + 2 * x + t % 2, t * 4 + 2 * x + (t + step) % 2))
        return out

    def to_owner(local, near, far):
        near = lax.ppermute(near, ("seq", "chan"), link((1, 2)))
        far = lax.ppermute(far, ("seq", "chan"), link((3,)))
        return local, near, far

    def slots(local, near, far):
        return jnp.stack([jnp.where(even, local, near), jnp.where(even, near, far)])

    local, near, far = to_owner(local, near, far)
    pre_oth = lax.ppermute(pre, "chan", across)
    slope1, slope1_came = owner_slope(1, gated(place, pre))
    near, far = gated((near, far), slope1)
    far_pooled = swap(gated(beyond, pre), 1)
    sums_pieces = local, near, far
    pre_oth = gated(pre_oth, (near, far, slope1))
    pieces = [jnp.where(own_block, pre, pre_oth) for own_block in target]
    local, near, far = to_owner(*pieces)
    sums_mine = gated(slots(*sums_pieces), pieces)
    sums_came = lax.ppermute(sums_mine, "chan", cores)

    (pred,) = call(
        pred_kernel,
        [pred],
        [((stem_c, 2 * pairs), BF16)],
        [((2 * pairs, 128), F32)],
        limit=5,
        name="pred",
    )
    pred = pred.T
    (g_dec,) = call(
        functools.partial(dec_grad_kernel, pairs=pairs),
        [place, sums_mine, sums_came, centre, beside, beyond, far_pooled],
        [((KW, stem_c, enc_c), F32)],
        [
            ((2, rows, stem_c), F32),
            ((KW, devices * pairs, stem_c), BF16),
            ((devices * pairs, enc_c), BF16),
        ],
        limit=12,
        name="dec_grad",
    )
    near, far = gated((near, far), (g_dec, pred))
    pre_mine = slots(local, near, far)
    pre_came = lax.ppermute(pre_mine, "chan", cores)

    def enc_grad(first, *arrays):
        count = 1 if first else 2
        half = (KW * stem_c // count, enc_c)
        return pl.pallas_call(
            functools.partial(enc_grad_kernel, first=first),
            grid=(count,),
            in_specs=[SCALARS, pl.BlockSpec((half[0], 2 * pairs * devices), lambda k: (k, 0))]
            + [whole(p.shape) for p in arrays[:3]]
            + [pl.BlockSpec(half, lambda k: (k, 0))] * len(arrays[3:]),
            out_specs=pl.BlockSpec(half, lambda k: (k, 0)),
            out_shape=jax.ShapeDtypeStruct((KW * stem_c, enc_c), F32),
            scratch_shapes=[pltpu.VMEM((4 * pairs, enc_c), BF16)],
            compiler_params=pltpu.CompilerParams(vmem_limit_bytes=13 * MIB),
            name="enc_grad",
        )(place, taps, *arrays)

    g_enc = enc_grad(True, pre_mine, slope0, slope1)
    g_enc = enc_grad(False, pre_came, slope0_came, slope1_came, g_enc)
    g_enc = g_enc.reshape(KW, stem_c, enc_c).transpose(2, 0, 1)
    return (pred, g_enc, g_dec.transpose(1, 0, 2))


def extended(block, sides, width):
    for axis, dim in sides:
        count = lax.axis_size(axis)
        forward = [(i, i + 1) for i in range(count - 1)]
        backward = [(target, source) for source, target in forward]
        low = lax.ppermute(
            lax.slice_in_dim(block, block.shape[dim] - width, None, axis=dim), axis, forward
        )
        high = lax.ppermute(lax.slice_in_dim(block, 0, width, axis=dim), axis, backward)
        block = jnp.concatenate([low, block, high], axis=dim)
    return block


def rim_cells(block, margin):
    return extended(block, (("seq", 0),), margin)


def channel_sum(partial_value):
    return lax.psum_scatter(partial_value, "chan", scatter_dimension=1, tiled=True)


def channel_gather(block):
    return lax.all_gather(block, "chan", axis=1, tiled=True)


def conv_rows(padded, weight):
    row_count = padded.shape[0] - 4
    total = jnp.zeros((row_count, weight.shape[0]), jnp.float32)
    for k in range(KW):
        total = total + lax.dot_general(
            padded[k : k + row_count],
            weight[:, k, :],
            (((1,), (1,)), ((), ())),
            preferred_element_type=jnp.float32,
        )
    return total


def grad_taps(picked, padded):
    row_count = picked.shape[0]
    pieces = [
        lax.dot_general(
            picked,
            padded[k : k + row_count],
            (((0,), (0,)), ((), ())),
            preferred_element_type=jnp.float32,
        )
        for k in range(KW)
    ]
    return jnp.stack(pieces, axis=1)


def weight_grad(cotangent, padded):
    rounded = grad_taps(cotangent, padded).astype(jnp.bfloat16)
    return lax.psum_scatter(
        lax.optimization_barrier(rounded).astype(jnp.float32),
        "seq",
        scatter_dimension=0,
        tiled=True,
    )


def general_shards(dna_bases, w_stem, w_enc, w_dec, targets):
    row_count = dna_bases.shape[0]
    devices = lax.axis_size("seq")
    length = row_count * devices
    onehot = (dna_bases[:, None] == jnp.arange(4, dtype=jnp.int32)[None, :]).astype(jnp.bfloat16)
    onehot_pad = rim_cells(onehot, 2)
    stem_out = gelu_value(conv_rows(onehot_pad, w_stem)).astype(jnp.bfloat16)
    stem_pad = rim_cells(stem_out, 2)
    enc_pre = channel_sum(conv_rows(stem_pad, w_enc))
    active = gelu_value(enc_pre).astype(jnp.bfloat16).astype(jnp.float32)
    pooled = (0.5 * active.reshape(row_count // 2, 2, -1).sum(axis=1)).astype(jnp.bfloat16)
    pooled_pad = rim_cells(pooled, 1)
    up_pad = jnp.repeat(pooled_pad, 2, axis=0)
    output = channel_sum(conv_rows(up_pad, w_dec)) + stem_out.astype(jnp.float32)
    pred = output.astype(jnp.bfloat16)
    scale = 1.0 / math.sqrt(length)
    slope_out = ((output - targets.astype(jnp.float32)) * scale).astype(jnp.bfloat16)
    slope_all = channel_gather(slope_out)
    g_dec = weight_grad(slope_all, up_pad)
    slope_pad = rim_cells(slope_all, 2)
    up_grad = jnp.zeros((row_count, w_dec.shape[2]), jnp.float32)
    for k in range(KW):
        up_grad = up_grad + jnp.dot(
            slope_pad[4 - k : 4 - k + row_count], w_dec[:, k, :], preferred_element_type=jnp.float32
        )
    pool_grad = up_grad.reshape(row_count // 2, 2, -1).sum(axis=1)
    act_grad = 0.5 * jnp.repeat(pool_grad, 2, axis=0)
    pre_grad = (act_grad * gelu_slope(enc_pre)).astype(jnp.bfloat16)
    pre_all = channel_gather(pre_grad)
    g_enc = weight_grad(pre_all, stem_pad)
    return (pred, g_enc, g_dec)


def solution(mesh):
    sizes = mesh.shape["seq"], mesh.shape["chan"]
    return jax.shard_map(
        shards if sizes == (4, 4) else general_shards,
        mesh=mesh,
        in_specs=(
            P(("groups", "seq")),
            P("chan", None, None),
            P(None, None, "chan"),
            P(None, None, "chan"),
            P(("groups", "seq"), "chan"),
        ),
        out_specs=(
            P(("groups", "seq"), "chan"),
            P(("groups", "seq"), None, "chan"),
            P(("groups", "seq"), None, "chan"),
        ),
        check_vma=False,
    )
```
